256 devices in a mesh: dp: 2 (over z_lo), row: 4 (over y), col: 32 (over z_hi, x, core).
Axes of the slice: x: 4, y: 4, z: 8 (z_hi: 4, z_lo: 2; z = z_hi * 2 + z_lo), core: 2. Of those that a mesh axis runs over, the one named last changes fastest.
Arguments:
- states: bfloat16 [2, 1024, 5120], P('dp', 'row', 'col'), may hold values from -80 to 80
- cotangent: bfloat16 [2, 1024, 5120], P('dp', 'row', 'col'), may hold values from -6 to 6
- shift_mod: float32 [2, 5120], P('dp', 'col'), may hold values from -5 to 5
- scale_mod: float32 [2, 5120], P('dp', 'col'), may hold values from -2.5 to 2.5
- gate_mod: float32 [2, 5120], P('dp', 'col'), may hold values from -5 to 5
- first_weight: bfloat16 [5120, 13824], P('row', 'col'), may hold values from -0.15625 to 0.15625
- second_weight: bfloat16 [5120, 13824], P('row', 'col'), may hold values from -0.09375 to 0.09375
Outputs:
- grad_states: float32 [2, 1024, 5120], P('dp', 'row', 'col')
- grad_first: float32 [5120, 13824], P('row', 'col')
- grad_second: float32 [5120, 13824], P('row', 'col')
- grad_shift: float32 [2, 5120], P('dp', 'col')
- grad_scale: float32 [2, 5120], P('dp', 'col')
- grad_gate: float32 [2, 5120], P('dp', 'col')
The draws below stay inside these ranges and needn't reach their ends.
All inputs are finite; a program needn't handle non-finite values.
Results may differ from the reference program's by a relative error of at most 0.039.
Values may be sent and summed in bfloat16 or wider, within the bound.
No kernel may reach another device: no remote copies, remote signals or barrier semaphores. Data moves between devices by JAX's collectives and lax.ppermute only.
A program may use at most 128 MiB of HBM per device.

```python
import math
import jax
import jax.numpy as jnp
from jax import lax

D = 5120
FF = 13824
TOK_DEV = 256
TOKENS = 1024
CLIPS = 2
N_ROW = 4
N_COL = 32


def draw_states(key, part):
    key = jax.random.fold_in(key, 11)
    first, second, third = jax.random.split(key, 3)
    ramp = math.log(3.0) * jnp.arange(D, dtype=jnp.float32) / D
    columns = jnp.exp(jax.random.uniform(third, (1, 1, D), jnp.float32, -0.6, 0.6) + ramp)
    base = jnp.clip(jax.random.normal(first, (CLIPS, TOKENS, D), jnp.float32), -4.0, 4.0)
    rows = jnp.exp(jax.random.uniform(second, (CLIPS, TOKENS, 1), jnp.float32, -1.2, 1.2))
    return (base * rows * columns).astype(jnp.bfloat16)


def strengthened(entries, own_key, source, target, parts, factor):
    owner, partner = [(jnp.arange(entries.shape[axis_at]) // (entries.shape[axis_at] // parts)).reshape([-1 if axis == axis_at else 1 for axis in range(entries.ndim)]) for axis_at in (source, target)]
    chosen = jax.random.permutation(own_key, parts)[partner]
    strong = (owner == chosen) | (owner == (partner + parts // 2) % parts)
    return jnp.where(strong, factor * entries, entries)


def level_of(rng, shape, cuts, least, largest):
    factor_of, own = 1.0, jax.random.fold_in(rng, 6)
    for axis_at, parts in cuts:
        heights = jnp.exp(jax.random.uniform(jax.random.fold_in(own, axis_at), (parts,), jnp.float32, least / len(cuts), largest / len(cuts)))
        factor_of = factor_of * jnp.repeat(heights, shape[axis_at] // parts).reshape([-1 if axis == axis_at else 1 for axis in range(len(shape))])
    return factor_of


def bell_draw(key, shape, width, reach, cuts=(), kind=jnp.bfloat16):
    entries = jax.random.normal(key, shape, jnp.float32) * width
    if len(cuts) > 0:
        entries = level_of(key, shape, cuts, -0.22, 0.18) * entries
    return jnp.clip(entries, min=-reach, max=reach).astype(kind)


def gaussian_with(own_key, extent, scale, reach, cuts, heavy, held_as=jnp.bfloat16):
    result = scale * jax.random.normal(own_key, extent, jnp.float32)
    if cuts:
        result = result * level_of(own_key, extent, cuts, -0.22, 0.18)
    return jnp.clip(strengthened(result, jax.random.fold_in(own_key, 3), *heavy), -reach, reach).astype(held_as)


def setup_inputs(seed: int = 0) -> dict:
    arg_keys = jax.random.split(jax.random.key(seed), 8)
    return {
        "states": draw_states(jax.random.fold_in(arg_keys[7], 71), 0),
        "cotangent": bell_draw(arg_keys[1], (CLIPS, TOKENS, D), 1.0, 6.0, ((0, 2), (1, 4), (2, 32))),
        "shift_mod": bell_draw(arg_keys[2], (CLIPS, D), 1.0, 5.0, ((0, 2), (1, 32)), jnp.float32),
        "scale_mod": bell_draw(arg_keys[3], (CLIPS, D), 0.5, 2.5, ((0, 2), (1, 32)), jnp.float32),
        "gate_mod": bell_draw(arg_keys[4], (CLIPS, D), 1.0, 5.0, ((0, 2), (1, 32)), jnp.float32),
        "first_weight": gaussian_with(arg_keys[5], (D, FF), D ** -0.5, 0.15625, ((0, 4), (1, 32)), (1, 0, 32, 2.75)),
        "second_weight": gaussian_with(arg_keys[6], (D, FF), FF ** -0.5, 0.09375, ((0, 4), (1, 32)), (1, 0, 32, 2.75)),
    }


eps = 1e-06
tanh_factor = 0.7978845608028654
cubic_term = 0.044715

def gelu_tanh(values):
    inner = jnp.tanh(tanh_factor * (values + cubic_term * values * values * values))
    return 0.5 * values * (1.0 + inner)

def gelu_slope(values):
    inner = jnp.tanh(tanh_factor * (values + cubic_term * values * values * values))
    return 0.5 * (1.0 + inner) + 0.5 * values * (1.0 - inner * inner) * tanh_factor * (1.0 + 3.0 * cubic_term * values * values)

def rounded(values):
    return lax.optimization_barrier(values.astype(jnp.bfloat16)).astype(jnp.float32)

def reference(states, cotangent, shift_mod, scale_mod, gate_mod, first_weight, second_weight):
    highest = lax.Precision.HIGHEST
    block = FF // N_COL
    wide_one = first_weight.astype(jnp.float32)
    wide_two = second_weight.astype(jnp.float32)
    blocks_one = wide_one.reshape(D, N_COL, block).transpose(1, 0, 2)
    blocks_two = wide_two.reshape(D, N_COL, block).transpose(1, 0, 2)
    token_scale = 1.0 / math.sqrt(TOKENS)
    weight_scale = 1.0 / math.sqrt(CLIPS * TOKENS)

    def block_sum(left, blocks):
        left_blocks = left.reshape(TOKENS, N_COL, block).transpose(1, 0, 2)

        def add_block(total, pair):
            part = jnp.dot(pair[0], pair[1].T, precision=highest)
            return (total + rounded(part), None)
        total, _ = lax.scan(add_block, jnp.zeros((TOKENS, D), jnp.float32), (left_blocks, blocks))
        return total

    def token_blocks(left, right):
        left_rows = left.reshape(N_ROW, TOK_DEV, D)
        right_rows = right.reshape(N_ROW, TOK_DEV, FF)

        def add_rows(total, pair):
            part = jnp.dot(pair[0].T, pair[1], precision=highest) * weight_scale
            return (total + rounded(part), None)
        total, _ = lax.scan(add_rows, jnp.zeros((D, FF), jnp.float32), (left_rows, right_rows))
        return total
    grad_first = jnp.zeros((D, FF), jnp.float32)
    grad_second = jnp.zeros((D, FF), jnp.float32)
    states_out, shift_out, scale_out, gate_out = ([], [], [], [])
    for clip_index in range(CLIPS):
        inputs = states[clip_index].astype(jnp.float32)
        centre = lax.optimization_barrier(jnp.mean(inputs, -1, keepdims=True))
        offset = inputs - centre
        spread = lax.optimization_barrier(jnp.mean(offset * offset, -1, keepdims=True))
        inverse = lax.rsqrt(spread + eps)
        normed = offset * inverse
        modulated = (normed * (1.0 + scale_mod[clip_index]) + shift_mod[clip_index]).astype(jnp.bfloat16)
        pre_act = jnp.dot(modulated.astype(jnp.float32), wide_one, precision=highest)
        hidden = gelu_tanh(pre_act).astype(jnp.bfloat16)
        hidden_wide = hidden.astype(jnp.float32)
        output = block_sum(hidden_wide, blocks_two)
        upstream = cotangent[clip_index].astype(jnp.float32)
        gate_out.append(lax.optimization_barrier(jnp.sum(upstream * output, 0)) * token_scale)
        scaled = (upstream * gate_mod[clip_index]).astype(jnp.bfloat16)
        scaled_wide = scaled.astype(jnp.float32)
        grad_hidden = jnp.dot(scaled_wide, wide_two, precision=highest)
        grad_pre = (grad_hidden * gelu_slope(pre_act)).astype(jnp.bfloat16)
        grad_pre_wide = grad_pre.astype(jnp.float32)
        grad_mod = block_sum(grad_pre_wide, blocks_one)
        shift_out.append(lax.optimization_barrier(jnp.sum(grad_mod, 0)) * token_scale)
        scale_out.append(lax.optimization_barrier(jnp.sum(grad_mod * normed, 0)) * token_scale)
        grad_normed = grad_mod * (1.0 + scale_mod[clip_index])
        first_mean = lax.optimization_barrier(jnp.mean(grad_normed, -1, keepdims=True))
        second_mean = lax.optimization_barrier(jnp.mean(grad_normed * normed, -1, keepdims=True))
        states_out.append(upstream + inverse * (grad_normed - first_mean - normed * second_mean))
        grad_first = grad_first + token_blocks(modulated.astype(jnp.float32), grad_pre_wide)
        grad_second = grad_second + token_blocks(scaled_wide, hidden_wide)
    return (jnp.stack(states_out), grad_first, grad_second, jnp.stack(shift_out), jnp.stack(scale_out), jnp.stack(gate_out))
```

```python
import math

import jax
import jax.numpy as jnp
from jax import lax
from jax.experimental import pallas as pl
from jax.experimental.pallas import tpu as pltpu
from jax.sharding import PartitionSpec as P

D = 5120
FF = 13824
ROWS = 4
COLS = 32
INNER = 8
CHANNELS = D // COLS
UNITS = FF // COLS
TOK = 256
SLICE = D // ROWS

bf16, f32 = jnp.bfloat16, jnp.float32

eps = 1e-06
tanh_factor = 0.7978845608028654
cubic_term = 0.044715
token_scale = 1.0 / math.sqrt(ROWS * TOK)
weight_scale = 1.0 / math.sqrt(2 * ROWS * TOK)


def gelu_pair(values):
    squares = values * values
    inner = jnp.tanh(tanh_factor * (values + cubic_term * squares * values))
    half = 0.5 * (1.0 + inner)
    slope = half + 0.5 * values * (1.0 - inner * inner) * tanh_factor * (
        1.0 + 3.0 * cubic_term * squares
    )
    return values * half, slope


def turn(value, offset):
    return lax.rem(value + (offset + 4), 4)


def spread_rows(values, shift):
    pairs = [
        (a * COLS + b * INNER + i, b * COLS + ((a + shift) % 4) * INNER + i)
        for a in range(4)
        for b in range(4)
        for i in range(INNER)
    ]
    return lax.ppermute(values, ("row", "col"), pairs)


def return_rows(values, shift):
    pairs = [
        (a * COLS + b * INNER + i, ((b + shift) % 4) * COLS + a * INNER + i)
        for a in range(4)
        for b in range(4)
        for i in range(INNER)
    ]
    return lax.ppermute(values, ("row", "col"), pairs)


def along_x(values, shift):
    pairs = [
        (h * 8 + x * 2 + k, h * 8 + ((x + shift) % 4) * 2 + k)
        for h in range(4)
        for x in range(4)
        for k in range(2)
    ]
    return lax.ppermute(values, "col", pairs)


def across(values, mask=1):
    return lax.ppermute(values, "col", [(c, c ^ mask) for c in range(COLS)])


def along_row(values, shift):
    return lax.ppermute(values, "row", [(a, (a + shift) % 4) for a in range(4)])


def swap_clips(values):
    return lax.ppermute(values, "dp", [(0, 1), (1, 0)])


def call(kernel, grid, in_specs, out_specs, out_shape, scratch=(), flops=0, moved=0):
    return pl.pallas_call(
        kernel,
        grid_spec=pltpu.PrefetchScalarGridSpec(
            num_scalar_prefetch=1,
            grid=grid,
            in_specs=in_specs,
            out_specs=out_specs,
            scratch_shapes=list(scratch),
        ),
        out_shape=out_shape,
        compiler_params=pltpu.CompilerParams(vmem_limit_bytes=48 * 1024 * 1024),
        cost_estimate=pl.CostEstimate(flops=flops, bytes_accessed=moved, transcendentals=0),
    )


def full(shape):
    return pl.BlockSpec(shape, lambda i, pos: (0,) * len(shape))


def stats_kernel(pos, *refs):
    blocks, out = refs[:8], refs[8]
    total = 0.0
    for ref in blocks:
        total = total + jnp.sum(ref[0, 0].astype(f32), 0, keepdims=True)
    mean = total / SLICE
    square = 0.0
    for ref in blocks:
        offset = ref[0, 0].astype(f32) - mean
        square = square + jnp.sum(offset * offset, 0, keepdims=True)
    out[0, 0:1] = mean
    out[0, 1:2] = square


def combined(stats):
    centre = 0.25 * (stats[0][0:1] + stats[1][0:1] + stats[2][0:1] + stats[3][0:1])
    spread = 0.0
    for part in stats:
        spread = spread + part[1:2] + SLICE * (part[0:1] - centre) ** 2
    return centre, lax.rsqrt(spread / D + eps)


def forward_kernel(pos, *refs):
    blocks, stats, mods, w1, w2 = refs[:8], refs[8:12], refs[12], refs[13], refs[14]
    sums, normed_out, c_out, modulated_s, scaled_s = refs[15:]
    token = turn(pos[1], -pl.program_id(0))
    centre, inverse = combined([ref[token] for ref in stats])
    for q in range(4):
        for flip in range(2):
            ref = blocks[2 * q + flip]
            core = pos[3] if flip == 0 else 1 - pos[3]
            j = turn(pos[2], -q) * 2 + core
            column = mods[j]
            shift, factor, gate = column[:, 0:1], column[:, 1:2], column[:, 2:3]
            normed = (ref[0, 0].astype(f32) - centre) * inverse
            normed_out[0, j] = normed.astype(bf16)
            modulated_s[j] = (normed * factor + shift).astype(bf16)
            c_out[0, j] = ref[0, 1]
            scaled_s[j] = (ref[0, 1].astype(f32) * gate).astype(bf16)
    sums[0, 0] = jnp.dot(
        w1[...], modulated_s[...].reshape(SLICE, TOK), preferred_element_type=f32
    ).astype(bf16)
    sums[0, 1] = jnp.dot(
        w2[...], scaled_s[...].reshape(SLICE, TOK), preferred_element_type=f32
    ).astype(bf16)


def hidden_kernel(pos, own, one, two, three, through, out, norm_sums):
    pre = own[0, 0].astype(f32) + one[0].astype(f32) + two[0].astype(f32) + three[0].astype(f32)
    gh = own[0, 1].astype(f32) + one[1].astype(f32) + two[1].astype(f32) + three[1].astype(f32)
    hidden, slope = gelu_pair(pre)
    grad_pre = (gh * slope).astype(bf16)
    out[0] = hidden.astype(bf16)
    out[1] = grad_pre
    wide = grad_pre.astype(f32)
    norm_sums[0:1] = jnp.sum(wide * through[:, 1:2], 0, keepdims=True)
    norm_sums[1:2] = jnp.sum(wide * (pre - through[:, 0:1]), 0, keepdims=True)


def mod_kernel(pos, g0, g1, g2, g3, w1, keep, send):
    own_rows = pl.ds(pl.multiple_of(pos[3] * CHANNELS, 16), CHANNELS)
    other_rows = pl.ds(pl.multiple_of((1 - pos[3]) * CHANNELS, 16), CHANNELS)
    for q, ref in enumerate((g0, g1, g2, g3)):
        s = turn(turn(pos[0], -q), -pos[1])
        grad = ref[0]
        keep[0, s] = jnp.dot(w1[own_rows, :], grad, preferred_element_type=f32).astype(bf16)
        send[0, s] = jnp.dot(w1[other_rows, :], grad, preferred_element_type=f32).astype(bf16)


def weight_kernel(pos, b0, b1, b2, b3, normed, cot, mods, w1, w2, first, second, send, sums):
    across_tokens = (((1,), (1,)), ((), ()))
    raw_first = raw_second = total = 0.0
    for q, ref in enumerate((b0, b1, b2, b3)):
        token = turn(pos[0], -q)
        raw_second += lax.dot_general(
            ref[0], cot[token], across_tokens, preferred_element_type=f32
        )
        raw_first += lax.dot_general(
            ref[1], normed[token], across_tokens, preferred_element_type=f32
        )
        total += jnp.sum(ref[1].astype(f32), 1, keepdims=True)
    shift, factor, gate = mods[0:1], mods[1:2], mods[2:3]
    weight = w1[...].astype(f32)
    sums[0:1] = jnp.sum(weight * total, 0, keepdims=True)
    sums[1:2] = jnp.sum(weight * raw_first, 0, keepdims=True)
    sums[2:3] = jnp.sum(w2[...].astype(f32) * raw_second, 0, keepdims=True)
    grad_first = (raw_first * factor + total * shift) * weight_scale
    grad_second = raw_second * (gate * weight_scale)
    first[...] = grad_first
    second[...] = grad_second
    send[0] = grad_first.astype(bf16)
    send[1] = grad_second.astype(bf16)


def clips_kernel(pos, first, second, other, first_out, second_out):
    first_out[...] = first[...] + other[0].astype(f32)
    second_out[...] = second[...] + other[1].astype(f32)


def core_kernel(pos, keep, other, o0, o1, o2, o3):
    for p, out in enumerate((o0, o1, o2, o3)):
        out[...] = (keep[p].astype(f32) + other[p].astype(f32)).astype(bf16)


def plane_kernel(pos, own, one, two, three, o0, o1, o2, o3):
    for s, out in enumerate((o0, o1, o2, o3)):
        out[...] = (
            own[s].astype(f32) + one[s].astype(f32) + two[s].astype(f32) + three[s].astype(f32)
        ).astype(bf16)


def states_kernel(pos, a0, a1, a2, a3, pair, t0, t1, t2, t3, norm_sums, scale, out):
    centre, inverse = combined([ref[pos[0]] for ref in (t0, t1, t2, t3)])
    grad_mod = a0[...].astype(f32) + a1[...].astype(f32) + a2[...].astype(f32) + a3[...].astype(f32)
    normed = (pair[0].astype(f32) - centre) * inverse
    grad_normed = grad_mod * (1.0 + scale[...])
    result = pair[1].astype(f32) + inverse * (
        grad_normed - norm_sums[0:1] / D - normed * (norm_sums[1:2] / D)
    )
    out[...] = result


def three_parts(values):
    first = values.astype(bf16)
    rest = values - first.astype(f32)
    second = rest.astype(bf16)
    third = (rest - second.astype(f32)).astype(bf16)
    return [first, second, third]


def shaped(shape, kind=bf16):
    return jax.ShapeDtypeStruct(shape, kind)


def on_device(states, cotangent, shift_mod, scale_mod, gate_mod, first_weight, second_weight):
    row, col = lax.axis_index("row"), lax.axis_index("col")
    high, x, core = col // INNER, lax.rem(col, INNER) // 2, lax.rem(col, 2)
    weight_one, weight_two = first_weight.T, second_weight.T
    pos = jnp.stack([row, high, x, core]).astype(jnp.int32)

    pair = jnp.stack([states[0].T, cotangent[0].T])
    planes = jnp.stack([spread_rows(pair, s) for s in range(4)])
    lines = [planes] + [along_x(planes, q) for q in (1, 2, 3)]
    blocks = []
    for line in lines:
        blocks += [line, across(line)]

    own_mods = jnp.stack([shift_mod[0], 1.0 + scale_mod[0], gate_mod[0]])
    moved = spread_rows(own_mods, 0)
    around = jnp.stack([moved, along_x(moved, 3), along_x(moved, 2), along_x(moved, 1)])
    around = jnp.roll(around, x, 0)
    facing = across(around)
    mods = jnp.stack(
        [jnp.where(core == 0, around, facing), jnp.where(core == 0, facing, around)], 1
    )
    mods_row = mods.transpose(2, 0, 1, 3).reshape(3, SLICE)
    mods_column = mods.reshape(INNER, 3, CHANNELS).transpose(0, 2, 1)

    parts = jnp.stack(three_parts(mods_row[0]) + three_parts(mods_row[1]))
    through = jnp.dot(parts, first_weight, preferred_element_type=f32)
    through = through.reshape(2, 3, UNITS).sum(1)
    through = through + along_row(through, 1) + along_row(through, 2) + along_row(through, 3)
    through = through.T

    block = pl.BlockSpec((1, 1, CHANNELS, TOK), lambda i, pos: (i, 0, 0, 0))
    stats = call(
        stats_kernel,
        (4,),
        [block] * 8,
        pl.BlockSpec((1, 2, TOK), lambda i, pos: (turn(pos[1], -i), 0, 0)),
        shaped((4, 2, TOK), f32),
        flops=4 * SLICE * TOK * 4,
        moved=SLICE * TOK * 8,
    )(pos, *blocks)
    stats = [stats] + [along_row(stats, q) for q in (1, 2, 3)]

    both = pl.BlockSpec((1, 2, CHANNELS, TOK), lambda i, pos: (i, 0, 0, 0))
    per_token = pl.BlockSpec(
        (1, INNER, CHANNELS, TOK), lambda i, pos: (turn(pos[1], -i), 0, 0, 0)
    )
    sums, normed, cot = call(
        forward_kernel,
        (4,),
        [both] * 8
        + [full((4, 2, TOK))] * 4
        + [full((INNER, CHANNELS, 3)), full((UNITS, SLICE)), full((UNITS, SLICE))],
        [
            pl.BlockSpec(
                (1, 2, UNITS, TOK),
                lambda i, pos: (turn(turn(pos[1], -i), -pos[0]), 0, 0, 0),
            ),
            per_token,
            per_token,
        ],
        [
            shaped((4, 2, UNITS, TOK)),
            shaped((4, INNER, CHANNELS, TOK)),
            shaped((4, INNER, CHANNELS, TOK)),
        ],
        [pltpu.VMEM((INNER, CHANNELS, TOK), bf16), pltpu.VMEM((INNER, CHANNELS, TOK), bf16)],
        flops=4 * 4 * UNITS * SLICE * TOK,
        moved=16 * SLICE * TOK + 4 * UNITS * SLICE,
    )(pos, *blocks, *stats, mods_column, weight_one, weight_two)
    normed = normed.reshape(4, SLICE, TOK)
    cot = cot.reshape(4, SLICE, TOK)

    arrived = [along_row(sums[q], q) for q in (1, 2, 3)]
    own_both, norm_sums = call(
        hidden_kernel,
        (1,),
        [full((1, 2, UNITS, TOK))] + [full((2, UNITS, TOK))] * 3 + [full((UNITS, 2))],
        [full((2, UNITS, TOK)), full((2, TOK))],
        [shaped((2, UNITS, TOK)), shaped((2, TOK), f32)],
        flops=2 * UNITS * TOK * 40,
        moved=20 * UNITS * TOK,
    )(pos, sums, *arrived, through)
    units = [own_both] + [along_row(own_both, q) for q in (1, 2, 3)]
    for mask in (1, 2, 4, 8, 16):
        norm_sums = norm_sums + across(norm_sums, mask)

    chunk = SLICE // 5
    rows = pl.BlockSpec((UNITS, chunk), lambda i, pos: (0, i))
    two_rows = pl.BlockSpec((2, UNITS, chunk), lambda i, pos: (0, 0, i))
    acts = pl.BlockSpec((4, chunk, TOK), lambda i, pos: (0, i, 0))
    vectors = pl.BlockSpec((3, chunk), lambda i, pos: (0, i))
    own_first, own_second, send_weights, mod_sums = call(
        weight_kernel,
        (5,),
        [full((2, UNITS, TOK))] * 4 + [acts, acts, vectors, rows, rows],
        [rows, rows, two_rows, vectors],
        [
            shaped((UNITS, SLICE), f32),
            shaped((UNITS, SLICE), f32),
            shaped((2, UNITS, SLICE)),
            shaped((3, SLICE), f32),
        ],
        flops=4 * 4 * UNITS * SLICE * TOK,
        moved=16 * SLICE * TOK + 16 * UNITS * SLICE,
    )(pos, *units, normed, cot, mods_row, weight_one, weight_two)
    other_weights = swap_clips(send_weights)

    grads = pl.BlockSpec((1, UNITS, TOK), lambda i, pos: (1, 0, 0))
    toward = pl.BlockSpec(
        (1, 4, CHANNELS, TOK), lambda i, pos: (turn(i, -pos[2]), 0, 0, 0)
    )
    keep, send = call(
        mod_kernel,
        (4,),
        [grads] * 4 + [pl.BlockSpec((2 * CHANNELS, UNITS), lambda i, pos: (i, 0))],
        [toward, toward],
        [shaped((4, 4, CHANNELS, TOK))] * 2,
        flops=2 * 4 * UNITS * SLICE * TOK,
        moved=8 * SLICE * TOK + 2 * UNITS * SLICE,
    )(pos, *units, first_weight)
    quarter = (4, CHANNELS, TOK)
    lines = call(
        core_kernel,
        (1,),
        [full((4, 4, CHANNELS, TOK))] * 2,
        [full(quarter)] * 4,
        [shaped(quarter)] * 4,
        flops=SLICE * TOK * 4,
        moved=12 * SLICE * TOK,
    )(pos, keep, across(send))
    planes = call(
        plane_kernel,
        (1,),
        [full(quarter)] * 4,
        [full((CHANNELS, TOK))] * 4,
        [shaped((CHANNELS, TOK))] * 4,
        flops=SLICE * TOK * 4,
        moved=4 * SLICE * TOK,
    )(pos, lines[0], *[along_x(lines[p], p) for p in (1, 2, 3)])
    pieces = [return_rows(planes[s], s) for s in range(4)]

    grad_states = call(
        states_kernel,
        (1,),
        [full((CHANNELS, TOK))] * 4
        + [full((2, CHANNELS, TOK))]
        + [full((4, 2, TOK))] * 4
        + [full((2, TOK)), full((CHANNELS, 1))],
        full((CHANNELS, TOK)),
        shaped((CHANNELS, TOK), f32),
        flops=CHANNELS * TOK * 20,
        moved=CHANNELS * TOK * 20,
    )(pos, *pieces, pair, *stats, norm_sums, scale_mod.T)

    mod_sums = mod_sums.reshape(3, 4, 2, CHANNELS)
    mine = jnp.where(core == 0, mod_sums[:, :, 0], mod_sums[:, :, 1])
    theirs = jnp.where(core == 0, mod_sums[:, :, 1], mod_sums[:, :, 0])
    mine = jnp.roll(mine + across(theirs), -x, 1)
    mine = mine[:, 0] + sum(along_x(mine[:, p], p) for p in (1, 2, 3))
    mine = sum(return_rows(mine, s) for s in range(4)) * token_scale

    grad_first, grad_second = call(
        clips_kernel,
        (5,),
        [rows, rows, two_rows],
        [rows, rows],
        [shaped((UNITS, SLICE), f32)] * 2,
        flops=2 * SLICE * UNITS,
        moved=20 * SLICE * UNITS,
    )(pos, own_first, own_second, other_weights)
    return (
        grad_states.T[None],
        grad_first.T,
        grad_second.T,
        mine[0][None],
        mine[1][None],
        mine[2][None],
    )


def solution(mesh):
    return jax.shard_map(
        on_device,
        mesh=mesh,
        in_specs=(
            P("dp", "row", "col"),
            P("dp", "row", "col"),
            P("dp", "col"),
            P("dp", "col"),
            P("dp", "col"),
            P("row", "col"),
            P("row", "col"),
        ),
        out_specs=(
            P("dp", "row", "col"),
            P("row", "col"),
            P("row", "col"),
            P("dp", "col"),
            P("dp", "col"),
            P("dp", "col"),
        ),
        check_vma=False,
    )
```

```python
import functools
import math

import jax
import jax.numpy as jnp
from jax import lax
from jax.experimental import pallas as pl
from jax.experimental.pallas import tpu as pltpu
from jax.sharding import PartitionSpec as P

D = 5120
FF = 13824
ROWS = 4
COLS = 32
INNER = 8
CHANNELS = D // COLS
UNITS = FF // COLS
TOK = 256
SLICE = D // ROWS
TOKENS = ROWS * TOK
EXTRA = 16
CHUNK = 256

bf16, f32 = jnp.bfloat16, jnp.float32

eps = 1e-06
tanh_factor = 0.7978845608028654
cubic_term = 0.044715
token_scale = 1.0 / math.sqrt(ROWS * TOK)
weight_scale = 1.0 / math.sqrt(2 * ROWS * TOK)
across_tokens = (((1,), (1,)), ((), ()))


def gelu_pair(values):
    squares = values * values
    inner = jnp.tanh(tanh_factor * (values + cubic_term * squares * values))
    half = 0.5 * (1.0 + inner)
    slope = half + 0.5 * values * (1.0 - inner * inner) * tanh_factor * (
        1.0 + 3.0 * cubic_term * squares
    )
    return values * half, slope


def turn(value, offset):
    return lax.rem(value + offset + 8, 4)


def spread_rows(values, shift):
    pairs = [
        (a * COLS + b * INNER + i, b * COLS + ((a + shift) % 4) * INNER + i)
        for a in range(4)
        for b in range(4)
        for i in range(INNER)
    ]
    return lax.ppermute(values, ("row", "col"), pairs)


def return_rows(values, shift):
    pairs = [
        (a * COLS + b * INNER + i, ((b + shift) % 4) * COLS + a * INNER + i)
        for a in range(4)
        for b in range(4)
        for i in range(INNER)
    ]
    return lax.ppermute(values, ("row", "col"), pairs)


def along_x(values, shift):
    pairs = [
        (h * 8 + x * 2 + k, h * 8 + ((x + shift) % 4) * 2 + k)
        for h in range(4)
        for x in range(4)
        for k in range(2)
    ]
    return lax.ppermute(values, "col", pairs)


def across(values):
    return lax.ppermute(values, "col", [(c, c ^ 1) for c in range(COLS)])


def along_row(values, shift):
    return lax.ppermute(values, "row", [(a, (a + shift) % 4) for a in range(4)])


def all_rows(values):
    return [values] + [along_row(values, q) for q in (1, 2, 3)]


def to_rows(values):
    return [values[0]] + [along_row(values[q], q) for q in (1, 2, 3)]


def swap_clips(values):
    return lax.ppermute(values, "dp", [(0, 1), (1, 0)])


def both_cores(lines):
    blocks = []
    for line in lines:
        blocks += [line, across(line)]
    return blocks


def after(values, other):
    return lax.optimization_barrier((values, other))[0]


cheap = pl.CostEstimate(flops=1024, bytes_accessed=1024, transcendentals=0)
some = pl.CostEstimate(flops=1024, bytes_accessed=8000000, transcendentals=0)
limit = pltpu.CompilerParams(vmem_limit_bytes=16 * 1024 * 1024)


def call(kernel, grid, in_specs, out_specs, out_shape, scratch=()):
    return pl.pallas_call(
        kernel,
        grid_spec=pltpu.PrefetchScalarGridSpec(
            num_scalar_prefetch=1,
            grid=grid,
            in_specs=in_specs,
            out_specs=out_specs,
            scratch_shapes=list(scratch),
        ),
        out_shape=out_shape,
        compiler_params=limit,
        cost_estimate=cheap,
    )


def whole(kernel, out_shape, scratch=(), cost=cheap):
    vmem = pl.BlockSpec(memory_space=pltpu.VMEM)

    def run(pos, *args):
        return pl.pallas_call(
            kernel,
            in_specs=[pl.BlockSpec(memory_space=pltpu.SMEM)] + [vmem] * len(args),
            out_specs=[vmem] * len(out_shape),
            out_shape=out_shape,
            scratch_shapes=list(scratch),
            compiler_params=limit,
            cost_estimate=cost,
        )(pos, *args)

    return run


def full(shape):
    return pl.BlockSpec(shape, lambda i, pos: (0,) * len(shape))


def shaped(shape, kind=bf16):
    return jax.ShapeDtypeStruct(shape, kind)


def place_of(pos, token):
    return turn(pos[1] - token, -1)


def channel_block(pos, q, flip):
    core = pos[3] if flip == 0 else 1 - pos[3]
    return turn(pos[2], -q) * 2 + core


def parts_of(values, count):
    parts = []
    for _ in range(count):
        parts.append(values.astype(bf16).astype(f32))
        values = values - parts[-1]
    return parts


def packed(values):
    return jnp.concatenate(parts_of(values, 2), 0).astype(bf16)


def unpacked(rows):
    wide = rows.astype(f32)
    return wide[0:8] + wide[8:16]


def pack_kernel(pos, plain, mods, out):
    rows = parts_of(mods[...], 3) + [jnp.zeros((EXTRA - 9, CHANNELS), f32)]
    out[: 2 * CHANNELS] = plain[...]
    out[2 * CHANNELS :] = jnp.zeros((EXTRA, TOK), bf16)
    out[2 * CHANNELS :, :CHANNELS] = jnp.concatenate(rows, 0).astype(bf16)


def sort_kernel(pos, b0, b1, b2, b3, x, cot):
    for at, ref in enumerate((b0, b1, b2, b3)):
        rows = slice(at * CHANNELS, (at + 1) * CHANNELS)
        x[rows] = ref[:CHANNELS]
        cot[rows] = ref[CHANNELS : 2 * CHANNELS]
    x[4 * CHANNELS :] = b3[2 * CHANNELS :]


def mods_kernel(pos, *refs):
    mods, w1, mods_column, mods_row, through_out = refs[:8], refs[8], refs[9], refs[10], refs[11]
    for q in range(4):
        for flip in range(2):
            rows = mods[2 * q + flip][4 * CHANNELS :].astype(f32)
            values = jnp.concatenate([rows[0:3] + rows[3:6] + rows[6:9], rows[9:14]], 0)
            mods_column[channel_block(pos, q, flip)] = values.T[:CHANNELS]
    values = mods_column[...].reshape(SLICE, 8).T
    mods_row[...] = values
    rows = jnp.concatenate(parts_of(values, 3) + [jnp.zeros_like(values)], 0).astype(bf16)
    through = lax.dot_general(rows, w1[...], across_tokens, preferred_element_type=f32)
    through = through[0:8] + through[8:16] + through[16:24]
    through_out[...] = jnp.zeros((8, TOK), f32)
    for at, line in ((0, through[1:2]), (2, through[0:1])):
        through_out[at : at + 1] = line[:, :TOK]
        through_out[at + 1 : at + 2, : UNITS - TOK] = line[:, TOK:]


def first_kernel(shift, pos, *refs):
    blocks, mods, through, w1, out, offsets = refs[:8], refs[8], refs[9], refs[10], refs[11], refs[12]
    place = place_of(pos, turn(pos[0], shift))
    rows = pl.ds(pl.multiple_of(place * CHANNELS, 32), CHANNELS)
    total = 0.0
    for ref in blocks:
        total = total + jnp.sum(ref[rows, :].astype(f32), 0, keepdims=True)
    mean = total / SLICE
    square = 0.0
    for q in range(4):
        for flip in range(2):
            j = channel_block(pos, q, flip)
            offset = blocks[2 * q + flip][rows, :].astype(f32) - mean
            square = square + jnp.sum(offset * offset, 0, keepdims=True)
            offsets[j] = (offset * mods[j][:, 1:2]).astype(bf16)
    out[:UNITS] = jnp.dot(
        w1[...], offsets[...].reshape(SLICE, TOK), preferred_element_type=f32
    ).astype(bf16)
    four = jnp.concatenate([mean, square, through[0:2]], 0)
    extra = parts_of(four, 3) + parts_of(through[2:4], 2)
    out[UNITS:] = jnp.concatenate(extra, 0).astype(bf16)


def hidden_kernel(pos, p0, p1, p2, p3, hidden_out, slope_out, rest_out, factor_out, stats_out):
    parts = (p0, p1, p2, p3)
    extras = [ref[UNITS:].astype(f32) for ref in parts]
    fours = [e[0:4] + e[4:8] + e[8:12] for e in extras]
    shifts = sum(e[12:14] + e[14:16] for e in extras)
    centre = 0.25 * (fours[0][0:1] + fours[1][0:1] + fours[2][0:1] + fours[3][0:1])
    spread = 0.0
    for four in fours:
        spread = spread + four[1:2] + SLICE * (four[0:1] - centre) ** 2
    inverse = lax.rsqrt(spread / D + eps)
    stats = jnp.concatenate([centre, inverse], 0)
    stats_out[...] = stats
    hidden_out[UNITS:] = jnp.concatenate(
        parts_of(stats, 3) + [jnp.zeros((EXTRA - 6, TOK), f32)], 0
    ).astype(bf16)
    columns = jnp.concatenate([four[2:4] for four in fours] + [shifts] * 4, 0).T
    for half, at in ((0, slice(0, TOK)), (1, slice(TOK, UNITS))):
        size = at.stop - at.start
        rest, total = 0.0, 0.0
        for i, ref in enumerate(parts):
            factor = columns[:size, 2 * i + half : 2 * i + half + 1]
            total = total + factor
            rest = rest + (ref[at].astype(f32) + factor * (fours[i][0:1] - centre))
        rest = rest * inverse
        hidden, slope = gelu_pair(rest + columns[:size, 8 + half : 9 + half])
        hidden_out[at] = hidden.astype(bf16)
        slope_out[at] = slope
        rest_out[at] = rest
        factor_out[at] = total


def second_kernel(pos, *refs):
    blocks, mods, w2 = refs[:8], refs[8], refs[9]
    sums, cot_out, scaled = refs[10:14], refs[14], refs[15]
    for shift, out in enumerate(sums):
        token = turn(pos[0], shift)
        source = pl.ds(pl.multiple_of(place_of(pos, token) * CHANNELS, 32), CHANNELS)
        lanes = pl.ds(pl.multiple_of(token * TOK, TOK), TOK)
        for q in range(4):
            for flip in range(2):
                j = channel_block(pos, q, flip)
                block = blocks[2 * q + flip][source, :]
                rows = pl.ds(pl.multiple_of(j * CHANNELS, 32), CHANNELS)
                cot_out[rows, lanes] = block
                scaled[shift, rows, :] = (block.astype(f32) * mods[j][:, 2:3]).astype(bf16)
        out[...] = jnp.dot(w2[...], scaled[shift], preferred_element_type=f32).astype(bf16)


def grad_kernel(pos, own, one, two, three, slope, rest, factor, out):
    grad = own[...].astype(f32) + one[...].astype(f32)
    grad = grad + (two[...].astype(f32) + three[...].astype(f32))
    grad = (grad * slope[...]).astype(bf16)
    out[:UNITS] = grad
    wide = grad.astype(f32)
    first = jnp.sum(wide * factor[...], 0, keepdims=True)
    second = jnp.sum(wide * rest[...], 0, keepdims=True)
    line = lax.broadcasted_iota(jnp.int32, (8, TOK), 0)
    out[UNITS:] = packed(jnp.where(line == 3, first, jnp.where(line == 4, second, 0.0)))


def normed_kernel(pos, *refs):
    blocks, hiddens, out = refs[:8], refs[8:12], refs[12]
    for at, ref in enumerate(hiddens):
        token = turn(pos[0], -at)
        source = pl.ds(pl.multiple_of(place_of(pos, token) * CHANNELS, 32), CHANNELS)
        lanes = pl.ds(pl.multiple_of(token * TOK, TOK), TOK)
        extra = ref[UNITS:].astype(f32)
        stats = extra[0:2] + extra[2:4] + extra[4:6]
        centre, inverse = stats[0:1], stats[1:2]
        for q in range(4):
            for flip in range(2):
                j = channel_block(pos, q, flip)
                normed = (blocks[2 * q + flip][source, :].astype(f32) - centre) * inverse
                rows = pl.ds(pl.multiple_of(j * CHANNELS, 32), CHANNELS)
                out[rows, lanes] = normed.astype(bf16)


def collect(pos, refs, store):
    for q, ref in enumerate(refs):
        at = pl.multiple_of(turn(pos[0], -q) * TOK, TOK)
        store[:, pl.ds(at, TOK)] = ref[:UNITS]


def second_weight_kernel(pos, b0, b1, b2, b3, cot, mods, w2, send, sums, store):
    collect(pos, (b0, b1, b2, b3), store)
    line = lax.broadcasted_iota(jnp.int32, (8, CHUNK), 0)
    for at in range(0, SLICE, CHUNK):
        part = slice(at, at + CHUNK)
        raw = lax.dot_general(
            store[...], cot[part, :], across_tokens, preferred_element_type=f32
        )
        total = jnp.sum(w2[:, part].astype(f32) * raw, 0, keepdims=True)
        sums[part, :] = jnp.where(line == 2, total, 0.0).T
        send[:, part] = (raw * (mods[2:3, part] * weight_scale)).astype(bf16)


def first_weight_kernel(pos, b0, b1, b2, b3, normed, mods, w1, send, sums, store):
    collect(pos, (b0, b1, b2, b3), store)
    total = jnp.sum(store[...].astype(f32), 1, keepdims=True)
    line = lax.broadcasted_iota(jnp.int32, (8, CHUNK), 0)
    for at in range(0, SLICE, CHUNK):
        part = slice(at, at + CHUNK)
        raw = lax.dot_general(
            store[...], normed[part, :], across_tokens, preferred_element_type=f32
        )
        weight = w1[:, part].astype(f32)
        shift = jnp.sum(weight * total, 0, keepdims=True)
        scale = jnp.sum(weight * raw, 0, keepdims=True)
        sums[part, :] = jnp.where(line == 0, shift, jnp.where(line == 1, scale, 0.0)).T
        grad = (raw * mods[1:2, part] + total * mods[0:1, part]) * weight_scale
        send[:, part] = grad.astype(bf16)


def mod_kernel(pos, g0, g1, g2, g3, w1, sums_one, sums_two, *rest):
    keeps, sends, store, line = rest[:4], rest[4:8], rest[8], rest[9]
    grads = (g0, g1, g2, g3)
    collect(pos, grads, store)
    line[...] = jnp.zeros((8, TOK), f32)
    smalls = [unpacked(ref[UNITS:]) for ref in grads]
    for core, outs in ((pos[3], keeps), (1 - pos[3], sends)):
        for p, out in enumerate(outs):
            j = turn(pos[2], p) * 2 + core
            rows = pl.ds(pl.multiple_of(j * CHANNELS, 32), CHANNELS)
            product = jnp.dot(w1[rows, :], store[...], preferred_element_type=f32).astype(bf16)
            for token in range(4):
                out[turn(token, -pos[1]), :CHANNELS] = product[
                    :, token * TOK : (token + 1) * TOK
                ]
            line[:, :CHANNELS] = (sums_one[j] + sums_two[j]).T
            for q, small in enumerate(smalls):
                out[turn(pos[0], -q - pos[1]), CHANNELS:] = packed(small + line[...])


def add_up(out, parts):
    total = parts[0][:CHANNELS].astype(f32)
    small = unpacked(parts[0][CHANNELS:])
    for part in parts[1:]:
        total = total + part[:CHANNELS].astype(f32)
        small = small + unpacked(part[CHANNELS:])
    out[:CHANNELS] = total.astype(bf16)
    out[CHANNELS:] = packed(small)


def core_kernel(pos, *refs):
    for keep, other, out in zip(refs[:4], refs[4:8], refs[8:]):
        for s in range(4):
            add_up(out.at[s], [keep.at[s], other.at[s]])


def plane_kernel(pos, own, one, two, three, o0, o1, o2, o3):
    for s, out in enumerate((o0, o1, o2, o3)):
        add_up(out, [ref.at[s] for ref in (own, one, two, three)])


def states_kernel(pos, a0, a1, a2, a3, x, cot, stats, scale, out, mods_out):
    centre, inverse = stats[0:1], stats[1:2]
    grad_mod, small = 0.0, 0.0
    for ref in (a0, a1, a2, a3):
        grad_mod = grad_mod + ref[:CHANNELS].astype(f32)
        small = small + unpacked(ref[CHANNELS:])
    normed = (x[...].astype(f32) - centre) * inverse
    grad_normed = grad_mod * (1.0 + scale[...])
    out[...] = cot[...].astype(f32) + inverse * (
        grad_normed - small[3:4] / D - normed * (small[4:5] / D)
    )
    mods_out[...] = small * token_scale


def clips_kernel(pos, own, other, out):
    out[...] = own[...].astype(f32) + other[...].astype(f32)


def on_device(states, cotangent, shift_mod, scale_mod, gate_mod, first_weight, second_weight):
    row, col = lax.axis_index("row"), lax.axis_index("col")
    high, x, core = col // INNER, lax.rem(col, INNER) // 2, lax.rem(col, 2)
    pos = jnp.stack([row, high, x, core]).astype(jnp.int32)
    weight_one, weight_two = first_weight.T, second_weight.T
    own_x, own_c = states[0].T, cotangent[0].T

    own = (CHANNELS, TOK)
    piece = (CHANNELS + EXTRA, TOK)
    units = (UNITS, TOK)
    wide_units = (UNITS + EXTRA, TOK)
    stage = pltpu.VMEM((INNER, CHANNELS, TOK), bf16)

    pair = (2 * CHANNELS, TOK)
    wide_pair = (2 * CHANNELS + EXTRA, TOK)
    plain = jnp.concatenate([own_x, own_c], 0)
    (with_mods,) = whole(pack_kernel, [shaped(wide_pair)])(
        pos, plain, jnp.concatenate([shift_mod, 1.0 + scale_mod, gate_mod], 0)
    )
    x_planes, c_planes = whole(
        sort_kernel,
        [shaped((4 * CHANNELS + EXTRA, TOK)), shaped((4 * CHANNELS, TOK))],
    )(pos, *[spread_rows(plain, s) for s in (1, 2, 3)], spread_rows(with_mods, 0))
    x_lines = [x_planes] + [along_x(x_planes, q) for q in (1, 2, 3)]
    x_blocks = both_cores(x_lines)
    c_planes = after(c_planes, x_lines)
    c_lines = [c_planes] + [along_x(c_planes, q) for q in (1, 2, 3)]

    mods_column, mods_row, through = whole(
        mods_kernel,
        [
            shaped((INNER, CHANNELS, 8), f32),
            shaped((8, SLICE), f32),
            shaped((8, TOK), f32),
        ],
    )(pos, *x_blocks, weight_one)

    pre_sums = [None] * 4
    blocks = x_blocks
    for shift in (2, 1, 3, 0):
        (pre_sums[shift],) = whole(
            functools.partial(first_kernel, shift), [shaped(wide_units)], [stage], some
        )(pos, *blocks, mods_column, through, weight_one)
        blocks = after(blocks, pre_sums[shift])
    pre_sums = to_rows(pre_sums)
    c_blocks = both_cores(after(c_lines, (pre_sums[0], pre_sums[2])))
    *grad_sums, cot = whole(
        second_kernel,
        [shaped(units)] * 4 + [shaped((SLICE, TOKENS))],
        [pltpu.VMEM((4, SLICE, TOK), bf16)],
    )(pos, *c_blocks, mods_column, weight_two)
    grad_sums = to_rows(grad_sums)
    hidden, slope, rest, factor, stats = whole(
        hidden_kernel,
        [
            shaped(wide_units),
            shaped(units, f32),
            shaped(units, f32),
            shaped((UNITS, 1), f32),
            shaped((2, TOK), f32),
        ],
    )(pos, *after(pre_sums, cot))
    hidden = all_rows(hidden)

    weights = pl.BlockSpec((UNITS, CHUNK), lambda i, pos: (0, i))
    scratch = [pltpu.VMEM((UNITS, TOKENS), bf16)]

    def gradient_call(kernel, arrays, activations, weight):
        return whole(kernel, [shaped((UNITS, SLICE)), shaped((SLICE, 8), f32)], scratch)(
            pos, *arrays, activations, mods_row, weight
        )

    own_second, sums_second = gradient_call(
        second_weight_kernel, hidden, cot, weight_two
    )
    other_second = swap_clips(own_second)
    (grad_pre,) = whole(grad_kernel, [shaped(wide_units)])(
        pos, *grad_sums, slope, rest, factor
    )
    grad_pre = all_rows(grad_pre)
    (normed,) = whole(normed_kernel, [shaped((SLICE, TOKENS))])(
        pos, *after(x_blocks, grad_pre[1]), *hidden
    )
    own_first, sums_first = gradient_call(first_weight_kernel, grad_pre, normed, weight_one)
    other_first = swap_clips(own_first)

    quarter = (4,) + piece
    terms = whole(
        mod_kernel, [shaped(quarter)] * 8, scratch + [pltpu.VMEM((8, TOK), f32)]
    )(
        pos,
        *grad_pre,
        first_weight,
        sums_first.reshape(INNER, CHANNELS, 8),
        sums_second.reshape(INNER, CHANNELS, 8),
    )
    lines = whole(core_kernel, [shaped(quarter)] * 4)(
        pos, *terms[:4], *[across(term) for term in terms[4:]]
    )
    planes = whole(plane_kernel, [shaped(piece)] * 4)(
        pos, lines[0], *after([along_x(lines[p], p) for p in (1, 2, 3)], other_second)
    )
    pieces = [return_rows(planes[s], s) for s in range(4)]

    def clips_call(own, other):
        return call(
            clips_kernel,
            (SLICE // CHUNK,),
            [weights, weights],
            weights,
            shaped((UNITS, SLICE), f32),
        )(pos, own, other)

    grad_second = clips_call(own_second, other_second)
    grad_first = clips_call(own_first, other_first)
    grad_states, mods_grad = whole(
        states_kernel, [shaped(own, f32), shaped((8, TOK), f32)]
    )(pos, *pieces, own_x, own_c, stats, scale_mod.T)
    return (
        grad_states.T[None],
        grad_first.T,
        grad_second.T,
        mods_grad[0:1, :CHANNELS],
        mods_grad[1:2, :CHANNELS],
        mods_grad[2:3, :CHANNELS],
    )


def solution(mesh):
    return jax.shard_map(
        on_device,
        mesh=mesh,
        in_specs=(
            P("dp", "row", "col"),
            P("dp", "row", "col"),
            P("dp", "col"),
            P("dp", "col"),
            P("dp", "col"),
            P("row", "col"),
            P("row", "col"),
        ),
        out_specs=(
            P("dp", "row", "col"),
            P("row", "col"),
            P("row", "col"),
            P("dp", "col"),
            P("dp", "col"),
            P("dp", "col"),
        ),
        check_vma=False,
    )
```

```python
import functools
import math

import jax
import jax.numpy as jnp
from jax import lax
from jax.experimental import pallas as pl
from jax.experimental.pallas import tpu as pltpu
from jax.sharding import PartitionSpec as P

D = 5120
FF = 13824
ROWS = 4
COLS = 32
INNER = 8
CHANNELS = D // COLS
UNITS = FF // COLS
TOK = 256
SLICE = D // ROWS
TOKENS = ROWS * TOK
EXTRA = 16
CHUNK = 256

bf16, f32 = jnp.bfloat16, jnp.float32

eps = 1e-06
tanh_factor = 0.7978845608028654
cubic_term = 0.044715
token_scale = 1.0 / math.sqrt(ROWS * TOK)
weight_scale = 1.0 / math.sqrt(2 * ROWS * TOK)
across_tokens = (((1,), (1,)), ((), ()))


def gelu_pair(values):
    squares = values * values
    inner = jnp.tanh(tanh_factor * (values + cubic_term * squares * values))
    half = 0.5 * (1.0 + inner)
    slope = half + 0.5 * values * (1.0 - inner * inner) * tanh_factor * (
        1.0 + 3.0 * cubic_term * squares
    )
    return values * half, slope


def turn(value, offset):
    return lax.rem(value + offset + 8, 4)


def spread_rows(values, shift):
    pairs = [
        (a * COLS + b * INNER + i, b * COLS + ((a + shift) % 4) * INNER + i)
        for a in range(4)
        for b in range(4)
        for i in range(INNER)
    ]
    return lax.ppermute(values, ("row", "col"), pairs)


def return_rows(values, shift):
    pairs = [
        (a * COLS + b * INNER + i, ((b + shift) % 4) * COLS + a * INNER + i)
        for a in range(4)
        for b in range(4)
        for i in range(INNER)
    ]
    return lax.ppermute(values, ("row", "col"), pairs)


def along_x(values, shift):
    pairs = [
        (h * 8 + x * 2 + k, h * 8 + ((x + shift) % 4) * 2 + k)
        for h in range(4)
        for x in range(4)
        for k in range(2)
    ]
    return lax.ppermute(values, "col", pairs)


def across(values):
    return lax.ppermute(values, "col", [(c, c ^ 1) for c in range(COLS)])


def along_row(values, shift):
    return lax.ppermute(values, "row", [(a, (a + shift) % 4) for a in range(4)])


def all_rows(values):
    return [values] + [along_row(values, q) for q in (1, 2, 3)]


def to_rows(values):
    return [values[0]] + [along_row(values[q], q) for q in (1, 2, 3)]


def swap_clips(values):
    return lax.ppermute(values, "dp", [(0, 1), (1, 0)])


def both_cores(pos, lines):
    shape = shaped((2 * lines[0].shape[0], TOK))
    packs = whole(pair_kernel, [shape, shape])(pos, *lines)
    return list(lines) + [across(pack) for pack in packs]


def after(values, other):
    return lax.optimization_barrier((values, other))[0]


cheap = pl.CostEstimate(flops=1024, bytes_accessed=1024, transcendentals=0)
some = pl.CostEstimate(flops=1024, bytes_accessed=8000000, transcendentals=0)
limit = pltpu.CompilerParams(vmem_limit_bytes=16 * 1024 * 1024)


def call(kernel, grid, in_specs, out_specs, out_shape, scratch=()):
    return pl.pallas_call(
        kernel,
        grid_spec=pltpu.PrefetchScalarGridSpec(
            num_scalar_prefetch=1,
            grid=grid,
            in_specs=in_specs,
            out_specs=out_specs,
            scratch_shapes=list(scratch),
        ),
        out_shape=out_shape,
        compiler_params=limit,
        cost_estimate=cheap,
    )


def whole(kernel, out_shape, scratch=(), cost=cheap):
    vmem = pl.BlockSpec(memory_space=pltpu.VMEM)

    def run(pos, *args):
        return pl.pallas_call(
            kernel,
            in_specs=[pl.BlockSpec(memory_space=pltpu.SMEM)] + [vmem] * len(args),
            out_specs=[vmem] * len(out_shape),
            out_shape=out_shape,
            scratch_shapes=list(scratch),
            compiler_params=limit,
            cost_estimate=cost,
        )(pos, *args)

    return run


def full(shape):
    return pl.BlockSpec(shape, lambda i, pos: (0,) * len(shape))


def shaped(shape, kind=bf16):
    return jax.ShapeDtypeStruct(shape, kind)


def place_of(pos, token):
    return turn(pos[1] - token, -1)


def channel_block(pos, q, flip):
    core = pos[3] if flip == 0 else 1 - pos[3]
    return turn(pos[2], -q) * 2 + core


def parts_of(values, count):
    parts = []
    for _ in range(count):
        parts.append(values.astype(bf16).astype(f32))
        values = values - parts[-1]
    return parts


def packed(values):
    return jnp.concatenate(parts_of(values, 2), 0).astype(bf16)


def unpacked(rows):
    wide = rows.astype(f32)
    return wide[0:8] + wide[8:16]


def pack_kernel(pos, plain, mods, out):
    rows = parts_of(mods[...], 3) + [jnp.zeros((EXTRA - 9, CHANNELS), f32)]
    out[: 2 * CHANNELS] = plain[...]
    out[2 * CHANNELS :] = jnp.zeros((EXTRA, TOK), bf16)
    out[2 * CHANNELS :, :CHANNELS] = jnp.concatenate(rows, 0).astype(bf16)


def pair_kernel(pos, l0, l1, l2, l3, first, second):
    rows = l0.shape[0]
    first[:rows], first[rows:] = l0[...], l1[...]
    second[:rows], second[rows:] = l2[...], l3[...]


def block_of(blocks, q, flip, at, size):
    if flip == 0:
        return blocks[q][pl.ds(at, size), :]
    rows = blocks[0].shape[0]
    return blocks[4 + q // 2][pl.ds(at + (q % 2) * rows, size), :]


def sort_kernel(pos, b0, b1, b2, b3, x, cot):
    for at, ref in enumerate((b0, b1, b2, b3)):
        rows = slice(at * CHANNELS, (at + 1) * CHANNELS)
        x[rows] = ref[:CHANNELS]
        cot[rows] = ref[CHANNELS : 2 * CHANNELS]
    x[4 * CHANNELS :] = b3[2 * CHANNELS :]


def turned_kernel(pos, w1, out):
    out[...] = w1[...].T


def mods_kernel(pos, *refs):
    blocks, w1, mods_column, mods_row, through_out = refs[:6], refs[6], refs[7], refs[8], refs[9]
    for q in range(4):
        for flip in range(2):
            rows = block_of(blocks, q, flip, 4 * CHANNELS, EXTRA).astype(f32)
            values = jnp.concatenate([rows[0:3] + rows[3:6] + rows[6:9], rows[9:14]], 0)
            mods_column[channel_block(pos, q, flip)] = values.T[:CHANNELS]
    values = mods_column[...].reshape(SLICE, 8).T
    mods_row[...] = values
    rows = jnp.concatenate(parts_of(values, 3) + [jnp.zeros_like(values)], 0).astype(bf16)
    through = lax.dot_general(rows, w1[...], across_tokens, preferred_element_type=f32)
    through = through[0:8] + through[8:16] + through[16:24]
    through_out[...] = jnp.zeros((8, TOK), f32)
    for at, line in ((0, through[1:2]), (2, through[0:1])):
        through_out[at : at + 1] = line[:, :TOK]
        through_out[at + 1 : at + 2, : UNITS - TOK] = line[:, TOK:]


def first_kernel(shift, pos, *refs):
    blocks, mods, through, w1 = refs[:6], refs[6], refs[7], refs[8]
    out, offset_out, mean_out, offsets = refs[9:]
    place = place_of(pos, turn(pos[0], shift))
    at = pl.multiple_of(place * CHANNELS, 32)
    total = 0.0
    for q in range(4):
        for flip in range(2):
            block = block_of(blocks, q, flip, at, CHANNELS).astype(f32)
            total = total + jnp.sum(block, 0, keepdims=True)
    mean = total / SLICE
    square = 0.0
    for q in range(4):
        for flip in range(2):
            j = channel_block(pos, q, flip)
            offset = block_of(blocks, q, flip, at, CHANNELS).astype(f32) - mean
            square = square + jnp.sum(offset * offset, 0, keepdims=True)
            offsets[j] = (offset * mods[j][:, 1:2]).astype(bf16)
            rows = pl.ds(pl.multiple_of(j * CHANNELS, 32), CHANNELS)
            offset_out[rows, :] = offset.astype(bf16)
    mean_out[...] = mean
    out[:UNITS] = jnp.dot(
        w1[...], offsets[...].reshape(SLICE, TOK), preferred_element_type=f32
    ).astype(bf16)
    four = jnp.concatenate([mean, square, through[0:2]], 0)
    extra = parts_of(four, 3) + parts_of(through[2:4], 2)
    out[UNITS:] = jnp.concatenate(extra, 0).astype(bf16)


def hidden_kernel(pos, p0, p1, p2, p3, hidden_out, slope_out, rest_out, factor_out, stats_out):
    parts = (p0, p1, p2, p3)
    extras = [ref[UNITS:].astype(f32) for ref in parts]
    fours = [e[0:4] + e[4:8] + e[8:12] for e in extras]
    shifts = sum(e[12:14] + e[14:16] for e in extras)
    centre = 0.25 * (fours[0][0:1] + fours[1][0:1] + fours[2][0:1] + fours[3][0:1])
    spread = 0.0
    for four in fours:
        spread = spread + four[1:2] + SLICE * (four[0:1] - centre) ** 2
    inverse = lax.rsqrt(spread / D + eps)
    stats = jnp.concatenate([centre, inverse], 0)
    stats_out[...] = stats
    hidden_out[UNITS:] = jnp.concatenate(
        parts_of(stats, 3) + [jnp.zeros((EXTRA - 6, TOK), f32)], 0
    ).astype(bf16)
    columns = jnp.concatenate([four[2:4] for four in fours] + [shifts] * 4, 0).T
    for half, at in ((0, slice(0, TOK)), (1, slice(TOK, UNITS))):
        size = at.stop - at.start
        rest, total = 0.0, 0.0
        for i, ref in enumerate(parts):
            factor = columns[:size, 2 * i + half : 2 * i + half + 1]
            total = total + factor
            rest = rest + (ref[at].astype(f32) + factor * (fours[i][0:1] - centre))
        rest = rest * inverse
        hidden, slope = gelu_pair(rest + columns[:size, 8 + half : 9 + half])
        hidden_out[at] = hidden.astype(bf16)
        slope_out[at] = slope
        rest_out[at] = rest
        factor_out[at] = total


def second_kernel(pos, *refs):
    blocks, mods, w2 = refs[:6], refs[6], refs[7]
    sums, cot_out, scaled = refs[8:12], refs[12], refs[13]
    for shift, out in enumerate(sums):
        token = turn(pos[0], shift)
        at = pl.multiple_of(place_of(pos, token) * CHANNELS, 32)
        lanes = pl.ds(pl.multiple_of(token * TOK, TOK), TOK)
        for q in range(4):
            for flip in range(2):
                j = channel_block(pos, q, flip)
                block = block_of(blocks, q, flip, at, CHANNELS)
                rows = pl.ds(pl.multiple_of(j * CHANNELS, 32), CHANNELS)
                cot_out[rows, lanes] = block
                scaled[shift, rows, :] = (block.astype(f32) * mods[j][:, 2:3]).astype(bf16)
        out[...] = jnp.dot(w2[...], scaled[shift], preferred_element_type=f32).astype(bf16)


def grad_kernel(pos, own, one, two, three, slope, rest, factor, out):
    grad = own[...].astype(f32) + one[...].astype(f32)
    grad = grad + (two[...].astype(f32) + three[...].astype(f32))
    grad = (grad * slope[...]).astype(bf16)
    out[:UNITS] = grad
    wide = grad.astype(f32)
    first = jnp.sum(wide * factor[...], 0, keepdims=True)
    second = jnp.sum(wide * rest[...], 0, keepdims=True)
    line = lax.broadcasted_iota(jnp.int32, (8, TOK), 0)
    out[UNITS:] = packed(jnp.where(line == 3, first, jnp.where(line == 4, second, 0.0)))


def collect(pos, refs, store):
    for q, ref in enumerate(refs):
        at = pl.multiple_of(turn(pos[0], -q) * TOK, TOK)
        store[:, pl.ds(at, TOK)] = ref[:UNITS]


def second_weight_kernel(pos, b0, b1, b2, b3, cot, mods, w2, send, sums, store):
    collect(pos, (b0, b1, b2, b3), store)
    line = lax.broadcasted_iota(jnp.int32, (8, CHUNK), 0)
    for at in range(0, SLICE, CHUNK):
        part = slice(at, at + CHUNK)
        raw = lax.dot_general(
            store[...], cot[part, :], across_tokens, preferred_element_type=f32
        )
        total = jnp.sum(w2[:, part].astype(f32) * raw, 0, keepdims=True)
        sums[part, :] = jnp.where(line == 2, total, 0.0).T
        send[:, part] = (raw * (mods[2:3, part] * weight_scale)).astype(bf16)


def first_weight_kernel(pos, *refs):
    grads, hiddens, offsets, means = refs[:4], refs[4:8], refs[8:12], refs[12:16]
    mods, w1, send, sums, store, others = refs[16:]
    total, lift = 0.0, 0.0
    for q in range(4):
        at = (4 - q) % 4
        extra = hiddens[q][UNITS:].astype(f32)
        stats = extra[0:2] + extra[2:4] + extra[4:6]
        grad = grads[q][:UNITS].astype(f32)
        total = total + jnp.sum(grad, 1, keepdims=True)
        grad = grad * stats[1:2]
        lift = lift + jnp.sum(grad * (means[at][...] - stats[0:1]), 1, keepdims=True)
        lanes = slice(at * TOK, (at + 1) * TOK)
        store[:, lanes] = grad.astype(bf16)
        others[:, lanes] = offsets[at][...]
    line = lax.broadcasted_iota(jnp.int32, (8, CHUNK), 0)
    for at in range(0, SLICE, CHUNK):
        part = slice(at, at + CHUNK)
        raw = lift + lax.dot_general(
            store[...], others[part, :], across_tokens, preferred_element_type=f32
        )
        weight = w1[:, part].astype(f32)
        shift = jnp.sum(weight * total, 0, keepdims=True)
        scale = jnp.sum(weight * raw, 0, keepdims=True)
        sums[part, :] = jnp.where(line == 0, shift, jnp.where(line == 1, scale, 0.0)).T
        grad = (raw * mods[1:2, part] + total * mods[0:1, part]) * weight_scale
        send[:, part] = grad.astype(bf16)


def mod_kernel(pos, g0, g1, g2, g3, w1, sums_one, sums_two, *rest):
    keeps, sends, store, line = rest[:4], rest[4:8], rest[8], rest[9]
    grads = (g0, g1, g2, g3)
    collect(pos, grads, store)
    line[...] = jnp.zeros((8, TOK), f32)
    smalls = [unpacked(ref[UNITS:]) for ref in grads]
    for core, outs in ((pos[3], keeps), (1 - pos[3], sends)):
        for p, out in enumerate(outs):
            j = turn(pos[2], p) * 2 + core
            rows = pl.ds(pl.multiple_of(j * CHANNELS, 32), CHANNELS)
            product = jnp.dot(w1[rows, :], store[...], preferred_element_type=f32).astype(bf16)
            for token in range(4):
                out[turn(token, -pos[1]), :CHANNELS] = product[
                    :, token * TOK : (token + 1) * TOK
                ]
            line[:, :CHANNELS] = (sums_one[j] + sums_two[j]).T
            for q, small in enumerate(smalls):
                out[turn(pos[0], -q - pos[1]), CHANNELS:] = packed(small + line[...])


def add_up(out, parts):
    total = parts[0][:CHANNELS].astype(f32)
    small = unpacked(parts[0][CHANNELS:])
    for part in parts[1:]:
        total = total + part[:CHANNELS].astype(f32)
        small = small + unpacked(part[CHANNELS:])
    out[:CHANNELS] = total.astype(bf16)
    out[CHANNELS:] = packed(small)


def core_kernel(pos, *refs):
    for keep, other, out in zip(refs[:4], refs[4:8], refs[8:]):
        for s in range(4):
            add_up(out.at[s], [keep.at[s], other.at[s]])


def plane_kernel(pos, own, one, two, three, o0, o1, o2, o3):
    for s, out in enumerate((o0, o1, o2, o3)):
        add_up(out, [ref.at[s] for ref in (own, one, two, three)])


def states_kernel(pos, a0, a1, a2, a3, x, cot, stats, scale, out, mods_out):
    centre, inverse = stats[0:1], stats[1:2]
    grad_mod, small = 0.0, 0.0
    for ref in (a0, a1, a2, a3):
        grad_mod = grad_mod + ref[:CHANNELS].astype(f32)
        small = small + unpacked(ref[CHANNELS:])
    normed = (x[...].astype(f32) - centre) * inverse
    grad_normed = grad_mod * (1.0 + scale[...])
    out[...] = cot[...].astype(f32) + inverse * (
        grad_normed - small[3:4] / D - normed * (small[4:5] / D)
    )
    mods_out[...] = small * token_scale


def clips_kernel(pos, own, other, out):
    out[...] = own[...].astype(f32) + other[...].astype(f32)


def on_device(states, cotangent, shift_mod, scale_mod, gate_mod, first_weight, second_weight):
    row, col = lax.axis_index("row"), lax.axis_index("col")
    high, x, core = col // INNER, lax.rem(col, INNER) // 2, lax.rem(col, 2)
    pos = jnp.stack([row, high, x, core]).astype(jnp.int32)
    weight_one, weight_two = first_weight.T, second_weight.T
    own_x, own_c = states[0].T, cotangent[0].T

    own = (CHANNELS, TOK)
    piece = (CHANNELS + EXTRA, TOK)
    units = (UNITS, TOK)
    wide_units = (UNITS + EXTRA, TOK)
    stage = pltpu.VMEM((INNER, CHANNELS, TOK), bf16)

    pair = (2 * CHANNELS, TOK)
    wide_pair = (2 * CHANNELS + EXTRA, TOK)
    plain = jnp.concatenate([own_x, own_c], 0)
    (with_mods,) = whole(pack_kernel, [shaped(wide_pair)])(
        pos, plain, jnp.concatenate([shift_mod, 1.0 + scale_mod, gate_mod], 0)
    )
    x_planes, c_planes = whole(
        sort_kernel,
        [shaped((4 * CHANNELS + EXTRA, TOK)), shaped((4 * CHANNELS, TOK))],
    )(pos, *[spread_rows(plain, s) for s in (1, 2, 3)], spread_rows(with_mods, 0))
    x_lines = [x_planes] + [along_x(x_planes, q) for q in (1, 2, 3)]
    (first_turned,) = whole(turned_kernel, [shaped((SLICE, UNITS))])(pos, weight_one)
    x_blocks = both_cores(pos, after(x_lines, first_turned))
    c_lines = [c_planes] + [along_x(c_planes, q) for q in (1, 2, 3)]

    mods_column, mods_row, through = whole(
        mods_kernel,
        [
            shaped((INNER, CHANNELS, 8), f32),
            shaped((8, SLICE), f32),
            shaped((8, TOK), f32),
        ],
    )(pos, *x_blocks, weight_one)

    pre_sums, offsets, means = [None] * 4, [None] * 4, [None] * 4
    blocks = x_blocks
    for shift in (2, 1, 3, 0):
        pre_sums[shift], offsets[shift], means[shift] = whole(
            functools.partial(first_kernel, shift),
            [shaped(wide_units), shaped((SLICE, TOK)), shaped((1, TOK), f32)],
            [stage],
            some,
        )(pos, *blocks, mods_column, through, weight_one)
        blocks = after(blocks, pre_sums[shift])
    pre_sums = to_rows(pre_sums)
    hidden, slope, rest, factor, stats = whole(
        hidden_kernel,
        [
            shaped(wide_units),
            shaped(units, f32),
            shaped(units, f32),
            shaped((UNITS, 1), f32),
            shaped((2, TOK), f32),
        ],
    )(pos, *pre_sums)
    c_blocks = both_cores(pos, after(c_lines, pre_sums))
    *grad_sums, cot = whole(
        second_kernel,
        [shaped(units)] * 4 + [shaped((SLICE, TOKENS))],
        [pltpu.VMEM((4, SLICE, TOK), bf16)],
    )(pos, *after(c_blocks, hidden), mods_column, weight_two)
    grad_sums = to_rows(grad_sums)
    hidden = all_rows(hidden)

    weights = pl.BlockSpec((UNITS, CHUNK), lambda i, pos: (0, i))
    scratch = [pltpu.VMEM((UNITS, TOKENS), bf16)]

    weight_shapes = [shaped((UNITS, SLICE)), shaped((SLICE, 8), f32)]
    own_second, sums_second = whole(second_weight_kernel, weight_shapes, scratch)(
        pos, *hidden, cot, mods_row, weight_two
    )
    other_second = swap_clips(own_second)
    (grad_pre,) = whole(grad_kernel, [shaped(wide_units)])(
        pos, *grad_sums, slope, rest, factor
    )
    grad_pre = all_rows(grad_pre)
    own_first, sums_first = whole(
        first_weight_kernel, weight_shapes, scratch + [pltpu.VMEM((SLICE, TOKENS), bf16)]
    )(pos, *grad_pre, *hidden, *offsets, *means, mods_row, weight_one)
    other_first = swap_clips(own_first)

    quarter = (4,) + piece
    terms = whole(
        mod_kernel, [shaped(quarter)] * 8, scratch + [pltpu.VMEM((8, TOK), f32)]
    )(
        pos,
        *grad_pre,
        first_turned,
        sums_first.reshape(INNER, CHANNELS, 8),
        sums_second.reshape(INNER, CHANNELS, 8),
    )
    lines = whole(core_kernel, [shaped(quarter)] * 4)(
        pos, *terms[:4], *[across(term) for term in terms[4:]]
    )
    planes = whole(plane_kernel, [shaped(piece)] * 4)(
        pos, lines[0], *after([along_x(lines[p], p) for p in (1, 2, 3)], other_second)
    )
    pieces = [return_rows(planes[s], s) for s in range(4)]

    def clips_call(own, other):
        return call(
            clips_kernel,
            (SLICE // CHUNK,),
            [weights, weights],
            weights,
            shaped((UNITS, SLICE), f32),
        )(pos, own, other)

    grad_second = clips_call(own_second, other_second)
    grad_first = clips_call(own_first, other_first)
    grad_states, mods_grad = whole(
        states_kernel, [shaped(own, f32), shaped((8, TOK), f32)]
    )(pos, *after(pieces, grad_first), own_x, own_c, stats, scale_mod.T)
    return (
        grad_states.T[None],
        grad_first.T,
        grad_second.T,
        mods_grad[0:1, :CHANNELS],
        mods_grad[1:2, :CHANNELS],
        mods_grad[2:3, :CHANNELS],
    )


def solution(mesh):
    return jax.shard_map(
        on_device,
        mesh=mesh,
        in_specs=(
            P("dp", "row", "col"),
            P("dp", "row", "col"),
            P("dp", "col"),
            P("dp", "col"),
            P("dp", "col"),
            P("row", "col"),
            P("row", "col"),
        ),
        out_specs=(
            P("dp", "row", "col"),
            P("row", "col"),
            P("row", "col"),
            P("dp", "col"),
            P("dp", "col"),
            P("dp", "col"),
        ),
        check_vma=False,
    )
```

```python
import functools
import math

import jax
import jax.numpy as jnp
from jax import lax
from jax.experimental import pallas as pl
from jax.experimental.pallas import tpu as pltpu
from jax.sharding import PartitionSpec as P

D = 5120
FF = 13824
ROWS = 4
COLS = 32
INNER = 8
CHANNELS = D // COLS
UNITS = FF // COLS
TOK = 256
SLICE = D // ROWS
TOKENS = ROWS * TOK
EXTRA = 16
CHUNK = 256

bf16, f32 = jnp.bfloat16, jnp.float32

eps = 1e-06
tanh_factor = 0.7978845608028654
cubic_term = 0.044715
token_scale = 1.0 / math.sqrt(ROWS * TOK)
weight_scale = 1.0 / math.sqrt(2 * ROWS * TOK)
across_tokens = (((1,), (1,)), ((), ()))


def gelu_pair(values):
    squares = values * values
    inner = jnp.tanh(tanh_factor * (values + cubic_term * squares * values))
    half = 0.5 * (1.0 + inner)
    slope = half + 0.5 * values * (1.0 - inner * inner) * tanh_factor * (
        1.0 + 3.0 * cubic_term * squares
    )
    return values * half, slope


def turn(value, offset):
    return lax.rem(value + offset + 8, 4)


def spread_rows(values, shift):
    pairs = [
        (a * COLS + b * INNER + i, b * COLS + ((a + shift) % 4) * INNER + i)
        for a in range(4)
        for b in range(4)
        for i in range(INNER)
    ]
    return lax.ppermute(values, ("row", "col"), pairs)


def along_x(values, shift):
    pairs = [
        (h * 8 + x * 2 + k, h * 8 + ((x + shift) % 4) * 2 + k)
        for h in range(4)
        for x in range(4)
        for k in range(2)
    ]
    return lax.ppermute(values, "col", pairs)


def across(values):
    return lax.ppermute(values, "col", [(c, c ^ 1) for c in range(COLS)])


def along_row(values, shift):
    return lax.ppermute(values, "row", [(a, (a + shift) % 4) for a in range(4)])


def all_rows(values):
    return [values] + [along_row(values, q) for q in (1, 2, 3)]


def to_rows(values):
    return [values[0]] + [along_row(values[q], q) for q in (1, 2, 3)]


high_groups = [[h * 8 + i for h in range(4)] for i in range(INNER)]


def exchange(values, axis, groups=None):
    return lax.all_to_all(values, axis, 0, 0, axis_index_groups=groups, tiled=True)


def swap_clips(values):
    return lax.ppermute(values, "dp", [(0, 1), (1, 0)])


def both_cores(pos, lines):
    shape = shaped((2 * lines[0].shape[0], TOK))
    packs = whole(pair_kernel, [shape, shape])(pos, *lines)
    return list(lines) + [across(pack) for pack in packs]


def after(values, other):
    return lax.optimization_barrier((values, other))[0]


cheap = pl.CostEstimate(flops=1024, bytes_accessed=1024, transcendentals=0)
some = pl.CostEstimate(flops=1024, bytes_accessed=8000000, transcendentals=0)
limit = pltpu.CompilerParams(vmem_limit_bytes=16 * 1024 * 1024)


def call(kernel, grid, in_specs, out_specs, out_shape, scratch=()):
    return pl.pallas_call(
        kernel,
        grid_spec=pltpu.PrefetchScalarGridSpec(
            num_scalar_prefetch=1,
            grid=grid,
            in_specs=in_specs,
            out_specs=out_specs,
            scratch_shapes=list(scratch),
        ),
        out_shape=out_shape,
        compiler_params=limit,
        cost_estimate=cheap,
    )


def whole(kernel, out_shape, scratch=(), cost=cheap):
    vmem = pl.BlockSpec(memory_space=pltpu.VMEM)

    def run(pos, *args):
        return pl.pallas_call(
            kernel,
            in_specs=[pl.BlockSpec(memory_space=pltpu.SMEM)] + [vmem] * len(args),
            out_specs=[vmem] * len(out_shape),
            out_shape=out_shape,
            scratch_shapes=list(scratch),
            compiler_params=limit,
            cost_estimate=cost,
        )(pos, *args)

    return run


def full(shape):
    return pl.BlockSpec(shape, lambda i, pos: (0,) * len(shape))


def shaped(shape, kind=bf16):
    return jax.ShapeDtypeStruct(shape, kind)


def place_of(pos, token):
    return turn(pos[1] - token, -1)


def channel_block(pos, q, flip):
    core = pos[3] if flip == 0 else 1 - pos[3]
    return turn(pos[2], -q) * 2 + core


def parts_of(values, count):
    parts = []
    for _ in range(count):
        parts.append(values.astype(bf16).astype(f32))
        values = values - parts[-1]
    return parts


def packed(values):
    return jnp.concatenate(parts_of(values, 2), 0).astype(bf16)


def unpacked(rows):
    wide = rows.astype(f32)
    return wide[0:8] + wide[8:16]


def pack_kernel(pos, plain, mods, out):
    rows = parts_of(mods[...], 3) + [jnp.zeros((EXTRA - 9, CHANNELS), f32)]
    out[: 2 * CHANNELS] = plain[...]
    out[2 * CHANNELS :] = jnp.zeros((EXTRA, TOK), bf16)
    out[2 * CHANNELS :, :CHANNELS] = jnp.concatenate(rows, 0).astype(bf16)


def pair_kernel(pos, l0, l1, l2, l3, first, second):
    rows = l0.shape[0]
    first[:rows], first[rows:] = l0[...], l1[...]
    second[:rows], second[rows:] = l2[...], l3[...]


def block_of(blocks, q, flip, at, size):
    if flip == 0:
        return blocks[q][pl.ds(at, size), :]
    rows = blocks[0].shape[0]
    return blocks[4 + q // 2][pl.ds(at + (q % 2) * rows, size), :]


def sort_kernel(pos, b0, b1, b2, b3, x, cot):
    for at, ref in enumerate((b0, b1, b2, b3)):
        rows = slice(at * CHANNELS, (at + 1) * CHANNELS)
        x[rows] = ref[:CHANNELS]
        cot[rows] = ref[CHANNELS : 2 * CHANNELS]
    x[4 * CHANNELS :] = b3[2 * CHANNELS :]


def turned_kernel(pos, w1, out):
    out[...] = w1[...].T


def mods_kernel(pos, *refs):
    blocks, w1, mods_column, mods_row, through_out = refs[:6], refs[6], refs[7], refs[8], refs[9]
    for q in range(4):
        for flip in range(2):
            rows = block_of(blocks, q, flip, 4 * CHANNELS, EXTRA).astype(f32)
            values = jnp.concatenate([rows[0:3] + rows[3:6] + rows[6:9], rows[9:14]], 0)
            mods_column[channel_block(pos, q, flip)] = values.T[:CHANNELS]
    values = mods_column[...].reshape(SLICE, 8).T
    mods_row[...] = values
    rows = jnp.concatenate(parts_of(values, 3) + [jnp.zeros_like(values)], 0).astype(bf16)
    through = lax.dot_general(rows, w1[...], across_tokens, preferred_element_type=f32)
    through = through[0:8] + through[8:16] + through[16:24]
    through_out[...] = jnp.zeros((8, TOK), f32)
    for at, line in ((0, through[1:2]), (2, through[0:1])):
        through_out[at : at + 1] = line[:, :TOK]
        through_out[at + 1 : at + 2, : UNITS - TOK] = line[:, TOK:]


def first_kernel(shift, pos, *refs):
    blocks, mods, through, w1 = refs[:6], refs[6], refs[7], refs[8]
    out, offset_out, mean_out, offsets = refs[9:]
    place = place_of(pos, turn(pos[0], shift))
    at = pl.multiple_of(place * CHANNELS, 32)
    total = 0.0
    for q in range(4):
        for flip in range(2):
            block = block_of(blocks, q, flip, at, CHANNELS).astype(f32)
            total = total + jnp.sum(block, 0, keepdims=True)
    mean = total / SLICE
    square = 0.0
    for q in range(4):
        for flip in range(2):
            j = channel_block(pos, q, flip)
            offset = block_of(blocks, q, flip, at, CHANNELS).astype(f32) - mean
            square = square + jnp.sum(offset * offset, 0, keepdims=True)
            offsets[j] = (offset * mods[j][:, 1:2]).astype(bf16)
            rows = pl.ds(pl.multiple_of(j * CHANNELS, 32), CHANNELS)
            offset_out[rows, :] = offset.astype(bf16)
    mean_out[...] = mean
    out[:UNITS] = jnp.dot(
        w1[...], offsets[...].reshape(SLICE, TOK), preferred_element_type=f32
    ).astype(bf16)
    four = jnp.concatenate([mean, square, through[0:2]], 0)
    extra = parts_of(four, 3) + parts_of(through[2:4], 2)
    out[UNITS:] = jnp.concatenate(extra, 0).astype(bf16)


def hidden_kernel(pos, p0, p1, p2, p3, hidden_out, slope_out, rest_out, factor_out, stats_out):
    parts = (p0, p1, p2, p3)
    extras = [ref[UNITS:].astype(f32) for ref in parts]
    fours = [e[0:4] + e[4:8] + e[8:12] for e in extras]
    shifts = sum(e[12:14] + e[14:16] for e in extras)
    centre = 0.25 * (fours[0][0:1] + fours[1][0:1] + fours[2][0:1] + fours[3][0:1])
    spread = 0.0
    for four in fours:
        spread = spread + four[1:2] + SLICE * (four[0:1] - centre) ** 2
    inverse = lax.rsqrt(spread / D + eps)
    stats = jnp.concatenate([centre, inverse], 0)
    stats_out[...] = stats
    hidden_out[UNITS:] = jnp.concatenate(
        parts_of(stats, 3) + [jnp.zeros((EXTRA - 6, TOK), f32)], 0
    ).astype(bf16)
    columns = jnp.concatenate([four[2:4] for four in fours] + [shifts] * 4, 0).T
    for half, at in ((0, slice(0, TOK)), (1, slice(TOK, UNITS))):
        size = at.stop - at.start
        rest, total = 0.0, 0.0
        for i, ref in enumerate(parts):
            factor = columns[:size, 2 * i + half : 2 * i + half + 1]
            total = total + factor
            rest = rest + (ref[at].astype(f32) + factor * (fours[i][0:1] - centre))
        rest = rest * inverse
        hidden, slope = gelu_pair(rest + columns[:size, 8 + half : 9 + half])
        hidden_out[at] = hidden.astype(bf16)
        slope_out[at] = slope
        rest_out[at] = rest
        factor_out[at] = total


def second_kernel(pos, *refs):
    blocks, mods, w2 = refs[:6], refs[6], refs[7]
    sums, cot_out, scaled = refs[8:12], refs[12], refs[13]
    for shift, out in enumerate(sums):
        token = turn(pos[0], shift)
        at = pl.multiple_of(place_of(pos, token) * CHANNELS, 32)
        lanes = pl.ds(pl.multiple_of(token * TOK, TOK), TOK)
        for q in range(4):
            for flip in range(2):
                j = channel_block(pos, q, flip)
                block = block_of(blocks, q, flip, at, CHANNELS)
                rows = pl.ds(pl.multiple_of(j * CHANNELS, 32), CHANNELS)
                cot_out[rows, lanes] = block
                scaled[shift, rows, :] = (block.astype(f32) * mods[j][:, 2:3]).astype(bf16)
        out[...] = jnp.dot(w2[...], scaled[shift], preferred_element_type=f32).astype(bf16)


def grad_kernel(pos, own, one, two, three, slope, rest, factor, out):
    grad = own[...].astype(f32) + one[...].astype(f32)
    grad = grad + (two[...].astype(f32) + three[...].astype(f32))
    grad = (grad * slope[...]).astype(bf16)
    out[:UNITS] = grad
    wide = grad.astype(f32)
    first = jnp.sum(wide * factor[...], 0, keepdims=True)
    second = jnp.sum(wide * rest[...], 0, keepdims=True)
    line = lax.broadcasted_iota(jnp.int32, (8, TOK), 0)
    out[UNITS:] = packed(jnp.where(line == 3, first, jnp.where(line == 4, second, 0.0)))


def collect(pos, refs, store):
    for q, ref in enumerate(refs):
        at = pl.multiple_of(turn(pos[0], -q) * TOK, TOK)
        store[:, pl.ds(at, TOK)] = ref[:UNITS]


def second_weight_kernel(pos, b0, b1, b2, b3, cot, mods, w2, send, sums, store):
    collect(pos, (b0, b1, b2, b3), store)
    line = lax.broadcasted_iota(jnp.int32, (8, CHUNK), 0)
    for at in range(0, SLICE, CHUNK):
        part = slice(at, at + CHUNK)
        raw = lax.dot_general(
            store[...], cot[part, :], across_tokens, preferred_element_type=f32
        )
        total = jnp.sum(w2[:, part].astype(f32) * raw, 0, keepdims=True)
        sums[part, :] = jnp.where(line == 2, total, 0.0).T
        send[:, part] = (raw * (mods[2:3, part] * weight_scale)).astype(bf16)


def first_weight_kernel(pos, *refs):
    grads, hiddens, offsets, means = refs[:4], refs[4:8], refs[8:12], refs[12:16]
    mods, w1, send, sums, store, others = refs[16:]
    total, lift = 0.0, 0.0
    for q in range(4):
        at = (4 - q) % 4
        extra = hiddens[q][UNITS:].astype(f32)
        stats = extra[0:2] + extra[2:4] + extra[4:6]
        grad = grads[q][:UNITS].astype(f32)
        total = total + jnp.sum(grad, 1, keepdims=True)
        grad = grad * stats[1:2]
        lift = lift + jnp.sum(grad * (means[at][...] - stats[0:1]), 1, keepdims=True)
        lanes = slice(at * TOK, (at + 1) * TOK)
        store[:, lanes] = grad.astype(bf16)
        others[:, lanes] = offsets[at][...]
    line = lax.broadcasted_iota(jnp.int32, (8, CHUNK), 0)
    for at in range(0, SLICE, CHUNK):
        part = slice(at, at + CHUNK)
        raw = lift + lax.dot_general(
            store[...], others[part, :], across_tokens, preferred_element_type=f32
        )
        weight = w1[:, part].astype(f32)
        shift = jnp.sum(weight * total, 0, keepdims=True)
        scale = jnp.sum(weight * raw, 0, keepdims=True)
        sums[part, :] = jnp.where(line == 0, shift, jnp.where(line == 1, scale, 0.0)).T
        grad = (raw * mods[1:2, part] + total * mods[0:1, part]) * weight_scale
        send[:, part] = grad.astype(bf16)


def mod_kernel(pos, g0, g1, g2, g3, w1, sums_one, sums_two, *rest):
    keeps, sends, store, line = rest[:4], rest[4:8], rest[8], rest[9]
    grads = (g0, g1, g2, g3)
    collect(pos, grads, store)
    line[...] = jnp.zeros((8, TOK), f32)
    smalls = [unpacked(ref[UNITS:]) for ref in grads]
    for core, outs in ((pos[3], keeps), (1 - pos[3], sends)):
        for p, out in enumerate(outs):
            j = turn(pos[2], p) * 2 + core
            rows = pl.ds(pl.multiple_of(j * CHANNELS, 32), CHANNELS)
            product = jnp.dot(w1[rows, :], store[...], preferred_element_type=f32).astype(bf16)
            for token in range(4):
                out[token, :CHANNELS] = product[
                    :, token * TOK : (token + 1) * TOK
                ]
            line[:, :CHANNELS] = (sums_one[j] + sums_two[j]).T
            for q, small in enumerate(smalls):
                out[turn(pos[0], -q), CHANNELS:] = packed(small + line[...])


def add_up(out, parts):
    total = parts[0][:CHANNELS].astype(f32)
    small = unpacked(parts[0][CHANNELS:])
    for part in parts[1:]:
        total = total + part[:CHANNELS].astype(f32)
        small = small + unpacked(part[CHANNELS:])
    out[:CHANNELS] = total.astype(bf16)
    out[CHANNELS:] = packed(small)


def core_kernel(pos, *refs):
    for keep, other, out in zip(refs[:4], refs[4:8], refs[8:]):
        for s in range(4):
            add_up(out.at[s], [keep.at[s], other.at[s]])


def plane_kernel(pos, own, one, two, three, out):
    for token in range(4):
        add_up(out.at[token], [ref.at[token] for ref in (own, one, two, three)])


def states_kernel(pos, terms, x, cot, stats, scale, out, mods_out):
    centre, inverse = stats[0:1], stats[1:2]
    grad_mod, small = 0.0, 0.0
    for at in range(4):
        grad_mod = grad_mod + terms[at, :CHANNELS].astype(f32)
        small = small + unpacked(terms[at, CHANNELS:])
    normed = (x[...].astype(f32) - centre) * inverse
    grad_normed = grad_mod * (1.0 + scale[...])
    out[...] = cot[...].astype(f32) + inverse * (
        grad_normed - small[3:4] / D - normed * (small[4:5] / D)
    )
    mods_out[...] = small * token_scale


def clips_kernel(pos, own, other, out):
    out[...] = own[...].astype(f32) + other[...].astype(f32)


def on_device(states, cotangent, shift_mod, scale_mod, gate_mod, first_weight, second_weight):
    row, col = lax.axis_index("row"), lax.axis_index("col")
    high, x, core = col // INNER, lax.rem(col, INNER) // 2, lax.rem(col, 2)
    pos = jnp.stack([row, high, x, core]).astype(jnp.int32)
    weight_one, weight_two = first_weight.T, second_weight.T
    own_x, own_c = states[0].T, cotangent[0].T

    own = (CHANNELS, TOK)
    piece = (CHANNELS + EXTRA, TOK)
    units = (UNITS, TOK)
    wide_units = (UNITS + EXTRA, TOK)
    stage = pltpu.VMEM((INNER, CHANNELS, TOK), bf16)

    pair = (2 * CHANNELS, TOK)
    wide_pair = (2 * CHANNELS + EXTRA, TOK)
    plain = jnp.concatenate([own_x, own_c], 0)
    (with_mods,) = whole(pack_kernel, [shaped(wide_pair)])(
        pos, plain, jnp.concatenate([shift_mod, 1.0 + scale_mod, gate_mod], 0)
    )
    x_planes, c_planes = whole(
        sort_kernel,
        [shaped((4 * CHANNELS + EXTRA, TOK)), shaped((4 * CHANNELS, TOK))],
    )(pos, *[spread_rows(plain, s) for s in (1, 2, 3)], spread_rows(with_mods, 0))
    x_lines = [x_planes] + [along_x(x_planes, q) for q in (1, 2, 3)]
    (first_turned,) = whole(turned_kernel, [shaped((SLICE, UNITS))])(pos, weight_one)
    x_blocks = both_cores(pos, after(x_lines, first_turned))
    c_lines = [c_planes] + [along_x(c_planes, q) for q in (1, 2, 3)]

    mods_column, mods_row, through = whole(
        mods_kernel,
        [
            shaped((INNER, CHANNELS, 8), f32),
            shaped((8, SLICE), f32),
            shaped((8, TOK), f32),
        ],
    )(pos, *x_blocks, weight_one)

    pre_sums, offsets, means = [None] * 4, [None] * 4, [None] * 4
    blocks = x_blocks
    for shift in (2, 1, 3, 0):
        pre_sums[shift], offsets[shift], means[shift] = whole(
            functools.partial(first_kernel, shift),
            [shaped(wide_units), shaped((SLICE, TOK)), shaped((1, TOK), f32)],
            [stage],
            some,
        )(pos, *blocks, mods_column, through, weight_one)
        blocks = after(blocks, pre_sums[shift])
    pre_sums = to_rows(pre_sums)
    hidden, slope, rest, factor, stats = whole(
        hidden_kernel,
        [
            shaped(wide_units),
            shaped(units, f32),
            shaped(units, f32),
            shaped((UNITS, 1), f32),
            shaped((2, TOK), f32),
        ],
    )(pos, *pre_sums)
    c_blocks = both_cores(pos, after(c_lines, pre_sums))
    *grad_sums, cot = whole(
        second_kernel,
        [shaped(units)] * 4 + [shaped((SLICE, TOKENS))],
        [pltpu.VMEM((4, SLICE, TOK), bf16)],
    )(pos, *after(c_blocks, hidden), mods_column, weight_two)
    grad_sums = to_rows(grad_sums)
    hidden = all_rows(hidden)

    weights = pl.BlockSpec((UNITS, CHUNK), lambda i, pos: (0, i))
    scratch = [pltpu.VMEM((UNITS, TOKENS), bf16)]

    weight_shapes = [shaped((UNITS, SLICE)), shaped((SLICE, 8), f32)]
    own_second, sums_second = whole(second_weight_kernel, weight_shapes, scratch)(
        pos, *hidden, cot, mods_row, weight_two
    )
    other_second = swap_clips(own_second)
    (grad_pre,) = whole(grad_kernel, [shaped(wide_units)])(
        pos, *grad_sums, slope, rest, factor
    )
    grad_pre = all_rows(grad_pre)
    own_first, sums_first = whole(
        first_weight_kernel, weight_shapes, scratch + [pltpu.VMEM((SLICE, TOKENS), bf16)]
    )(pos, *grad_pre, *hidden, *offsets, *means, mods_row, weight_one)
    other_first = swap_clips(own_first)

    quarter = (4,) + piece
    terms = whole(
        mod_kernel, [shaped(quarter)] * 8, scratch + [pltpu.VMEM((8, TOK), f32)]
    )(
        pos,
        *grad_pre,
        first_turned,
        sums_first.reshape(INNER, CHANNELS, 8),
        sums_second.reshape(INNER, CHANNELS, 8),
    )
    lines = whole(core_kernel, [shaped(quarter)] * 4)(
        pos, *terms[:4], *[across(term) for term in terms[4:]]
    )
    def clips_call(own, other):
        return call(
            clips_kernel,
            (SLICE // CHUNK,),
            [weights, weights],
            weights,
            shaped((UNITS, SLICE), f32),
        )(pos, own, other)

    grad_second = clips_call(own_second, other_second)
    (planes,) = whole(plane_kernel, [shaped(quarter)])(
        pos, lines[0], *after([along_x(lines[p], p) for p in (1, 2, 3)], grad_second)
    )
    pieces = exchange(exchange(after(planes, other_first), "row"), "col", high_groups)
    grad_first = clips_call(own_first, after(other_first, pieces))
    grad_states, mods_grad = whole(
        states_kernel, [shaped(own, f32), shaped((8, TOK), f32)]
    )(pos, pieces, own_x, own_c, stats, scale_mod.T)
    return (
        grad_states.T[None],
        grad_first.T,
        grad_second.T,
        mods_grad[0:1, :CHANNELS],
        mods_grad[1:2, :CHANNELS],
        mods_grad[2:3, :CHANNELS],
    )


def solution(mesh):
    return jax.shard_map(
        on_device,
        mesh=mesh,
        in_specs=(
            P("dp", "row", "col"),
            P("dp", "row", "col"),
            P("dp", "col"),
            P("dp", "col"),
            P("dp", "col"),
            P("row", "col"),
            P("row", "col"),
        ),
        out_specs=(
            P("dp", "row", "col"),
            P("row", "col"),
            P("row", "col"),
            P("dp", "col"),
            P("dp", "col"),
            P("dp", "col"),
        ),
        check_vma=False,
    )
```

```python
import functools
import math

import jax
import jax.numpy as jnp
from jax import lax
from jax.experimental import pallas as pl
from jax.experimental.pallas import tpu as pltpu
from jax.sharding import PartitionSpec as P

D = 5120
FF = 13824
ROWS = 4
COLS = 32
INNER = 8
CHANNELS = D // COLS
UNITS = FF // COLS
TOK = 256
SLICE = D // ROWS
TOKENS = ROWS * TOK
EXTRA = 16
CHUNK = 256

bf16, f32 = jnp.bfloat16, jnp.float32

eps = 1e-06
tanh_factor = 0.7978845608028654
cubic_term = 0.044715
token_scale = 1.0 / math.sqrt(ROWS * TOK)
weight_scale = 1.0 / math.sqrt(2 * ROWS * TOK)
across_tokens = (((1,), (1,)), ((), ()))


def gelu_pair(values):
    squares = values * values
    inner = jnp.tanh(tanh_factor * (values + cubic_term * squares * values))
    half = 0.5 * (1.0 + inner)
    slope = half + 0.5 * values * (1.0 - inner * inner) * tanh_factor * (
        1.0 + 3.0 * cubic_term * squares
    )
    return values * half, slope


def turn(value, offset):
    return lax.rem(value + offset + 8, 4)


def spread_rows(values, shift):
    pairs = [
        (a * COLS + b * INNER + i, b * COLS + ((a + shift) % 4) * INNER + i)
        for a in range(4)
        for b in range(4)
        for i in range(INNER)
    ]
    return lax.ppermute(values, ("row", "col"), pairs)


def return_rows(values, shift):
    pairs = [
        (a * COLS + b * INNER + i, ((b + shift) % 4) * COLS + a * INNER + i)
        for a in range(4)
        for b in range(4)
        for i in range(INNER)
    ]
    return lax.ppermute(values, ("row", "col"), pairs)


def along_x(values, shift):
    pairs = [
        (h * 8 + x * 2 + k, h * 8 + ((x + shift) % 4) * 2 + k)
        for h in range(4)
        for x in range(4)
        for k in range(2)
    ]
    return lax.ppermute(values, "col", pairs)


def across(values):
    return lax.ppermute(values, "col", [(c, c ^ 1) for c in range(COLS)])


def along_row(values, shift):
    return lax.ppermute(values, "row", [(a, (a + shift) % 4) for a in range(4)])


def all_rows(values):
    return [values] + [along_row(values, q) for q in (1, 2, 3)]


def to_rows(values):
    return [values[0]] + [along_row(values[q], q) for q in (1, 2, 3)]


def swap_clips(values):
    return lax.ppermute(values, "dp", [(0, 1), (1, 0)])


def both_cores(pos, lines):
    shape = shaped((2 * lines[0].shape[0], TOK))
    packs = whole(pair_kernel, [shape, shape])(pos, *lines)
    return list(lines) + [across(pack) for pack in packs]


def after(values, other):
    return lax.optimization_barrier((values, other))[0]


cheap = pl.CostEstimate(flops=1024, bytes_accessed=1024, transcendentals=0)
limit = pltpu.CompilerParams(vmem_limit_bytes=16 * 1024 * 1024)


def call(kernel, grid, in_specs, out_specs, out_shape, scratch=()):
    return pl.pallas_call(
        kernel,
        grid_spec=pltpu.PrefetchScalarGridSpec(
            num_scalar_prefetch=1,
            grid=grid,
            in_specs=in_specs,
            out_specs=out_specs,
            scratch_shapes=list(scratch),
        ),
        out_shape=out_shape,
        compiler_params=limit,
        cost_estimate=cheap,
    )


def whole(kernel, out_shape, scratch=()):
    vmem = pl.BlockSpec(memory_space=pltpu.VMEM)

    def run(pos, *args):
        return pl.pallas_call(
            kernel,
            in_specs=[pl.BlockSpec(memory_space=pltpu.SMEM)] + [vmem] * len(args),
            out_specs=[vmem] * len(out_shape),
            out_shape=out_shape,
            scratch_shapes=list(scratch),
            compiler_params=limit,
            cost_estimate=cheap,
        )(pos, *args)

    return run


def full(shape):
    return pl.BlockSpec(shape, lambda i, pos: (0,) * len(shape))


def shaped(shape, kind=bf16):
    return jax.ShapeDtypeStruct(shape, kind)


def place_of(pos, token):
    return turn(pos[1] - token, -1)


def channel_block(pos, q, flip):
    core = pos[3] if flip == 0 else 1 - pos[3]
    return turn(pos[2], -q) * 2 + core


def parts_of(values, count):
    parts = []
    for _ in range(count):
        parts.append(values.astype(bf16).astype(f32))
        values = values - parts[-1]
    return parts


def packed(values):
    return jnp.concatenate(parts_of(values, 2), 0).astype(bf16)


def unpacked(rows):
    wide = rows.astype(f32)
    return wide[0:8] + wide[8:16]


def pack_kernel(pos, plain, mods, out):
    rows = parts_of(mods[...], 3) + [jnp.zeros((EXTRA - 9, CHANNELS), f32)]
    out[: 2 * CHANNELS] = plain[...]
    out[2 * CHANNELS :] = jnp.zeros((EXTRA, TOK), bf16)
    out[2 * CHANNELS :, :CHANNELS] = jnp.concatenate(rows, 0).astype(bf16)


def pair_kernel(pos, l0, l1, l2, l3, first, second):
    rows = l0.shape[0]
    first[:rows], first[rows:] = l0[...], l1[...]
    second[:rows], second[rows:] = l2[...], l3[...]


def block_of(blocks, q, flip, at, size):
    if flip == 0:
        return blocks[q][pl.ds(at, size), :]
    rows = blocks[0].shape[0]
    return blocks[4 + q // 2][pl.ds(at + (q % 2) * rows, size), :]


def sort_kernel(pos, b0, b1, b2, b3, x, cot):
    for at, ref in enumerate((b0, b1, b2, b3)):
        rows = slice(at * CHANNELS, (at + 1) * CHANNELS)
        x[rows] = ref[:CHANNELS]
        cot[rows] = ref[CHANNELS : 2 * CHANNELS]
    x[4 * CHANNELS :] = b3[2 * CHANNELS :]


def turned_kernel(pos, w1, out):
    out[...] = w1[...].T


def mods_kernel(pos, *refs):
    blocks, w1, mods_column, mods_row, through_out = refs[:6], refs[6], refs[7], refs[8], refs[9]
    for q in range(4):
        for flip in range(2):
            rows = block_of(blocks, q, flip, 4 * CHANNELS, EXTRA).astype(f32)
            values = jnp.concatenate([rows[0:3] + rows[3:6] + rows[6:9], rows[9:14]], 0)
            mods_column[channel_block(pos, q, flip)] = values.T[:CHANNELS]
    values = mods_column[...].reshape(SLICE, 8).T
    mods_row[...] = values
    rows = jnp.concatenate(parts_of(values, 3) + [jnp.zeros_like(values)], 0).astype(bf16)
    through = lax.dot_general(rows, w1[...], across_tokens, preferred_element_type=f32)
    through = through[0:8] + through[8:16] + through[16:24]
    through_out[...] = jnp.zeros((8, TOK), f32)
    for at, line in ((0, through[1:2]), (2, through[0:1])):
        through_out[at : at + 1] = line[:, :TOK]
        through_out[at + 1 : at + 2, : UNITS - TOK] = line[:, TOK:]


def first_kernel(shift, pos, *refs):
    blocks, mods, through, w1 = refs[:6], refs[6], refs[7], refs[8]
    out, offset_out, mean_out, offsets = refs[9:]
    place = place_of(pos, turn(pos[0], shift))
    at = pl.multiple_of(place * CHANNELS, 32)
    total = 0.0
    for q in range(4):
        for flip in range(2):
            block = block_of(blocks, q, flip, at, CHANNELS).astype(f32)
            total = total + jnp.sum(block, 0, keepdims=True)
    mean = total / SLICE
    square = 0.0
    for q in range(4):
        for flip in range(2):
            j = channel_block(pos, q, flip)
            offset = block_of(blocks, q, flip, at, CHANNELS).astype(f32) - mean
            square = square + jnp.sum(offset * offset, 0, keepdims=True)
            offsets[j] = (offset * mods[j][:, 1:2]).astype(bf16)
            rows = pl.ds(pl.multiple_of(j * CHANNELS, 32), CHANNELS)
            offset_out[rows, :] = offset.astype(bf16)
    mean_out[...] = mean
    out[:UNITS] = jnp.dot(
        w1[...], offsets[...].reshape(SLICE, TOK), preferred_element_type=f32
    ).astype(bf16)
    four = jnp.concatenate([mean, square, through[0:2]], 0)
    extra = parts_of(four, 3) + parts_of(through[2:4], 2)
    out[UNITS:] = jnp.concatenate(extra, 0).astype(bf16)


def hidden_kernel(pos, *refs):
    parts, grads, out, stats_out = refs[:4], refs[4:8], refs[8], refs[9]
    extras = [ref[UNITS:].astype(f32) for ref in parts]
    fours = [e[0:4] + e[4:8] + e[8:12] for e in extras]
    shifts = sum(e[12:14] + e[14:16] for e in extras)
    centre = 0.25 * (fours[0][0:1] + fours[1][0:1] + fours[2][0:1] + fours[3][0:1])
    spread = 0.0
    for four in fours:
        spread = spread + four[1:2] + SLICE * (four[0:1] - centre) ** 2
    inverse = lax.rsqrt(spread / D + eps)
    stats_out[...] = jnp.concatenate([centre, inverse], 0)
    columns = jnp.concatenate([four[2:4] for four in fours] + [shifts] * 4, 0).T
    first = second = 0.0
    for half, at in ((0, slice(0, TOK)), (1, slice(TOK, UNITS))):
        size = at.stop - at.start
        rest, total, grad = 0.0, 0.0, 0.0
        for i in range(4):
            factor = columns[:size, 2 * i + half : 2 * i + half + 1]
            total = total + factor
            rest = rest + (parts[i][at].astype(f32) + factor * (fours[i][0:1] - centre))
            grad = grad + grads[i][at].astype(f32)
        rest = rest * inverse
        hidden, slope = gelu_pair(rest + columns[:size, 8 + half : 9 + half])
        grad = (grad * slope).astype(bf16)
        out[at] = hidden.astype(bf16)
        out[UNITS + at.start : UNITS + at.stop] = grad
        wide = grad.astype(f32)
        first = first + jnp.sum(wide * total, 0, keepdims=True)
        second = second + jnp.sum(wide * rest, 0, keepdims=True)
    rest_of_centre = centre - sum(parts_of(centre, 2))
    line = lax.broadcasted_iota(jnp.int32, (8, TOK), 0)
    values = jnp.zeros((8, TOK), f32)
    for at, value in ((3, first), (4, second), (5, centre), (6, inverse), (7, rest_of_centre)):
        values = jnp.where(line == at, value, values)
    out[2 * UNITS :] = packed(values)


def second_kernel(pos, *refs):
    blocks, mods, w2 = refs[:6], refs[6], refs[7]
    sums, cot_out, scaled = refs[8:12], refs[12], refs[13]
    for shift, out in enumerate(sums):
        token = turn(pos[0], shift)
        at = pl.multiple_of(place_of(pos, token) * CHANNELS, 32)
        lanes = pl.ds(pl.multiple_of(token * TOK, TOK), TOK)
        for q in range(4):
            for flip in range(2):
                j = channel_block(pos, q, flip)
                block = block_of(blocks, q, flip, at, CHANNELS)
                rows = pl.ds(pl.multiple_of(j * CHANNELS, 32), CHANNELS)
                cot_out[rows, lanes] = block
                scaled[shift, rows, :] = (block.astype(f32) * mods[j][:, 2:3]).astype(bf16)
        out[...] = jnp.dot(w2[...], scaled[shift], preferred_element_type=f32).astype(bf16)


def collect(pos, refs, first, store):
    for q, ref in enumerate(refs):
        at = pl.multiple_of(turn(pos[0], -q) * TOK, TOK)
        store[:, pl.ds(at, TOK)] = ref[first : first + UNITS]


def second_weight_kernel(pos, b0, b1, b2, b3, cot, mods, w2, send, sums, store):
    collect(pos, (b0, b1, b2, b3), 0, store)
    line = lax.broadcasted_iota(jnp.int32, (8, CHUNK), 0)
    for at in range(0, SLICE, CHUNK):
        part = slice(at, at + CHUNK)
        raw = lax.dot_general(
            store[...], cot[part, :], across_tokens, preferred_element_type=f32
        )
        total = jnp.sum(w2[:, part].astype(f32) * raw, 0, keepdims=True)
        sums[part, :] = jnp.where(line == 2, total, 0.0).T
        send[:, part] = (raw * (mods[2:3, part] * weight_scale)).astype(bf16)


def first_weight_kernel(pos, *refs):
    units, offsets, means = refs[:4], refs[4:8], refs[8:12]
    mods, w1, send, sums, store, others = refs[12:]
    total, lift = 0.0, 0.0
    for q in range(4):
        at = (4 - q) % 4
        small = unpacked(units[q][2 * UNITS :])
        centre, inverse = small[5:6] + small[7:8], small[6:7]
        grad = units[q][UNITS : 2 * UNITS].astype(f32)
        total = total + jnp.sum(grad, 1, keepdims=True)
        grad = grad * inverse
        lift = lift + jnp.sum(grad * (means[at][...] - centre), 1, keepdims=True)
        lanes = slice(at * TOK, (at + 1) * TOK)
        store[:, lanes] = grad.astype(bf16)
        others[:, lanes] = offsets[at][...]
    line = lax.broadcasted_iota(jnp.int32, (8, CHUNK), 0)
    for at in range(0, SLICE, CHUNK):
        part = slice(at, at + CHUNK)
        raw = lift + lax.dot_general(
            store[...], others[part, :], across_tokens, preferred_element_type=f32
        )
        weight = w1[:, part].astype(f32)
        shift = jnp.sum(weight * total, 0, keepdims=True)
        scale = jnp.sum(weight * raw, 0, keepdims=True)
        sums[part, :] = jnp.where(line == 0, shift, jnp.where(line == 1, scale, 0.0)).T
        grad = (raw * mods[1:2, part] + total * mods[0:1, part]) * weight_scale
        send[:, part] = grad.astype(bf16)


def mod_kernel(pos, g0, g1, g2, g3, w1, sums_one, sums_two, *rest):
    keeps, sends, store, line = rest[:4], rest[4:8], rest[8], rest[9]
    grads = (g0, g1, g2, g3)
    collect(pos, grads, UNITS, store)
    line[...] = jnp.zeros((8, TOK), f32)
    row = lax.broadcasted_iota(jnp.int32, (8, TOK), 0)
    norm_rows = (row == 3) | (row == 4)
    smalls = [jnp.where(norm_rows, unpacked(ref[2 * UNITS :]), 0.0) for ref in grads]
    for core, outs in ((pos[3], keeps), (1 - pos[3], sends)):
        for p, out in enumerate(outs):
            j = turn(pos[2], p) * 2 + core
            rows = pl.ds(pl.multiple_of(j * CHANNELS, 32), CHANNELS)
            product = jnp.dot(w1[rows, :], store[...], preferred_element_type=f32).astype(bf16)
            for token in range(4):
                out[turn(token, -pos[1]), :CHANNELS] = product[
                    :, token * TOK : (token + 1) * TOK
                ]
            line[:, :CHANNELS] = (sums_one[j] + sums_two[j]).T
            for q, small in enumerate(smalls):
                out[turn(pos[0], -q - pos[1]), CHANNELS:] = packed(small + line[...])


def add_up(out, parts):
    total = parts[0][:CHANNELS].astype(f32)
    small = unpacked(parts[0][CHANNELS:])
    for part in parts[1:]:
        total = total + part[:CHANNELS].astype(f32)
        small = small + unpacked(part[CHANNELS:])
    out[:CHANNELS] = total.astype(bf16)
    out[CHANNELS:] = packed(small)


def core_kernel(pos, *refs):
    for keep, other, out in zip(refs[:4], refs[4:8], refs[8:]):
        for s in range(4):
            add_up(out.at[s], [keep.at[s], other.at[s]])


def plane_kernel(pos, own, one, two, three, o0, o1, o2, o3):
    for s, out in enumerate((o0, o1, o2, o3)):
        add_up(out, [ref.at[s] for ref in (own, one, two, three)])


def states_kernel(pos, a0, a1, a2, a3, x, cot, stats, scale, out, mods_out):
    centre, inverse = stats[0:1], stats[1:2]
    grad_mod, small = 0.0, 0.0
    for ref in (a0, a1, a2, a3):
        grad_mod = grad_mod + ref[:CHANNELS].astype(f32)
        small = small + unpacked(ref[CHANNELS:])
    normed = (x[...].astype(f32) - centre) * inverse
    grad_normed = grad_mod * (1.0 + scale[...])
    out[...] = cot[...].astype(f32) + inverse * (
        grad_normed - small[3:4] / D - normed * (small[4:5] / D)
    )
    mods_out[...] = small * token_scale


def clips_kernel(pos, own, other, out):
    out[...] = own[...].astype(f32) + other[...].astype(f32)


def on_device(states, cotangent, shift_mod, scale_mod, gate_mod, first_weight, second_weight):
    row, col = lax.axis_index("row"), lax.axis_index("col")
    high, x, core = col // INNER, lax.rem(col, INNER) // 2, lax.rem(col, 2)
    pos = jnp.stack([row, high, x, core]).astype(jnp.int32)
    weight_one, weight_two = first_weight.T, second_weight.T
    own_x, own_c = states[0].T, cotangent[0].T

    own = (CHANNELS, TOK)
    piece = (CHANNELS + EXTRA, TOK)
    units = (UNITS, TOK)
    wide_units = (UNITS + EXTRA, TOK)
    stage = pltpu.VMEM((INNER, CHANNELS, TOK), bf16)

    pair = (2 * CHANNELS, TOK)
    wide_pair = (2 * CHANNELS + EXTRA, TOK)
    plain = jnp.concatenate([own_x, own_c], 0)
    (with_mods,) = whole(pack_kernel, [shaped(wide_pair)])(
        pos, plain, jnp.concatenate([shift_mod, 1.0 + scale_mod, gate_mod], 0)
    )
    x_planes, c_planes = whole(
        sort_kernel,
        [shaped((4 * CHANNELS + EXTRA, TOK)), shaped((4 * CHANNELS, TOK))],
    )(pos, *[spread_rows(plain, s) for s in (1, 2, 3)], spread_rows(with_mods, 0))
    x_lines = [x_planes] + [along_x(x_planes, q) for q in (1, 2, 3)]
    (first_turned,) = whole(turned_kernel, [shaped((SLICE, UNITS))])(pos, weight_one)
    x_blocks = both_cores(pos, after(x_lines, first_turned))
    c_lines = [c_planes] + [along_x(c_planes, q) for q in (1, 2, 3)]

    mods_column, mods_row, through = whole(
        mods_kernel,
        [
            shaped((INNER, CHANNELS, 8), f32),
            shaped((8, SLICE), f32),
            shaped((8, TOK), f32),
        ],
    )(pos, *x_blocks, weight_one)

    pre_sums, offsets, means = [None] * 4, [None] * 4, [None] * 4

    def first_sums(shift, blocks):
        pre_sums[shift], offsets[shift], means[shift] = whole(
            functools.partial(first_kernel, shift),
            [shaped(wide_units), shaped((SLICE, TOK)), shaped((1, TOK), f32)],
            [stage],
        )(pos, *blocks, mods_column, through, weight_one)

    blocks = x_blocks
    for shift in (1, 3, 2):
        first_sums(shift, blocks)
        blocks = after(blocks, pre_sums[shift])
    arrived = [along_row(pre_sums[q], q) for q in (1, 2, 3)]
    c_blocks = both_cores(pos, after(c_lines, arrived))
    *grad_sums, cot = whole(
        second_kernel,
        [shaped(units)] * 4 + [shaped((SLICE, TOKENS))],
        [pltpu.VMEM((4, SLICE, TOK), bf16)],
    )(pos, *c_blocks, mods_column, weight_two)
    grad_sums = to_rows(grad_sums)
    first_sums(0, after(x_blocks, grad_sums[1]))
    both, stats = whole(
        hidden_kernel, [shaped((2 * UNITS + EXTRA, TOK)), shaped((2, TOK), f32)]
    )(pos, pre_sums[0], *arrived, *grad_sums)
    both = all_rows(both)

    weights = pl.BlockSpec((UNITS, CHUNK), lambda i, pos: (0, i))
    scratch = [pltpu.VMEM((UNITS, TOKENS), bf16)]

    weight_shapes = [shaped((UNITS, SLICE)), shaped((SLICE, 8), f32)]
    own_second, sums_second = whole(second_weight_kernel, weight_shapes, scratch)(
        pos, *both, cot, mods_row, weight_two
    )
    other_second = swap_clips(own_second)
    own_first, sums_first = whole(
        first_weight_kernel, weight_shapes, scratch + [pltpu.VMEM((SLICE, TOKENS), bf16)]
    )(pos, *both, *offsets, *means, mods_row, weight_one)
    other_first = swap_clips(own_first)

    quarter = (4,) + piece
    terms = whole(
        mod_kernel, [shaped(quarter)] * 8, scratch + [pltpu.VMEM((8, TOK), f32)]
    )(
        pos,
        *both,
        first_turned,
        sums_first.reshape(INNER, CHANNELS, 8),
        sums_second.reshape(INNER, CHANNELS, 8),
    )
    lines = whole(core_kernel, [shaped(quarter)] * 4)(
        pos, *terms[:4], *[across(term) for term in terms[4:]]
    )
    planes = whole(plane_kernel, [shaped(piece)] * 4)(
        pos, lines[0], *after([along_x(lines[p], p) for p in (1, 2, 3)], other_second)
    )
    pieces = [return_rows(planes[s], s) for s in range(4)]

    def clips_call(own, other):
        return call(
            clips_kernel,
            (SLICE // CHUNK,),
            [weights, weights],
            weights,
            shaped((UNITS, SLICE), f32),
        )(pos, own, other)

    grad_second = clips_call(own_second, other_second)
    grad_first = clips_call(own_first, other_first)
    grad_states, mods_grad = whole(
        states_kernel, [shaped(own, f32), shaped((8, TOK), f32)]
    )(pos, *after(pieces, grad_first), own_x, own_c, stats, scale_mod.T)
    return (
        grad_states.T[None],
        grad_first.T,
        grad_second.T,
        mods_grad[0:1, :CHANNELS],
        mods_grad[1:2, :CHANNELS],
        mods_grad[2:3, :CHANNELS],
    )


def solution(mesh):
    return jax.shard_map(
        on_device,
        mesh=mesh,
        in_specs=(
            P("dp", "row", "col"),
            P("dp", "row", "col"),
            P("dp", "col"),
            P("dp", "col"),
            P("dp", "col"),
            P("row", "col"),
            P("row", "col"),
        ),
        out_specs=(
            P("dp", "row", "col"),
            P("row", "col"),
            P("row", "col"),
            P("dp", "col"),
            P("dp", "col"),
            P("dp", "col"),
        ),
        check_vma=False,
    )
```

```python
import functools
import math

import jax
import jax.numpy as jnp
from jax import lax
from jax.experimental import pallas as pl
from jax.experimental.pallas import tpu as pltpu
from jax.sharding import PartitionSpec as P

D = 5120
FF = 13824
ROWS = 4
COLS = 32
INNER = 8
CHANNELS = D // COLS
UNITS = FF // COLS
TOK = 256
SLICE = D // ROWS
TOKENS = ROWS * TOK
EXTRA = 16
CHUNK = 256

bf16, f32 = jnp.bfloat16, jnp.float32

eps = 1e-06
tanh_factor = 0.7978845608028654
cubic_term = 0.044715
token_scale = 1.0 / math.sqrt(ROWS * TOK)
weight_scale = 1.0 / math.sqrt(2 * ROWS * TOK)
across_tokens = (((1,), (1,)), ((), ()))


def gelu_pair(values):
    squares = values * values
    inner = jnp.tanh(tanh_factor * (values + cubic_term * squares * values))
    half = 0.5 * (1.0 + inner)
    slope = half + 0.5 * values * (1.0 - inner * inner) * tanh_factor * (
        1.0 + 3.0 * cubic_term * squares
    )
    return values * half, slope


def turn(value, offset):
    return lax.rem(value + offset + 8, 4)


def spread_rows(values, shift):
    pairs = [
        (a * COLS + b * INNER + i, b * COLS + ((a + shift) % 4) * INNER + i)
        for a in range(4)
        for b in range(4)
        for i in range(INNER)
    ]
    return lax.ppermute(values, ("row", "col"), pairs)


def return_rows(values, shift):
    pairs = [
        (a * COLS + b * INNER + i, ((b + shift) % 4) * COLS + a * INNER + i)
        for a in range(4)
        for b in range(4)
        for i in range(INNER)
    ]
    return lax.ppermute(values, ("row", "col"), pairs)


def along_x(values, shift):
    pairs = [
        (h * 8 + x * 2 + k, h * 8 + ((x + shift) % 4) * 2 + k)
        for h in range(4)
        for x in range(4)
        for k in range(2)
    ]
    return lax.ppermute(values, "col", pairs)


def across(values):
    return lax.ppermute(values, "col", [(c, c ^ 1) for c in range(COLS)])


def along_row(values, shift):
    return lax.ppermute(values, "row", [(a, (a + shift) % 4) for a in range(4)])


def all_rows(values):
    return [values] + [along_row(values, q) for q in (1, 2, 3)]


def to_rows(values):
    return [values[0]] + [along_row(values[q], q) for q in (1, 2, 3)]


def swap_clips(values):
    return lax.ppermute(values, "dp", [(0, 1), (1, 0)])


def both_cores(pos, lines):
    shape = shaped((2 * lines[0].shape[0], TOK))
    packs = whole(pair_kernel, [shape, shape])(pos, *lines)
    return list(lines) + [across(pack) for pack in packs]


def after(values, other):
    return lax.optimization_barrier((values, other))[0]


cheap = pl.CostEstimate(flops=1024, bytes_accessed=1024, transcendentals=0)
some = pl.CostEstimate(flops=1024, bytes_accessed=8000000, transcendentals=0)
limit = pltpu.CompilerParams(vmem_limit_bytes=16 * 1024 * 1024)


def call(kernel, grid, in_specs, out_specs, out_shape, scratch=()):
    return pl.pallas_call(
        kernel,
        grid_spec=pltpu.PrefetchScalarGridSpec(
            num_scalar_prefetch=1,
            grid=grid,
            in_specs=in_specs,
            out_specs=out_specs,
            scratch_shapes=list(scratch),
        ),
        out_shape=out_shape,
        compiler_params=limit,
        cost_estimate=cheap,
    )


def whole(kernel, out_shape, scratch=(), cost=cheap):
    vmem = pl.BlockSpec(memory_space=pltpu.VMEM)

    def run(pos, *args):
        return pl.pallas_call(
            kernel,
            in_specs=[pl.BlockSpec(memory_space=pltpu.SMEM)] + [vmem] * len(args),
            out_specs=[vmem] * len(out_shape),
            out_shape=out_shape,
            scratch_shapes=list(scratch),
            compiler_params=limit,
            cost_estimate=cost,
        )(pos, *args)

    return run


def full(shape):
    return pl.BlockSpec(shape, lambda i, pos: (0,) * len(shape))


def shaped(shape, kind=bf16):
    return jax.ShapeDtypeStruct(shape, kind)


def place_of(pos, token):
    return turn(pos[1] - token, -1)


def channel_block(pos, q, flip):
    core = pos[3] if flip == 0 else 1 - pos[3]
    return turn(pos[2], -q) * 2 + core


def parts_of(values, count):
    parts = []
    for _ in range(count):
        parts.append(values.astype(bf16).astype(f32))
        values = values - parts[-1]
    return parts


def packed(values):
    return jnp.concatenate(parts_of(values, 2), 0).astype(bf16)


def unpacked(rows):
    wide = rows.astype(f32)
    return wide[0:8] + wide[8:16]


def pack_kernel(pos, plain, mods, out):
    rows = parts_of(mods[...], 3) + [jnp.zeros((EXTRA - 9, CHANNELS), f32)]
    out[: 2 * CHANNELS] = plain[...]
    out[2 * CHANNELS :] = jnp.zeros((EXTRA, TOK), bf16)
    out[2 * CHANNELS :, :CHANNELS] = jnp.concatenate(rows, 0).astype(bf16)


def pair_kernel(pos, l0, l1, l2, l3, first, second):
    rows = l0.shape[0]
    first[:rows], first[rows:] = l0[...], l1[...]
    second[:rows], second[rows:] = l2[...], l3[...]


def block_of(blocks, q, flip, at, size):
    if flip == 0:
        return blocks[q][pl.ds(at, size), :]
    rows = blocks[0].shape[0]
    return blocks[4 + q // 2][pl.ds(at + (q % 2) * rows, size), :]


def sort_kernel(pos, b0, b1, b2, b3, x, cot):
    for at, ref in enumerate((b0, b1, b2, b3)):
        rows = slice(at * CHANNELS, (at + 1) * CHANNELS)
        x[rows] = ref[:CHANNELS]
        cot[rows] = ref[CHANNELS : 2 * CHANNELS]
    x[4 * CHANNELS :] = b3[2 * CHANNELS :]


def turned_kernel(pos, w1, out):
    out[...] = w1[...].T


def mods_kernel(pos, *refs):
    blocks, w1, mods_column, mods_row, through_out = refs[:6], refs[6], refs[7], refs[8], refs[9]
    for q in range(4):
        for flip in range(2):
            rows = block_of(blocks, q, flip, 4 * CHANNELS, EXTRA).astype(f32)
            values = jnp.concatenate([rows[0:3] + rows[3:6] + rows[6:9], rows[9:14]], 0)
            mods_column[channel_block(pos, q, flip)] = values.T[:CHANNELS]
    values = mods_column[...].reshape(SLICE, 8).T
    mods_row[...] = values
    rows = jnp.concatenate(parts_of(values, 3) + [jnp.zeros_like(values)], 0).astype(bf16)
    through = lax.dot_general(rows, w1[...], across_tokens, preferred_element_type=f32)
    through = through[0:8] + through[8:16] + through[16:24]
    through_out[...] = jnp.zeros((8, TOK), f32)
    for at, line in ((0, through[1:2]), (2, through[0:1])):
        through_out[at : at + 1] = line[:, :TOK]
        through_out[at + 1 : at + 2, : UNITS - TOK] = line[:, TOK:]


def first_kernel(shift, pos, *refs):
    blocks, mods, through, w1 = refs[:6], refs[6], refs[7], refs[8]
    out, offset_out, mean_out, offsets = refs[9:]
    place = place_of(pos, turn(pos[0], shift))
    at = pl.multiple_of(place * CHANNELS, 32)
    total = 0.0
    for q in range(4):
        for flip in range(2):
            block = block_of(blocks, q, flip, at, CHANNELS).astype(f32)
            total = total + jnp.sum(block, 0, keepdims=True)
    mean = total / SLICE
    square = 0.0
    for q in range(4):
        for flip in range(2):
            j = channel_block(pos, q, flip)
            offset = block_of(blocks, q, flip, at, CHANNELS).astype(f32) - mean
            square = square + jnp.sum(offset * offset, 0, keepdims=True)
            offsets[j] = (offset * mods[j][:, 1:2]).astype(bf16)
            rows = pl.ds(pl.multiple_of(j * CHANNELS, 32), CHANNELS)
            offset_out[rows, :] = offset.astype(bf16)
    mean_out[...] = mean
    out[:UNITS] = jnp.dot(
        w1[...], offsets[...].reshape(SLICE, TOK), preferred_element_type=f32
    ).astype(bf16)
    four = jnp.concatenate([mean, square, through[0:2]], 0)
    extra = parts_of(four, 3) + parts_of(through[2:4], 2)
    out[UNITS:] = jnp.concatenate(extra, 0).astype(bf16)


def hidden_kernel(pos, p0, p1, p2, p3, hidden_out, slope_out, rest_out, factor_out, stats_out):
    parts = (p0, p1, p2, p3)
    extras = [ref[UNITS:].astype(f32) for ref in parts]
    fours = [e[0:4] + e[4:8] + e[8:12] for e in extras]
    shifts = sum(e[12:14] + e[14:16] for e in extras)
    centre = 0.25 * (fours[0][0:1] + fours[1][0:1] + fours[2][0:1] + fours[3][0:1])
    spread = 0.0
    for four in fours:
        spread = spread + four[1:2] + SLICE * (four[0:1] - centre) ** 2
    inverse = lax.rsqrt(spread / D + eps)
    stats = jnp.concatenate([centre, inverse], 0)
    stats_out[...] = stats
    hidden_out[UNITS:] = jnp.concatenate(
        parts_of(stats, 3) + [jnp.zeros((EXTRA - 6, TOK), f32)], 0
    ).astype(bf16)
    columns = jnp.concatenate([four[2:4] for four in fours] + [shifts] * 4, 0).T
    for half, at in ((0, slice(0, TOK)), (1, slice(TOK, UNITS))):
        size = at.stop - at.start
        rest, total = 0.0, 0.0
        for i, ref in enumerate(parts):
            factor = columns[:size, 2 * i + half : 2 * i + half + 1]
            total = total + factor
            rest = rest + (ref[at].astype(f32) + factor * (fours[i][0:1] - centre))
        rest = rest * inverse
        hidden, slope = gelu_pair(rest + columns[:size, 8 + half : 9 + half])
        hidden_out[at] = hidden.astype(bf16)
        slope_out[at] = slope
        rest_out[at] = rest
        factor_out[at] = total


def second_kernel(pos, *refs):
    blocks, mods, w2 = refs[:6], refs[6], refs[7]
    sums, cot_out, scaled = refs[8:12], refs[12], refs[13]
    for shift, out in enumerate(sums):
        token = turn(pos[0], shift)
        at = pl.multiple_of(place_of(pos, token) * CHANNELS, 32)
        lanes = pl.ds(pl.multiple_of(token * TOK, TOK), TOK)
        for q in range(4):
            for flip in range(2):
                j = channel_block(pos, q, flip)
                block = block_of(blocks, q, flip, at, CHANNELS)
                rows = pl.ds(pl.multiple_of(j * CHANNELS, 32), CHANNELS)
                cot_out[rows, lanes] = block
                scaled[shift, rows, :] = (block.astype(f32) * mods[j][:, 2:3]).astype(bf16)
        out[...] = jnp.dot(w2[...], scaled[shift], preferred_element_type=f32).astype(bf16)


def grad_kernel(pos, own, one, two, three, slope, rest, factor, out):
    grad = own[...].astype(f32) + one[...].astype(f32)
    grad = grad + (two[...].astype(f32) + three[...].astype(f32))
    grad = (grad * slope[...]).astype(bf16)
    out[:UNITS] = grad
    wide = grad.astype(f32)
    first = jnp.sum(wide * factor[...], 0, keepdims=True)
    second = jnp.sum(wide * rest[...], 0, keepdims=True)
    line = lax.broadcasted_iota(jnp.int32, (8, TOK), 0)
    out[UNITS:] = packed(jnp.where(line == 3, first, jnp.where(line == 4, second, 0.0)))


def collect(pos, refs, store):
    for q, ref in enumerate(refs):
        at = pl.multiple_of(turn(pos[0], -q) * TOK, TOK)
        store[:, pl.ds(at, TOK)] = ref[:UNITS]


def second_weight_kernel(pos, b0, b1, b2, b3, cot, mods, w2, send, sums, store):
    collect(pos, (b0, b1, b2, b3), store)
    line = lax.broadcasted_iota(jnp.int32, (8, CHUNK), 0)
    for at in range(0, SLICE, CHUNK):
        part = slice(at, at + CHUNK)
        raw = lax.dot_general(
            store[...], cot[part, :], across_tokens, preferred_element_type=f32
        )
        total = jnp.sum(w2[:, part].astype(f32) * raw, 0, keepdims=True)
        sums[part, :] = jnp.where(line == 2, total, 0.0).T
        send[:, part] = (raw * (mods[2:3, part] * weight_scale)).astype(bf16)


def first_weight_kernel(pos, *refs):
    grads, hiddens, offsets, means = refs[:4], refs[4:8], refs[8:12], refs[12:16]
    mods, w1, send, sums, store, others = refs[16:]
    total, lift = 0.0, 0.0
    for q in range(4):
        at = (4 - q) % 4
        extra = hiddens[q][UNITS:].astype(f32)
        stats = extra[0:2] + extra[2:4] + extra[4:6]
        grad = grads[q][:UNITS].astype(f32)
        total = total + jnp.sum(grad, 1, keepdims=True)
        grad = grad * stats[1:2]
        lift = lift + jnp.sum(grad * (means[at][...] - stats[0:1]), 1, keepdims=True)
        lanes = slice(at * TOK, (at + 1) * TOK)
        store[:, lanes] = grad.astype(bf16)
        others[:, lanes] = offsets[at][...]
    line = lax.broadcasted_iota(jnp.int32, (8, CHUNK), 0)
    for at in range(0, SLICE, CHUNK):
        part = slice(at, at + CHUNK)
        raw = lift + lax.dot_general(
            store[...], others[part, :], across_tokens, preferred_element_type=f32
        )
        weight = w1[:, part].astype(f32)
        shift = jnp.sum(weight * total, 0, keepdims=True)
        scale = jnp.sum(weight * raw, 0, keepdims=True)
        sums[part, :] = jnp.where(line == 0, shift, jnp.where(line == 1, scale, 0.0)).T
        grad = (raw * mods[1:2, part] + total * mods[0:1, part]) * weight_scale
        send[:, part] = grad.astype(bf16)


def mod_kernel(pos, g0, g1, g2, g3, w1, sums_one, sums_two, *rest):
    keeps, sends, store, line = rest[:4], rest[4:8], rest[8], rest[9]
    grads = (g0, g1, g2, g3)
    collect(pos, grads, store)
    line[...] = jnp.zeros((8, TOK), f32)
    smalls = [unpacked(ref[UNITS:]) for ref in grads]
    for core, outs in ((pos[3], keeps), (1 - pos[3], sends)):
        for p, out in enumerate(outs):
            j = turn(pos[2], p) * 2 + core
            rows = pl.ds(pl.multiple_of(j * CHANNELS, 32), CHANNELS)
            product = jnp.dot(w1[rows, :], store[...], preferred_element_type=f32).astype(bf16)
            for token in range(4):
                out[turn(token, -pos[1]), :CHANNELS] = product[
                    :, token * TOK : (token + 1) * TOK
                ]
            line[:, :CHANNELS] = (sums_one[j] + sums_two[j]).T
            for q, small in enumerate(smalls):
                out[turn(pos[0], -q - pos[1]), CHANNELS:] = packed(small + line[...])


def add_up(out, parts):
    total = parts[0][:CHANNELS].astype(f32)
    small = unpacked(parts[0][CHANNELS:])
    for part in parts[1:]:
        total = total + part[:CHANNELS].astype(f32)
        small = small + unpacked(part[CHANNELS:])
    out[:CHANNELS] = total.astype(bf16)
    out[CHANNELS:] = packed(small)


def core_kernel(pos, *refs):
    for keep, other, out in zip(refs[:4], refs[4:8], refs[8:]):
        for s in range(4):
            add_up(out.at[s], [keep.at[s], other.at[s]])


def plane_kernel(pos, own, one, two, three, o0, o1, o2, o3):
    for s, out in enumerate((o0, o1, o2, o3)):
        add_up(out, [ref.at[s] for ref in (own, one, two, three)])


def states_kernel(pos, a0, a1, a2, a3, x, cot, stats, scale, out, mods_out):
    centre, inverse = stats[0:1], stats[1:2]
    grad_mod, small = 0.0, 0.0
    for ref in (a0, a1, a2, a3):
        grad_mod = grad_mod + ref[:CHANNELS].astype(f32)
        small = small + unpacked(ref[CHANNELS:])
    normed = (x[...].astype(f32) - centre) * inverse
    grad_normed = grad_mod * (1.0 + scale[...])
    out[...] = cot[...].astype(f32) + inverse * (
        grad_normed - small[3:4] / D - normed * (small[4:5] / D)
    )
    mods_out[...] = small * token_scale


def clips_kernel(pos, own, other, out):
    out[...] = own[...].astype(f32) + other[...].astype(f32)


def on_device(states, cotangent, shift_mod, scale_mod, gate_mod, first_weight, second_weight):
    row, col = lax.axis_index("row"), lax.axis_index("col")
    high, x, core = col // INNER, lax.rem(col, INNER) // 2, lax.rem(col, 2)
    pos = jnp.stack([row, high, x, core]).astype(jnp.int32)
    weight_one, weight_two = first_weight.T, second_weight.T
    own_x, own_c = states[0].T, cotangent[0].T

    own = (CHANNELS, TOK)
    piece = (CHANNELS + EXTRA, TOK)
    units = (UNITS, TOK)
    wide_units = (UNITS + EXTRA, TOK)
    stage = pltpu.VMEM((INNER, CHANNELS, TOK), bf16)

    pair = (2 * CHANNELS, TOK)
    wide_pair = (2 * CHANNELS + EXTRA, TOK)
    plain = jnp.concatenate([own_x, own_c], 0)
    (with_mods,) = whole(pack_kernel, [shaped(wide_pair)])(
        pos, plain, jnp.concatenate([shift_mod, 1.0 + scale_mod, gate_mod], 0)
    )
    x_planes, c_planes = whole(
        sort_kernel,
        [shaped((4 * CHANNELS + EXTRA, TOK)), shaped((4 * CHANNELS, TOK))],
    )(pos, *[spread_rows(plain, s) for s in (1, 2, 3)], spread_rows(with_mods, 0))
    x_lines = [x_planes] + [along_x(x_planes, q) for q in (1, 2, 3)]
    (first_turned,) = whole(turned_kernel, [shaped((SLICE, UNITS))])(pos, weight_one)
    x_blocks = both_cores(pos, after(x_lines, first_turned))
    c_lines = [c_planes] + [along_x(c_planes, q) for q in (1, 2, 3)]

    mods_column, mods_row, through = whole(
        mods_kernel,
        [
            shaped((INNER, CHANNELS, 8), f32),
            shaped((8, SLICE), f32),
            shaped((8, TOK), f32),
        ],
    )(pos, *x_blocks, weight_one)

    pre_sums, offsets, means = [None] * 4, [None] * 4, [None] * 4
    blocks = x_blocks
    for shift in (1, 3, 2, 0):
        pre_sums[shift], offsets[shift], means[shift] = whole(
            functools.partial(first_kernel, shift),
            [shaped(wide_units), shaped((SLICE, TOK)), shaped((1, TOK), f32)],
            [stage],
            some,
        )(pos, *blocks, mods_column, through, weight_one)
        blocks = after(blocks, pre_sums[shift])
    pre_sums = to_rows(pre_sums)
    hidden, slope, rest, factor, stats = whole(
        hidden_kernel,
        [
            shaped(wide_units),
            shaped(units, f32),
            shaped(units, f32),
            shaped((UNITS, 1), f32),
            shaped((2, TOK), f32),
        ],
    )(pos, *pre_sums)
    c_blocks = both_cores(pos, after(c_lines, pre_sums))
    *grad_sums, cot = whole(
        second_kernel,
        [shaped(units)] * 4 + [shaped((SLICE, TOKENS))],
        [pltpu.VMEM((4, SLICE, TOK), bf16)],
    )(pos, *c_blocks, mods_column, weight_two)
    hidden = all_rows(hidden)

    weights = pl.BlockSpec((UNITS, CHUNK), lambda i, pos: (0, i))
    scratch = [pltpu.VMEM((UNITS, TOKENS), bf16)]

    weight_shapes = [shaped((UNITS, SLICE)), shaped((SLICE, 8), f32)]
    own_second, sums_second = whole(second_weight_kernel, weight_shapes, scratch)(
        pos, *hidden, cot, mods_row, weight_two
    )
    other_second = swap_clips(own_second)
    grad_sums = to_rows(after(grad_sums, own_second))
    (grad_pre,) = whole(grad_kernel, [shaped(wide_units)])(
        pos, *grad_sums, slope, rest, factor
    )
    grad_pre = all_rows(grad_pre)
    own_first, sums_first = whole(
        first_weight_kernel, weight_shapes, scratch + [pltpu.VMEM((SLICE, TOKENS), bf16)]
    )(pos, *grad_pre, *hidden, *offsets, *means, mods_row, weight_one)
    other_first = swap_clips(own_first)

    quarter = (4,) + piece
    terms = whole(
        mod_kernel, [shaped(quarter)] * 8, scratch + [pltpu.VMEM((8, TOK), f32)]
    )(
        pos,
        *grad_pre,
        first_turned,
        sums_first.reshape(INNER, CHANNELS, 8),
        sums_second.reshape(INNER, CHANNELS, 8),
    )
    lines = whole(core_kernel, [shaped(quarter)] * 4)(
        pos, *terms[:4], *after([across(term) for term in terms[4:]], other_second)
    )
    def clips_call(own, other):
        return call(
            clips_kernel,
            (SLICE // CHUNK,),
            [weights, weights],
            weights,
            shaped((UNITS, SLICE), f32),
        )(pos, own, other)

    grad_second = clips_call(own_second, other_second)
    planes = whole(plane_kernel, [shaped(piece)] * 4)(
        pos, lines[0], *after([along_x(lines[p], p) for p in (1, 2, 3)], grad_second)
    )
    pieces = [return_rows(planes[s], s) for s in range(4)]

    grad_first = clips_call(own_first, other_first)
    grad_states, mods_grad = whole(
        states_kernel, [shaped(own, f32), shaped((8, TOK), f32)]
    )(pos, *after(pieces, grad_first), own_x, own_c, stats, scale_mod.T)
    return (
        grad_states.T[None],
        grad_first.T,
        grad_second.T,
        mods_grad[0:1, :CHANNELS],
        mods_grad[1:2, :CHANNELS],
        mods_grad[2:3, :CHANNELS],
    )


def solution(mesh):
    return jax.shard_map(
        on_device,
        mesh=mesh,
        in_specs=(
            P("dp", "row", "col"),
            P("dp", "row", "col"),
            P("dp", "col"),
            P("dp", "col"),
            P("dp", "col"),
            P("row", "col"),
            P("row", "col"),
        ),
        out_specs=(
            P("dp", "row", "col"),
            P("row", "col"),
            P("row", "col"),
            P("dp", "col"),
            P("dp", "col"),
            P("dp", "col"),
        ),
        check_vma=False,
    )
```

```python
import functools
import math

import jax
import jax.numpy as jnp
from jax import lax
from jax.experimental import pallas as pl
from jax.experimental.pallas import tpu as pltpu
from jax.sharding import PartitionSpec as P

D = 5120
FF = 13824
ROWS = 4
COLS = 32
INNER = 8
CHANNELS = D // COLS
UNITS = FF // COLS
TOK = 256
SLICE = D // ROWS
TOKENS = ROWS * TOK
EXTRA = 16
CHUNK = 256

bf16, f32 = jnp.bfloat16, jnp.float32

eps = 1e-06
tanh_factor = 0.7978845608028654
cubic_term = 0.044715
token_scale = 1.0 / math.sqrt(ROWS * TOK)
weight_scale = 1.0 / math.sqrt(2 * ROWS * TOK)
across_tokens = (((1,), (1,)), ((), ()))


def gelu_pair(values):
    squares = values * values
    inner = jnp.tanh(tanh_factor * (values + cubic_term * squares * values))
    half = 0.5 * (1.0 + inner)
    slope = half + 0.5 * values * (1.0 - inner * inner) * tanh_factor * (
        1.0 + 3.0 * cubic_term * squares
    )
    return values * half, slope


def turn(value, offset):
    return lax.rem(value + offset + 8, 4)


def spread_rows(values, shift):
    pairs = [
        (a * COLS + b * INNER + i, b * COLS + ((a + shift) % 4) * INNER + i)
        for a in range(4)
        for b in range(4)
        for i in range(INNER)
    ]
    return lax.ppermute(values, ("row", "col"), pairs)


def return_rows(values, shift):
    pairs = [
        (a * COLS + b * INNER + i, ((b + shift) % 4) * COLS + a * INNER + i)
        for a in range(4)
        for b in range(4)
        for i in range(INNER)
    ]
    return lax.ppermute(values, ("row", "col"), pairs)


def along_x(values, shift):
    pairs = [
        (h * 8 + x * 2 + k, h * 8 + ((x + shift) % 4) * 2 + k)
        for h in range(4)
        for x in range(4)
        for k in range(2)
    ]
    return lax.ppermute(values, "col", pairs)


def across(values):
    return lax.ppermute(values, "col", [(c, c ^ 1) for c in range(COLS)])


def along_row(values, shift):
    return lax.ppermute(values, "row", [(a, (a + shift) % 4) for a in range(4)])


def all_rows(values):
    return [values] + [along_row(values, q) for q in (1, 2, 3)]


def to_rows(values):
    return [values[0]] + [along_row(values[q], q) for q in (1, 2, 3)]


def swap_clips(values):
    return lax.ppermute(values, "dp", [(0, 1), (1, 0)])


def both_cores(pos, lines):
    shape = shaped((2 * lines[0].shape[0], TOK))
    packs = whole(pair_kernel, [shape, shape])(pos, *lines)
    return list(lines) + [across(pack) for pack in packs]


def after(values, other):
    return lax.optimization_barrier((values, other))[0]


cheap = pl.CostEstimate(flops=1024, bytes_accessed=1024, transcendentals=0)
some = pl.CostEstimate(flops=1024, bytes_accessed=8000000, transcendentals=0)
limit = pltpu.CompilerParams(vmem_limit_bytes=16 * 1024 * 1024)


def call(kernel, grid, in_specs, out_specs, out_shape, scratch=()):
    return pl.pallas_call(
        kernel,
        grid_spec=pltpu.PrefetchScalarGridSpec(
            num_scalar_prefetch=1,
            grid=grid,
            in_specs=in_specs,
            out_specs=out_specs,
            scratch_shapes=list(scratch),
        ),
        out_shape=out_shape,
        compiler_params=limit,
        cost_estimate=cheap,
    )


def whole(kernel, out_shape, scratch=(), cost=cheap):
    vmem = pl.BlockSpec(memory_space=pltpu.VMEM)

    def run(pos, *args):
        return pl.pallas_call(
            kernel,
            in_specs=[pl.BlockSpec(memory_space=pltpu.SMEM)] + [vmem] * len(args),
            out_specs=[vmem] * len(out_shape),
            out_shape=out_shape,
            scratch_shapes=list(scratch),
            compiler_params=limit,
            cost_estimate=cost,
        )(pos, *args)

    return run


def full(shape):
    return pl.BlockSpec(shape, lambda i, pos: (0,) * len(shape))


def shaped(shape, kind=bf16):
    return jax.ShapeDtypeStruct(shape, kind)


def place_of(pos, token):
    return turn(pos[1] - token, -1)


def channel_block(pos, q, flip):
    core = pos[3] if flip == 0 else 1 - pos[3]
    return turn(pos[2], -q) * 2 + core


def parts_of(values, count):
    parts = []
    for _ in range(count):
        parts.append(values.astype(bf16).astype(f32))
        values = values - parts[-1]
    return parts


def packed(values):
    return jnp.concatenate(parts_of(values, 2), 0).astype(bf16)


def unpacked(rows):
    wide = rows.astype(f32)
    return wide[0:8] + wide[8:16]


def pack_kernel(pos, plain, mods, out):
    line = lax.broadcasted_iota(jnp.int32, (3, CHANNELS), 0)
    values = mods[...] + jnp.where(line == 1, 1.0, 0.0)
    rows = parts_of(values, 3) + [jnp.zeros((EXTRA - 9, CHANNELS), f32)]
    out[: 2 * CHANNELS] = plain[...]
    out[2 * CHANNELS :] = jnp.zeros((EXTRA, TOK), bf16)
    out[2 * CHANNELS :, :CHANNELS] = jnp.concatenate(rows, 0).astype(bf16)


def pair_kernel(pos, l0, l1, l2, l3, first, second):
    rows = l0.shape[0]
    first[:rows], first[rows:] = l0[...], l1[...]
    second[:rows], second[rows:] = l2[...], l3[...]


def block_of(blocks, q, flip, at, size):
    if flip == 0:
        return blocks[q][pl.ds(at, size), :]
    rows = blocks[0].shape[0]
    return blocks[4 + q // 2][pl.ds(at + (q % 2) * rows, size), :]


def sort_kernel(pos, b0, b1, b2, b3, x, cot):
    for at, ref in enumerate((b0, b1, b2, b3)):
        rows = slice(at * CHANNELS, (at + 1) * CHANNELS)
        x[rows] = ref[:CHANNELS]
        cot[rows] = ref[CHANNELS : 2 * CHANNELS]
    x[4 * CHANNELS :] = b3[2 * CHANNELS :]


def turned_kernel(pos, w1, out):
    out[...] = w1[...].T


def mods_kernel(pos, *refs):
    blocks, w1, mods_column, mods_row, through_out = refs[:6], refs[6], refs[7], refs[8], refs[9]
    for q in range(4):
        for flip in range(2):
            rows = block_of(blocks, q, flip, 4 * CHANNELS, EXTRA).astype(f32)
            values = jnp.concatenate([rows[0:3] + rows[3:6] + rows[6:9], rows[9:14]], 0)
            mods_column[channel_block(pos, q, flip)] = values.T[:CHANNELS]
    values = mods_column[...].reshape(SLICE, 8).T
    mods_row[...] = values
    rows = jnp.concatenate(parts_of(values, 3) + [jnp.zeros_like(values)], 0).astype(bf16)
    through = lax.dot_general(rows, w1[...], across_tokens, preferred_element_type=f32)
    through = through[0:8] + through[8:16] + through[16:24]
    through_out[...] = jnp.zeros((8, TOK), f32)
    for at, line in ((0, through[1:2]), (2, through[0:1])):
        through_out[at : at + 1] = line[:, :TOK]
        through_out[at + 1 : at + 2, : UNITS - TOK] = line[:, TOK:]


def first_kernel(shift, pos, *refs):
    blocks, mods, through, w1 = refs[:6], refs[6], refs[7], refs[8]
    out, offset_out, mean_out, offsets = refs[9:]
    place = place_of(pos, turn(pos[0], shift))
    at = pl.multiple_of(place * CHANNELS, 32)
    total = 0.0
    for q in range(4):
        for flip in range(2):
            block = block_of(blocks, q, flip, at, CHANNELS).astype(f32)
            total = total + jnp.sum(block, 0, keepdims=True)
    mean = total / SLICE
    square = 0.0
    for q in range(4):
        for flip in range(2):
            j = channel_block(pos, q, flip)
            offset = block_of(blocks, q, flip, at, CHANNELS).astype(f32) - mean
            square = square + jnp.sum(offset * offset, 0, keepdims=True)
            offsets[j] = (offset * mods[j][:, 1:2]).astype(bf16)
            rows = pl.ds(pl.multiple_of(j * CHANNELS, 32), CHANNELS)
            offset_out[rows, :] = offset.astype(bf16)
    mean_out[...] = mean
    out[:UNITS] = jnp.dot(
        w1[...], offsets[...].reshape(SLICE, TOK), preferred_element_type=f32
    ).astype(bf16)
    four = jnp.concatenate([mean, square, through[0:2]], 0)
    extra = parts_of(four, 3) + parts_of(through[2:4], 2)
    out[UNITS:] = jnp.concatenate(extra, 0).astype(bf16)


def hidden_kernel(pos, p0, p1, p2, p3, hidden_out, slope_out, rest_out, factor_out, stats_out):
    parts = (p0, p1, p2, p3)
    extras = [ref[UNITS:].astype(f32) for ref in parts]
    fours = [e[0:4] + e[4:8] + e[8:12] for e in extras]
    shifts = sum(e[12:14] + e[14:16] for e in extras)
    centre = 0.25 * (fours[0][0:1] + fours[1][0:1] + fours[2][0:1] + fours[3][0:1])
    spread = 0.0
    for four in fours:
        spread = spread + four[1:2] + SLICE * (four[0:1] - centre) ** 2
    inverse = lax.rsqrt(spread / D + eps)
    stats = jnp.concatenate([centre, inverse], 0)
    stats_out[...] = stats
    hidden_out[UNITS:] = jnp.concatenate(
        parts_of(stats, 3) + [jnp.zeros((EXTRA - 6, TOK), f32)], 0
    ).astype(bf16)
    columns = jnp.concatenate([four[2:4] for four in fours] + [shifts] * 4, 0).T
    for half, at in ((0, slice(0, TOK)), (1, slice(TOK, UNITS))):
        size = at.stop - at.start
        rest, total = 0.0, 0.0
        for i, ref in enumerate(parts):
            factor = columns[:size, 2 * i + half : 2 * i + half + 1]
            total = total + factor
            rest = rest + (ref[at].astype(f32) + factor * (fours[i][0:1] - centre))
        rest = rest * inverse
        hidden, slope = gelu_pair(rest + columns[:size, 8 + half : 9 + half])
        hidden_out[at] = hidden.astype(bf16)
        slope_out[at] = slope
        rest_out[at] = rest
        factor_out[at] = total


def second_kernel(pos, *refs):
    blocks, mods, w2 = refs[:6], refs[6], refs[7]
    sums, cot_out, scaled = refs[8:12], refs[12], refs[13]
    for shift, out in enumerate(sums):
        token = turn(pos[0], shift)
        at = pl.multiple_of(place_of(pos, token) * CHANNELS, 32)
        lanes = pl.ds(pl.multiple_of(token * TOK, TOK), TOK)
        for q in range(4):
            for flip in range(2):
                j = channel_block(pos, q, flip)
                block = block_of(blocks, q, flip, at, CHANNELS)
                rows = pl.ds(pl.multiple_of(j * CHANNELS, 32), CHANNELS)
                cot_out[rows, lanes] = block
                scaled[shift, rows, :] = (block.astype(f32) * mods[j][:, 2:3]).astype(bf16)
        out[...] = jnp.dot(w2[...], scaled[shift], preferred_element_type=f32).astype(bf16)


def grad_kernel(pos, own, one, two, three, slope, rest, factor, out):
    grad = own[...].astype(f32) + one[...].astype(f32)
    grad = grad + (two[...].astype(f32) + three[...].astype(f32))
    grad = (grad * slope[...]).astype(bf16)
    out[:UNITS] = grad
    wide = grad.astype(f32)
    first = jnp.sum(wide * factor[...], 0, keepdims=True)
    second = jnp.sum(wide * rest[...], 0, keepdims=True)
    line = lax.broadcasted_iota(jnp.int32, (8, TOK), 0)
    out[UNITS:] = packed(jnp.where(line == 3, first, jnp.where(line == 4, second, 0.0)))


def collect(pos, refs, store):
    for q, ref in enumerate(refs):
        at = pl.multiple_of(turn(pos[0], -q) * TOK, TOK)
        store[:, pl.ds(at, TOK)] = ref[:UNITS]


def second_weight_kernel(pos, b0, b1, b2, b3, cot, mods, w2, send, sums, store):
    collect(pos, (b0, b1, b2, b3), store)
    line = lax.broadcasted_iota(jnp.int32, (8, CHUNK), 0)
    for at in range(0, SLICE, CHUNK):
        part = slice(at, at + CHUNK)
        raw = lax.dot_general(
            store[...], cot[part, :], across_tokens, preferred_element_type=f32
        )
        total = jnp.sum(w2[:, part].astype(f32) * raw, 0, keepdims=True)
        sums[part, :] = jnp.where(line == 2, total, 0.0).T
        send[:, part] = (raw * (mods[2:3, part] * weight_scale)).astype(bf16)


def first_weight_kernel(pos, *refs):
    grads, hiddens, offsets, means = refs[:4], refs[4:8], refs[8:12], refs[12:16]
    mods, w1, send, sums, store, others = refs[16:]
    total, lift = 0.0, 0.0
    for q in range(4):
        at = (4 - q) % 4
        extra = hiddens[q][UNITS:].astype(f32)
        stats = extra[0:2] + extra[2:4] + extra[4:6]
        grad = grads[q][:UNITS].astype(f32)
        total = total + jnp.sum(grad, 1, keepdims=True)
        grad = grad * stats[1:2]
        lift = lift + jnp.sum(grad * (means[at][...] - stats[0:1]), 1, keepdims=True)
        lanes = slice(at * TOK, (at + 1) * TOK)
        store[:, lanes] = grad.astype(bf16)
        others[:, lanes] = offsets[at][...]
    line = lax.broadcasted_iota(jnp.int32, (8, CHUNK), 0)
    for at in range(0, SLICE, CHUNK):
        part = slice(at, at + CHUNK)
        raw = lift + lax.dot_general(
            store[...], others[part, :], across_tokens, preferred_element_type=f32
        )
        weight = w1[:, part].astype(f32)
        shift = jnp.sum(weight * total, 0, keepdims=True)
        scale = jnp.sum(weight * raw, 0, keepdims=True)
        sums[part, :] = jnp.where(line == 0, shift, jnp.where(line == 1, scale, 0.0)).T
        grad = (raw * mods[1:2, part] + total * mods[0:1, part]) * weight_scale
        send[:, part] = grad.astype(bf16)


def mod_kernel(pos, g0, g1, g2, g3, w1, sums_one, sums_two, *rest):
    keeps, sends, store, line = rest[:4], rest[4:8], rest[8], rest[9]
    grads = (g0, g1, g2, g3)
    collect(pos, grads, store)
    line[...] = jnp.zeros((8, TOK), f32)
    smalls = [unpacked(ref[UNITS:]) for ref in grads]
    for core, outs in ((pos[3], keeps), (1 - pos[3], sends)):
        for p, out in enumerate(outs):
            j = turn(pos[2], p) * 2 + core
            rows = pl.ds(pl.multiple_of(j * CHANNELS, 32), CHANNELS)
            product = jnp.dot(w1[rows, :], store[...], preferred_element_type=f32).astype(bf16)
            for token in range(4):
                out[turn(token, -pos[1]), :CHANNELS] = product[
                    :, token * TOK : (token + 1) * TOK
                ]
            line[:, :CHANNELS] = (sums_one[j] + sums_two[j]).T
            for q, small in enumerate(smalls):
                out[turn(pos[0], -q - pos[1]), CHANNELS:] = packed(small + line[...])


def add_up(out, parts):
    total = parts[0][:CHANNELS].astype(f32)
    small = unpacked(parts[0][CHANNELS:])
    for part in parts[1:]:
        total = total + part[:CHANNELS].astype(f32)
        small = small + unpacked(part[CHANNELS:])
    out[:CHANNELS] = total.astype(bf16)
    out[CHANNELS:] = packed(small)


def core_kernel(pos, *refs):
    for keep, other, out in zip(refs[:4], refs[4:8], refs[8:]):
        for s in range(4):
            add_up(out.at[s], [keep.at[s], other.at[s]])


def plane_kernel(pos, own, one, two, three, o0, o1, o2, o3):
    for s, out in enumerate((o0, o1, o2, o3)):
        add_up(out, [ref.at[s] for ref in (own, one, two, three)])


def states_kernel(pos, a0, a1, a2, a3, x, cot, stats, scale, out, mods_out):
    centre, inverse = stats[0:1], stats[1:2]
    grad_mod, small = 0.0, 0.0
    for ref in (a0, a1, a2, a3):
        grad_mod = grad_mod + ref[:CHANNELS].astype(f32)
        small = small + unpacked(ref[CHANNELS:])
    normed = (x[...].astype(f32) - centre) * inverse
    grad_normed = grad_mod * (1.0 + scale[...])
    out[...] = cot[...].astype(f32) + inverse * (
        grad_normed - small[3:4] / D - normed * (small[4:5] / D)
    )
    mods_out[...] = small * token_scale


def clips_kernel(pos, own, other, out):
    out[...] = own[...].astype(f32) + other[...].astype(f32)


def on_device(states, cotangent, shift_mod, scale_mod, gate_mod, first_weight, second_weight):
    row, col = lax.axis_index("row"), lax.axis_index("col")
    high, x, core = col // INNER, lax.rem(col, INNER) // 2, lax.rem(col, 2)
    pos = jnp.stack([row, high, x, core]).astype(jnp.int32)
    weight_one, weight_two = first_weight.T, second_weight.T
    own_x, own_c = states[0].T, cotangent[0].T

    own = (CHANNELS, TOK)
    piece = (CHANNELS + EXTRA, TOK)
    units = (UNITS, TOK)
    wide_units = (UNITS + EXTRA, TOK)
    stage = pltpu.VMEM((INNER, CHANNELS, TOK), bf16)

    pair = (2 * CHANNELS, TOK)
    wide_pair = (2 * CHANNELS + EXTRA, TOK)
    plain = jnp.concatenate([own_x, own_c], 0)
    (with_mods,) = whole(pack_kernel, [shaped(wide_pair)])(
        pos, plain, jnp.concatenate([shift_mod, scale_mod, gate_mod], 0)
    )
    x_planes, c_planes = whole(
        sort_kernel,
        [shaped((4 * CHANNELS + EXTRA, TOK)), shaped((4 * CHANNELS, TOK))],
    )(pos, *[spread_rows(plain, s) for s in (1, 2, 3)], spread_rows(with_mods, 0))
    x_lines = [x_planes] + [along_x(x_planes, q) for q in (1, 2, 3)]
    (first_turned,) = whole(turned_kernel, [shaped((SLICE, UNITS))])(pos, weight_one)
    x_blocks = both_cores(pos, after(x_lines, first_turned))
    c_lines = [c_planes] + [along_x(c_planes, q) for q in (1, 2, 3)]

    mods_column, mods_row, through = whole(
        mods_kernel,
        [
            shaped((INNER, CHANNELS, 8), f32),
            shaped((8, SLICE), f32),
            shaped((8, TOK), f32),
        ],
    )(pos, *x_blocks, weight_one)

    pre_sums, offsets, means = [None] * 4, [None] * 4, [None] * 4
    blocks = x_blocks
    for shift in (1, 3, 2, 0):
        pre_sums[shift], offsets[shift], means[shift] = whole(
            functools.partial(first_kernel, shift),
            [shaped(wide_units), shaped((SLICE, TOK)), shaped((1, TOK), f32)],
            [stage],
            some,
        )(pos, *blocks, mods_column, through, weight_one)
        blocks = after(blocks, pre_sums[shift])
    pre_sums = to_rows(pre_sums)
    hidden, slope, rest, factor, stats = whole(
        hidden_kernel,
        [
            shaped(wide_units),
            shaped(units, f32),
            shaped(units, f32),
            shaped((UNITS, 1), f32),
            shaped((2, TOK), f32),
        ],
    )(pos, *pre_sums)
    c_blocks = both_cores(pos, after(c_lines, pre_sums))
    *grad_sums, cot = whole(
        second_kernel,
        [shaped(units)] * 4 + [shaped((SLICE, TOKENS))],
        [pltpu.VMEM((4, SLICE, TOK), bf16)],
    )(pos, *c_blocks, mods_column, weight_two)
    hidden = all_rows(hidden)

    weights = pl.BlockSpec((UNITS, CHUNK), lambda i, pos: (0, i))
    scratch = [pltpu.VMEM((UNITS, TOKENS), bf16)]

    weight_shapes = [shaped((UNITS, SLICE)), shaped((SLICE, 8), f32)]
    own_second, sums_second = whole(second_weight_kernel, weight_shapes, scratch)(
        pos, *hidden, cot, mods_row, weight_two
    )
    other_second = swap_clips(own_second)
    grad_sums = to_rows(after(grad_sums, hidden[2]))
    (grad_pre,) = whole(grad_kernel, [shaped(wide_units)])(
        pos, *grad_sums, slope, rest, factor
    )
    grad_pre = all_rows(grad_pre)
    own_first, sums_first = whole(
        first_weight_kernel, weight_shapes, scratch + [pltpu.VMEM((SLICE, TOKENS), bf16)]
    )(pos, *grad_pre, *hidden, *offsets, *means, mods_row, weight_one)
    other_first = swap_clips(own_first)

    quarter = (4,) + piece
    terms = whole(
        mod_kernel, [shaped(quarter)] * 8, scratch + [pltpu.VMEM((8, TOK), f32)]
    )(
        pos,
        *grad_pre,
        first_turned,
        sums_first.reshape(INNER, CHANNELS, 8),
        sums_second.reshape(INNER, CHANNELS, 8),
    )
    lines = whole(core_kernel, [shaped(quarter)] * 4)(
        pos, *terms[:4], *after([across(term) for term in terms[4:]], other_second)
    )
    def clips_call(own, other):
        return call(
            clips_kernel,
            (SLICE // CHUNK,),
            [weights, weights],
            weights,
            shaped((UNITS, SLICE), f32),
        )(pos, own, other)

    grad_second = clips_call(own_second, other_second)
    planes = whole(plane_kernel, [shaped(piece)] * 4)(
        pos, lines[0], *after([along_x(lines[p], p) for p in (1, 2, 3)], grad_second)
    )
    pieces = [return_rows(planes[s], s) for s in range(4)]

    grad_first = clips_call(own_first, other_first)
    grad_states, mods_grad = whole(
        states_kernel, [shaped(own, f32), shaped((8, TOK), f32)]
    )(pos, *after(pieces, grad_first), own_x, own_c, stats, scale_mod.T)
    return (
        grad_states.T[None],
        grad_first.T,
        grad_second.T,
        mods_grad[0:1, :CHANNELS],
        mods_grad[1:2, :CHANNELS],
        mods_grad[2:3, :CHANNELS],
    )


def solution(mesh):
    return jax.shard_map(
        on_device,
        mesh=mesh,
        in_specs=(
            P("dp", "row", "col"),
            P("dp", "row", "col"),
            P("dp", "col"),
            P("dp", "col"),
            P("dp", "col"),
            P("row", "col"),
            P("row", "col"),
        ),
        out_specs=(
            P("dp", "row", "col"),
            P("row", "col"),
            P("row", "col"),
            P("dp", "col"),
            P("dp", "col"),
            P("dp", "col"),
        ),
        check_vma=False,
    )
```

```python
import functools
import math

import jax
import jax.numpy as jnp
from jax import lax
from jax.experimental import pallas as pl
from jax.experimental.pallas import tpu as pltpu
from jax.sharding import PartitionSpec as P

D = 5120
FF = 13824
ROWS = 4
COLS = 32
INNER = 8
CHANNELS = D // COLS
UNITS = FF // COLS
TOK = 256
SLICE = D // ROWS
TOKENS = ROWS * TOK
EXTRA = 16
CHUNK = 256

bf16, f32 = jnp.bfloat16, jnp.float32

eps = 1e-06
tanh_factor = 0.7978845608028654
cubic_term = 0.044715
token_scale = 1.0 / math.sqrt(ROWS * TOK)
weight_scale = 1.0 / math.sqrt(2 * ROWS * TOK)
across_tokens = (((1,), (1,)), ((), ()))


def gelu_pair(values):
    squares = values * values
    inner = jnp.tanh(tanh_factor * (values + cubic_term * squares * values))
    half = 0.5 * (1.0 + inner)
    slope = half + 0.5 * values * (1.0 - inner * inner) * tanh_factor * (
        1.0 + 3.0 * cubic_term * squares
    )
    return values * half, slope


def turn(value, offset):
    return lax.rem(value + offset + 8, 4)


def spread_rows(values, shift):
    pairs = [
        (a * COLS + b * INNER + i, b * COLS + ((a + shift) % 4) * INNER + i)
        for a in range(4)
        for b in range(4)
        for i in range(INNER)
    ]
    return lax.ppermute(values, ("row", "col"), pairs)


def return_rows(values, shift):
    pairs = [
        (a * COLS + b * INNER + i, ((b + shift) % 4) * COLS + a * INNER + i)
        for a in range(4)
        for b in range(4)
        for i in range(INNER)
    ]
    return lax.ppermute(values, ("row", "col"), pairs)


def along_x(values, shift):
    pairs = [
        (h * 8 + x * 2 + k, h * 8 + ((x + shift) % 4) * 2 + k)
        for h in range(4)
        for x in range(4)
        for k in range(2)
    ]
    return lax.ppermute(values, "col", pairs)


def across(values):
    return lax.ppermute(values, "col", [(c, c ^ 1) for c in range(COLS)])


def along_row(values, shift):
    return lax.ppermute(values, "row", [(a, (a + shift) % 4) for a in range(4)])


def all_rows(values):
    return [values] + [along_row(values, q) for q in (1, 2, 3)]


def to_rows(values):
    return [values[0]] + [along_row(values[q], q) for q in (1, 2, 3)]


def swap_clips(values):
    return lax.ppermute(values, "dp", [(0, 1), (1, 0)])


def both_cores(pos, lines):
    shape = shaped((2 * lines[0].shape[0], TOK))
    packs = whole(pair_kernel, [shape, shape])(pos, *lines)
    return list(lines) + [across(pack) for pack in packs]


def after(values, other):
    return lax.optimization_barrier((values, other))[0]


cheap = pl.CostEstimate(flops=1024, bytes_accessed=1024, transcendentals=0)
some = pl.CostEstimate(flops=1024, bytes_accessed=8000000, transcendentals=0)
limit = pltpu.CompilerParams(vmem_limit_bytes=16 * 1024 * 1024)


def call(kernel, grid, in_specs, out_specs, out_shape, scratch=()):
    return pl.pallas_call(
        kernel,
        grid_spec=pltpu.PrefetchScalarGridSpec(
            num_scalar_prefetch=1,
            grid=grid,
            in_specs=in_specs,
            out_specs=out_specs,
            scratch_shapes=list(scratch),
        ),
        out_shape=out_shape,
        compiler_params=limit,
        cost_estimate=cheap,
    )


def whole(kernel, out_shape, scratch=(), cost=cheap):
    vmem = pl.BlockSpec(memory_space=pltpu.VMEM)

    def run(pos, *args):
        return pl.pallas_call(
            kernel,
            in_specs=[pl.BlockSpec(memory_space=pltpu.SMEM)] + [vmem] * len(args),
            out_specs=[vmem] * len(out_shape),
            out_shape=out_shape,
            scratch_shapes=list(scratch),
            compiler_params=limit,
            cost_estimate=cost,
        )(pos, *args)

    return run


def full(shape):
    return pl.BlockSpec(shape, lambda i, pos: (0,) * len(shape))


def shaped(shape, kind=bf16):
    return jax.ShapeDtypeStruct(shape, kind)


def place_of(pos, token):
    return turn(pos[1] - token, -1)


def channel_block(pos, q, flip):
    core = pos[3] if flip == 0 else 1 - pos[3]
    return turn(pos[2], -q) * 2 + core


def parts_of(values, count):
    parts = []
    for _ in range(count):
        parts.append(values.astype(bf16).astype(f32))
        values = values - parts[-1]
    return parts


def packed(values):
    return jnp.concatenate(parts_of(values, 2), 0).astype(bf16)


def unpacked(rows):
    wide = rows.astype(f32)
    return wide[0:8] + wide[8:16]


def pack_kernel(pos, plain, mods, out):
    line = lax.broadcasted_iota(jnp.int32, (3, CHANNELS), 0)
    values = mods[...] + jnp.where(line == 1, 1.0, 0.0)
    rows = parts_of(values, 3) + [jnp.zeros((EXTRA - 9, CHANNELS), f32)]
    out[: 2 * CHANNELS] = plain[...]
    out[2 * CHANNELS :] = jnp.zeros((EXTRA, TOK), bf16)
    out[2 * CHANNELS :, :CHANNELS] = jnp.concatenate(rows, 0).astype(bf16)


def pair_kernel(pos, l0, l1, l2, l3, first, second):
    rows = l0.shape[0]
    first[:rows], first[rows:] = l0[...], l1[...]
    second[:rows], second[rows:] = l2[...], l3[...]


def block_of(blocks, q, flip, at, size):
    if flip == 0:
        return blocks[q][pl.ds(at, size), :]
    rows = blocks[0].shape[0]
    return blocks[4 + q // 2][pl.ds(at + (q % 2) * rows, size), :]


def sort_kernel(pos, b0, b1, b2, b3, x, cot):
    for at, ref in enumerate((b0, b1, b2, b3)):
        rows = slice(at * CHANNELS, (at + 1) * CHANNELS)
        x[rows] = ref[:CHANNELS]
        cot[rows] = ref[CHANNELS : 2 * CHANNELS]
    x[4 * CHANNELS :] = b3[2 * CHANNELS :]


def turned_kernel(pos, w1, out):
    out[...] = w1[...].T


def mods_kernel(pos, *refs):
    blocks, w1, mods_column, mods_row, through_out = refs[:6], refs[6], refs[7], refs[8], refs[9]
    for q in range(4):
        for flip in range(2):
            rows = block_of(blocks, q, flip, 4 * CHANNELS, EXTRA).astype(f32)
            values = jnp.concatenate([rows[0:3] + rows[3:6] + rows[6:9], rows[9:14]], 0)
            mods_column[channel_block(pos, q, flip)] = values.T[:CHANNELS]
    values = mods_column[...].reshape(SLICE, 8).T
    mods_row[...] = values
    rows = jnp.concatenate(parts_of(values, 3) + [jnp.zeros_like(values)], 0).astype(bf16)
    through = lax.dot_general(rows, w1[...], across_tokens, preferred_element_type=f32)
    through = through[0:8] + through[8:16] + through[16:24]
    through_out[...] = jnp.zeros((8, TOK), f32)
    for at, line in ((0, through[1:2]), (2, through[0:1])):
        through_out[at : at + 1] = line[:, :TOK]
        through_out[at + 1 : at + 2, : UNITS - TOK] = line[:, TOK:]


def first_kernel(shift, pos, *refs):
    blocks, mods, through, w1 = refs[:6], refs[6], refs[7], refs[8]
    out, offset_out, mean_out, offsets = refs[9:]
    place = place_of(pos, turn(pos[0], shift))
    at = pl.multiple_of(place * CHANNELS, 32)
    total = 0.0
    for q in range(4):
        for flip in range(2):
            block = block_of(blocks, q, flip, at, CHANNELS).astype(f32)
            total = total + jnp.sum(block, 0, keepdims=True)
    mean = total / SLICE
    square = 0.0
    for q in range(4):
        for flip in range(2):
            j = channel_block(pos, q, flip)
            offset = block_of(blocks, q, flip, at, CHANNELS).astype(f32) - mean
            square = square + jnp.sum(offset * offset, 0, keepdims=True)
            offsets[j] = (offset * mods[j][:, 1:2]).astype(bf16)
            rows = pl.ds(pl.multiple_of(j * CHANNELS, 32), CHANNELS)
            offset_out[rows, :] = offset.astype(bf16)
    mean_out[...] = mean
    out[:UNITS] = jnp.dot(
        w1[...], offsets[...].reshape(SLICE, TOK), preferred_element_type=f32
    ).astype(bf16)
    four = jnp.concatenate([mean, square, through[0:2]], 0)
    extra = parts_of(four, 3) + parts_of(through[2:4], 2)
    out[UNITS:] = jnp.concatenate(extra, 0).astype(bf16)


def hidden_kernel(pos, p0, p1, p2, p3, hidden_out, slope_out, rest_out, factor_out, stats_out):
    parts = (p0, p1, p2, p3)
    extras = [ref[UNITS:].astype(f32) for ref in parts]
    fours = [e[0:4] + e[4:8] + e[8:12] for e in extras]
    shifts = sum(e[12:14] + e[14:16] for e in extras)
    centre = 0.25 * (fours[0][0:1] + fours[1][0:1] + fours[2][0:1] + fours[3][0:1])
    spread = 0.0
    for four in fours:
        spread = spread + four[1:2] + SLICE * (four[0:1] - centre) ** 2
    inverse = lax.rsqrt(spread / D + eps)
    stats = jnp.concatenate([centre, inverse], 0)
    stats_out[...] = stats
    hidden_out[UNITS:] = jnp.concatenate(
        parts_of(stats, 3) + [jnp.zeros((EXTRA - 6, TOK), f32)], 0
    ).astype(bf16)
    columns = jnp.concatenate([four[2:4] for four in fours] + [shifts] * 4, 0).T
    for half, at in ((0, slice(0, TOK)), (1, slice(TOK, UNITS))):
        size = at.stop - at.start
        rest, total = 0.0, 0.0
        for i, ref in enumerate(parts):
            factor = columns[:size, 2 * i + half : 2 * i + half + 1]
            total = total + factor
            rest = rest + (ref[at].astype(f32) + factor * (fours[i][0:1] - centre))
        rest = rest * inverse
        hidden, slope = gelu_pair(rest + columns[:size, 8 + half : 9 + half])
        hidden_out[at] = hidden.astype(bf16)
        slope_out[at] = slope
        rest_out[at] = rest
        factor_out[at] = total


def second_kernel(pos, *refs):
    blocks, mods, w2 = refs[:6], refs[6], refs[7]
    sums, cot_out, scaled = refs[8:12], refs[12], refs[13]
    for shift, out in enumerate(sums):
        token = turn(pos[0], shift)
        at = pl.multiple_of(place_of(pos, token) * CHANNELS, 32)
        lanes = pl.ds(pl.multiple_of(token * TOK, TOK), TOK)
        for q in range(4):
            for flip in range(2):
                j = channel_block(pos, q, flip)
                block = block_of(blocks, q, flip, at, CHANNELS)
                rows = pl.ds(pl.multiple_of(j * CHANNELS, 32), CHANNELS)
                cot_out[rows, lanes] = block
                scaled[shift, rows, :] = (block.astype(f32) * mods[j][:, 2:3]).astype(bf16)
        out[...] = jnp.dot(w2[...], scaled[shift], preferred_element_type=f32).astype(bf16)


def grad_kernel(pos, own, one, two, three, slope, rest, factor, out):
    grad = own[...].astype(f32) + one[...].astype(f32)
    grad = grad + (two[...].astype(f32) + three[...].astype(f32))
    grad = (grad * slope[...]).astype(bf16)
    out[:UNITS] = grad
    wide = grad.astype(f32)
    first = jnp.sum(wide * factor[...], 0, keepdims=True)
    second = jnp.sum(wide * rest[...], 0, keepdims=True)
    line = lax.broadcasted_iota(jnp.int32, (8, TOK), 0)
    out[UNITS:] = packed(jnp.where(line == 3, first, jnp.where(line == 4, second, 0.0)))


def collect(pos, refs, store):
    for q, ref in enumerate(refs):
        at = pl.multiple_of(turn(pos[0], -q) * TOK, TOK)
        store[:, pl.ds(at, TOK)] = ref[:UNITS]


def second_weight_kernel(pos, b0, b1, b2, b3, cot, mods, w2, send, sums, store):
    collect(pos, (b0, b1, b2, b3), store)
    line = lax.broadcasted_iota(jnp.int32, (8, CHUNK), 0)
    for at in range(0, SLICE, CHUNK):
        part = slice(at, at + CHUNK)
        raw = lax.dot_general(
            store[...], cot[part, :], across_tokens, preferred_element_type=f32
        )
        total = jnp.sum(w2[:, part].astype(f32) * raw, 0, keepdims=True)
        sums[part, :] = jnp.where(line == 2, total, 0.0).T
        send[:, part] = (raw * (mods[2:3, part] * weight_scale)).astype(bf16)


def first_weight_kernel(pos, *refs):
    grads, hiddens, offsets, means = refs[:4], refs[4:8], refs[8:12], refs[12:16]
    mods, w1, send, sums, store, others = refs[16:]
    total, lift = 0.0, 0.0
    for q in range(4):
        at = (4 - q) % 4
        extra = hiddens[q][UNITS:].astype(f32)
        stats = extra[0:2] + extra[2:4] + extra[4:6]
        grad = grads[q][:UNITS].astype(f32)
        total = total + jnp.sum(grad, 1, keepdims=True)
        grad = grad * stats[1:2]
        lift = lift + jnp.sum(grad * (means[at][...] - stats[0:1]), 1, keepdims=True)
        lanes = slice(at * TOK, (at + 1) * TOK)
        store[:, lanes] = grad.astype(bf16)
        others[:, lanes] = offsets[at][...]
    line = lax.broadcasted_iota(jnp.int32, (8, CHUNK), 0)
    for at in range(0, SLICE, CHUNK):
        part = slice(at, at + CHUNK)
        raw = lift + lax.dot_general(
            store[...], others[part, :], across_tokens, preferred_element_type=f32
        )
        weight = w1[:, part].astype(f32)
        shift = jnp.sum(weight * total, 0, keepdims=True)
        scale = jnp.sum(weight * raw, 0, keepdims=True)
        sums[part, :] = jnp.where(line == 0, shift, jnp.where(line == 1, scale, 0.0)).T
        grad = (raw * mods[1:2, part] + total * mods[0:1, part]) * weight_scale
        send[:, part] = grad.astype(bf16)


def mod_kernel(pos, g0, g1, g2, g3, w1, sums_one, sums_two, *rest):
    keeps, sends, store, line = rest[:4], rest[4:8], rest[8], rest[9]
    grads = (g0, g1, g2, g3)
    collect(pos, grads, store)
    line[...] = jnp.zeros((8, TOK), f32)
    smalls = [unpacked(ref[UNITS:]) for ref in grads]
    for core, outs in ((pos[3], keeps), (1 - pos[3], sends)):
        for p, out in enumerate(outs):
            j = turn(pos[2], p) * 2 + core
            rows = pl.ds(pl.multiple_of(j * CHANNELS, 32), CHANNELS)
            product = jnp.dot(w1[rows, :], store[...], preferred_element_type=f32).astype(bf16)
            for token in range(4):
                out[turn(token, -pos[1]), :CHANNELS] = product[
                    :, token * TOK : (token + 1) * TOK
                ]
            line[:, :CHANNELS] = (sums_one[j] + sums_two[j]).T
            for q, small in enumerate(smalls):
                out[turn(pos[0], -q - pos[1]), CHANNELS:] = packed(small + line[...])


def add_up(out, parts):
    total = parts[0][:CHANNELS].astype(f32)
    small = unpacked(parts[0][CHANNELS:])
    for part in parts[1:]:
        total = total + part[:CHANNELS].astype(f32)
        small = small + unpacked(part[CHANNELS:])
    out[:CHANNELS] = total.astype(bf16)
    out[CHANNELS:] = packed(small)


def core_kernel(pos, *refs):
    for keep, other, out in zip(refs[:4], refs[4:8], refs[8:]):
        for s in range(4):
            add_up(out.at[s], [keep.at[s], other.at[s]])


def plane_kernel(pos, own, one, two, three, o0, o1, o2, o3):
    for s, out in enumerate((o0, o1, o2, o3)):
        add_up(out, [ref.at[s] for ref in (own, one, two, three)])


def states_kernel(pos, a0, a1, a2, a3, x, cot, stats, scale, out, mods_out):
    centre, inverse = stats[0:1], stats[1:2]
    grad_mod, small = 0.0, 0.0
    for ref in (a0, a1, a2, a3):
        grad_mod = grad_mod + ref[:CHANNELS].astype(f32)
        small = small + unpacked(ref[CHANNELS:])
    normed = (x[...].astype(f32) - centre) * inverse
    grad_normed = grad_mod * (1.0 + scale[...])
    out[...] = cot[...].astype(f32) + inverse * (
        grad_normed - small[3:4] / D - normed * (small[4:5] / D)
    )
    mods_out[...] = small * token_scale


def clips_kernel(pos, own, other, out):
    out[...] = own[...].astype(f32) + other[...].astype(f32)


def on_device(states, cotangent, shift_mod, scale_mod, gate_mod, first_weight, second_weight):
    row, col = lax.axis_index("row"), lax.axis_index("col")
    high, x, core = col // INNER, lax.rem(col, INNER) // 2, lax.rem(col, 2)
    pos = jnp.stack([row, high, x, core]).astype(jnp.int32)
    weight_one, weight_two = first_weight.T, second_weight.T
    own_x, own_c = states[0].T, cotangent[0].T

    own = (CHANNELS, TOK)
    piece = (CHANNELS + EXTRA, TOK)
    units = (UNITS, TOK)
    wide_units = (UNITS + EXTRA, TOK)
    stage = pltpu.VMEM((INNER, CHANNELS, TOK), bf16)

    pair = (2 * CHANNELS, TOK)
    wide_pair = (2 * CHANNELS + EXTRA, TOK)
    plain = jnp.concatenate([own_x, own_c], 0)
    (with_mods,) = whole(pack_kernel, [shaped(wide_pair)])(
        pos, plain, jnp.concatenate([shift_mod, scale_mod, gate_mod], 0)
    )
    x_planes, c_planes = whole(
        sort_kernel,
        [shaped((4 * CHANNELS + EXTRA, TOK)), shaped((4 * CHANNELS, TOK))],
    )(pos, *[spread_rows(plain, s) for s in (1, 2, 3)], spread_rows(with_mods, 0))
    x_lines = [x_planes] + [along_x(x_planes, q) for q in (1, 2, 3)]
    (first_turned,) = whole(turned_kernel, [shaped((SLICE, UNITS))])(pos, weight_one)
    x_blocks = both_cores(pos, after(x_lines, first_turned))
    c_lines = [c_planes] + [along_x(c_planes, q) for q in (1, 2, 3)]

    mods_column, mods_row, through = whole(
        mods_kernel,
        [
            shaped((INNER, CHANNELS, 8), f32),
            shaped((8, SLICE), f32),
            shaped((8, TOK), f32),
        ],
    )(pos, *x_blocks, weight_one)

    pre_sums, offsets, means = [None] * 4, [None] * 4, [None] * 4
    blocks = x_blocks
    for shift in (1, 3, 2, 0):
        pre_sums[shift], offsets[shift], means[shift] = whole(
            functools.partial(first_kernel, shift),
            [shaped(wide_units), shaped((SLICE, TOK)), shaped((1, TOK), f32)],
            [stage],
            some,
        )(pos, *blocks, mods_column, through, weight_one)
        blocks = after(blocks, pre_sums[shift])
    pre_sums = to_rows(pre_sums)
    hidden, slope, rest, factor, stats = whole(
        hidden_kernel,
        [
            shaped(wide_units),
            shaped(units, f32),
            shaped(units, f32),
            shaped((UNITS, 1), f32),
            shaped((2, TOK), f32),
        ],
    )(pos, *pre_sums)
    c_blocks = both_cores(pos, after(c_lines, (pre_sums[1], pre_sums[0])))
    *grad_sums, cot = whole(
        second_kernel,
        [shaped(units)] * 4 + [shaped((SLICE, TOKENS))],
        [pltpu.VMEM((4, SLICE, TOK), bf16)],
    )(pos, *c_blocks, mods_column, weight_two)
    grad_sums = to_rows(grad_sums)
    (grad_pre,) = whole(grad_kernel, [shaped(wide_units)])(
        pos, *grad_sums, slope, rest, factor
    )
    hidden = all_rows(after(hidden, grad_pre))
    grad_pre = all_rows(grad_pre)

    weights = pl.BlockSpec((UNITS, CHUNK), lambda i, pos: (0, i))
    scratch = [pltpu.VMEM((UNITS, TOKENS), bf16)]

    weight_shapes = [shaped((UNITS, SLICE)), shaped((SLICE, 8), f32)]
    own_second, sums_second = whole(second_weight_kernel, weight_shapes, scratch)(
        pos, *after(hidden, grad_pre[2]), cot, mods_row, weight_two
    )
    other_second = swap_clips(own_second)
    own_first, sums_first = whole(
        first_weight_kernel, weight_shapes, scratch + [pltpu.VMEM((SLICE, TOKENS), bf16)]
    )(pos, *grad_pre, *hidden, *offsets, *means, mods_row, weight_one)
    other_first = swap_clips(own_first)

    quarter = (4,) + piece
    terms = whole(
        mod_kernel, [shaped(quarter)] * 8, scratch + [pltpu.VMEM((8, TOK), f32)]
    )(
        pos,
        *grad_pre,
        first_turned,
        sums_first.reshape(INNER, CHANNELS, 8),
        sums_second.reshape(INNER, CHANNELS, 8),
    )
    lines = whole(core_kernel, [shaped(quarter)] * 4)(
        pos, *terms[:4], *after([across(term) for term in terms[4:]], other_second)
    )
    def clips_call(own, other):
        return call(
            clips_kernel,
            (SLICE // CHUNK,),
            [weights, weights],
            weights,
            shaped((UNITS, SLICE), f32),
        )(pos, own, other)

    grad_second = clips_call(own_second, other_second)
    planes = whole(plane_kernel, [shaped(piece)] * 4)(
        pos, lines[0], *after([along_x(lines[p], p) for p in (1, 2, 3)], grad_second)
    )
    pieces = [return_rows(planes[s], s) for s in range(4)]

    grad_first = clips_call(own_first, other_first)
    grad_states, mods_grad = whole(
        states_kernel, [shaped(own, f32), shaped((8, TOK), f32)]
    )(pos, *after(pieces, grad_first), own_x, own_c, stats, scale_mod.T)
    return (
        grad_states.T[None],
        grad_first.T,
        grad_second.T,
        mods_grad[0:1, :CHANNELS],
        mods_grad[1:2, :CHANNELS],
        mods_grad[2:3, :CHANNELS],
    )


def solution(mesh):
    return jax.shard_map(
        on_device,
        mesh=mesh,
        in_specs=(
            P("dp", "row", "col"),
            P("dp", "row", "col"),
            P("dp", "col"),
            P("dp", "col"),
            P("dp", "col"),
            P("row", "col"),
            P("row", "col"),
        ),
        out_specs=(
            P("dp", "row", "col"),
            P("row", "col"),
            P("row", "col"),
            P("dp", "col"),
            P("dp", "col"),
            P("dp", "col"),
        ),
        check_vma=False,
    )
```

```python
import functools
import math

import jax
import jax.numpy as jnp
from jax import lax
from jax.experimental import pallas as pl
from jax.experimental.pallas import tpu as pltpu
from jax.sharding import PartitionSpec as P

D = 5120
FF = 13824
ROWS = 4
COLS = 32
INNER = 8
CHANNELS = D // COLS
UNITS = FF // COLS
TOK = 256
SLICE = D // ROWS
TOKENS = ROWS * TOK
EXTRA = 16
CHUNK = 256

bf16, f32 = jnp.bfloat16, jnp.float32

eps = 1e-06
tanh_factor = 0.7978845608028654
cubic_term = 0.044715
token_scale = 1.0 / math.sqrt(ROWS * TOK)
weight_scale = 1.0 / math.sqrt(2 * ROWS * TOK)
across_tokens = (((1,), (1,)), ((), ()))


def gelu_pair(values):
    squares = values * values
    inner = jnp.tanh(tanh_factor * (values + cubic_term * squares * values))
    half = 0.5 * (1.0 + inner)
    slope = half + 0.5 * values * (1.0 - inner * inner) * tanh_factor * (
        1.0 + 3.0 * cubic_term * squares
    )
    return values * half, slope


def turn(value, offset):
    return lax.rem(value + offset + 8, 4)


def spread_rows(values, shift):
    pairs = [
        (a * COLS + b * INNER + i, b * COLS + ((a + shift) % 4) * INNER + i)
        for a in range(4)
        for b in range(4)
        for i in range(INNER)
    ]
    return lax.ppermute(values, ("row", "col"), pairs)


def along_high(values, shift):
    pairs = [(h * 8 + i, ((h + shift) % 4) * 8 + i) for h in range(4) for i in range(INNER)]
    return lax.ppermute(values, "col", pairs)


def along_x(values, shift):
    pairs = [
        (h * 8 + x * 2 + k, h * 8 + ((x + shift) % 4) * 2 + k)
        for h in range(4)
        for x in range(4)
        for k in range(2)
    ]
    return lax.ppermute(values, "col", pairs)


def across(values):
    return lax.ppermute(values, "col", [(c, c ^ 1) for c in range(COLS)])


def along_row(values, shift):
    return lax.ppermute(values, "row", [(a, (a + shift) % 4) for a in range(4)])


def all_rows(values):
    return [values] + [along_row(values, q) for q in (1, 2, 3)]


def to_rows(values):
    return [values[0]] + [along_row(values[q], q) for q in (1, 2, 3)]


def swap_clips(values):
    return lax.ppermute(values, "dp", [(0, 1), (1, 0)])


def both_cores(pos, lines):
    shape = shaped((2 * lines[0].shape[0], TOK))
    packs = whole(pair_kernel, [shape, shape])(pos, *lines)
    return list(lines) + [across(pack) for pack in packs]


def after(values, other):
    return lax.optimization_barrier((values, other))[0]


cheap = pl.CostEstimate(flops=1024, bytes_accessed=1024, transcendentals=0)
some = pl.CostEstimate(flops=1024, bytes_accessed=8000000, transcendentals=0)
limit = pltpu.CompilerParams(vmem_limit_bytes=16 * 1024 * 1024)


def call(kernel, grid, in_specs, out_specs, out_shape, scratch=()):
    return pl.pallas_call(
        kernel,
        grid_spec=pltpu.PrefetchScalarGridSpec(
            num_scalar_prefetch=1,
            grid=grid,
            in_specs=in_specs,
            out_specs=out_specs,
            scratch_shapes=list(scratch),
        ),
        out_shape=out_shape,
        compiler_params=limit,
        cost_estimate=cheap,
    )


def whole(kernel, out_shape, scratch=(), cost=cheap):
    vmem = pl.BlockSpec(memory_space=pltpu.VMEM)

    def run(pos, *args):
        return pl.pallas_call(
            kernel,
            in_specs=[pl.BlockSpec(memory_space=pltpu.SMEM)] + [vmem] * len(args),
            out_specs=[vmem] * len(out_shape),
            out_shape=out_shape,
            scratch_shapes=list(scratch),
            compiler_params=limit,
            cost_estimate=cost,
        )(pos, *args)

    return run


def full(shape):
    return pl.BlockSpec(shape, lambda i, pos: (0,) * len(shape))


def shaped(shape, kind=bf16):
    return jax.ShapeDtypeStruct(shape, kind)


def place_of(pos, token):
    return turn(pos[1] - token, -1)


def channel_block(pos, q, flip):
    core = pos[3] if flip == 0 else 1 - pos[3]
    return turn(pos[2], -q) * 2 + core


def parts_of(values, count):
    parts = []
    for _ in range(count):
        parts.append(values.astype(bf16).astype(f32))
        values = values - parts[-1]
    return parts


def packed(values):
    return jnp.concatenate(parts_of(values, 2), 0).astype(bf16)


def unpacked(rows):
    wide = rows.astype(f32)
    return wide[0:8] + wide[8:16]


def pack_kernel(pos, plain, mods, out):
    line = lax.broadcasted_iota(jnp.int32, (3, CHANNELS), 0)
    values = mods[...] + jnp.where(line == 1, 1.0, 0.0)
    rows = parts_of(values, 3) + [jnp.zeros((EXTRA - 9, CHANNELS), f32)]
    out[: 2 * CHANNELS] = plain[...]
    out[2 * CHANNELS :] = jnp.zeros((EXTRA, TOK), bf16)
    out[2 * CHANNELS :, :CHANNELS] = jnp.concatenate(rows, 0).astype(bf16)


def pair_kernel(pos, l0, l1, l2, l3, first, second):
    rows = l0.shape[0]
    first[:rows], first[rows:] = l0[...], l1[...]
    second[:rows], second[rows:] = l2[...], l3[...]


def block_of(blocks, q, flip, at, size):
    if flip == 0:
        return blocks[q][pl.ds(at, size), :]
    rows = blocks[0].shape[0]
    return blocks[4 + q // 2][pl.ds(at + (q % 2) * rows, size), :]


def sort_kernel(pos, b0, b1, b2, b3, x, cot):
    for at, ref in enumerate((b0, b1, b2, b3)):
        rows = slice(at * CHANNELS, (at + 1) * CHANNELS)
        x[rows] = ref[:CHANNELS]
        cot[rows] = ref[CHANNELS : 2 * CHANNELS]
    x[4 * CHANNELS :] = b3[2 * CHANNELS :]


def turned_kernel(pos, w1, out):
    out[...] = w1[...].T


def mods_kernel(pos, *refs):
    blocks, w1, mods_column, mods_row, through_out = refs[:6], refs[6], refs[7], refs[8], refs[9]
    for q in range(4):
        for flip in range(2):
            rows = block_of(blocks, q, flip, 4 * CHANNELS, EXTRA).astype(f32)
            values = jnp.concatenate([rows[0:3] + rows[3:6] + rows[6:9], rows[9:14]], 0)
            mods_column[channel_block(pos, q, flip)] = values.T[:CHANNELS]
    values = mods_column[...].reshape(SLICE, 8).T
    mods_row[...] = values
    rows = jnp.concatenate(parts_of(values, 3) + [jnp.zeros_like(values)], 0).astype(bf16)
    through = lax.dot_general(rows, w1[...], across_tokens, preferred_element_type=f32)
    through = through[0:8] + through[8:16] + through[16:24]
    through_out[...] = jnp.zeros((8, TOK), f32)
    for at, line in ((0, through[1:2]), (2, through[0:1])):
        through_out[at : at + 1] = line[:, :TOK]
        through_out[at + 1 : at + 2, : UNITS - TOK] = line[:, TOK:]


def first_kernel(shift, pos, *refs):
    blocks, mods, through, w1 = refs[:6], refs[6], refs[7], refs[8]
    out, offset_out, mean_out, offsets = refs[9:]
    place = place_of(pos, turn(pos[0], shift))
    at = pl.multiple_of(place * CHANNELS, 32)
    total = 0.0
    for q in range(4):
        for flip in range(2):
            block = block_of(blocks, q, flip, at, CHANNELS).astype(f32)
            total = total + jnp.sum(block, 0, keepdims=True)
    mean = total / SLICE
    square = 0.0
    for q in range(4):
        for flip in range(2):
            j = channel_block(pos, q, flip)
            offset = block_of(blocks, q, flip, at, CHANNELS).astype(f32) - mean
            square = square + jnp.sum(offset * offset, 0, keepdims=True)
            offsets[j] = (offset * mods[j][:, 1:2]).astype(bf16)
            rows = pl.ds(pl.multiple_of(j * CHANNELS, 32), CHANNELS)
            offset_out[rows, :] = offset.astype(bf16)
    mean_out[...] = mean
    out[:UNITS] = jnp.dot(
        w1[...], offsets[...].reshape(SLICE, TOK), preferred_element_type=f32
    ).astype(bf16)
    four = jnp.concatenate([mean, square, through[0:2]], 0)
    extra = parts_of(four, 3) + parts_of(through[2:4], 2)
    out[UNITS:] = jnp.concatenate(extra, 0).astype(bf16)


def hidden_kernel(pos, p0, p1, p2, p3, hidden_out, slope_out, rest_out, factor_out, stats_out):
    parts = (p0, p1, p2, p3)
    extras = [ref[UNITS:].astype(f32) for ref in parts]
    fours = [e[0:4] + e[4:8] + e[8:12] for e in extras]
    shifts = sum(e[12:14] + e[14:16] for e in extras)
    centre = 0.25 * (fours[0][0:1] + fours[1][0:1] + fours[2][0:1] + fours[3][0:1])
    spread = 0.0
    for four in fours:
        spread = spread + four[1:2] + SLICE * (four[0:1] - centre) ** 2
    inverse = lax.rsqrt(spread / D + eps)
    stats = jnp.concatenate([centre, inverse], 0)
    stats_out[...] = stats
    hidden_out[UNITS:] = jnp.concatenate(
        parts_of(stats, 3) + [jnp.zeros((EXTRA - 6, TOK), f32)], 0
    ).astype(bf16)
    columns = jnp.concatenate([four[2:4] for four in fours] + [shifts] * 4, 0).T
    for half, at in ((0, slice(0, TOK)), (1, slice(TOK, UNITS))):
        size = at.stop - at.start
        rest, total = 0.0, 0.0
        for i, ref in enumerate(parts):
            factor = columns[:size, 2 * i + half : 2 * i + half + 1]
            total = total + factor
            rest = rest + (ref[at].astype(f32) + factor * (fours[i][0:1] - centre))
        rest = rest * inverse
        hidden, slope = gelu_pair(rest + columns[:size, 8 + half : 9 + half])
        hidden_out[at] = hidden.astype(bf16)
        slope_out[at] = slope
        rest_out[at] = rest
        factor_out[at] = total


def second_kernel(pos, *refs):
    blocks, mods, w2 = refs[:6], refs[6], refs[7]
    sums, cot_out, scaled = refs[8:12], refs[12], refs[13]
    for shift, out in enumerate(sums):
        token = turn(pos[0], shift)
        at = pl.multiple_of(place_of(pos, token) * CHANNELS, 32)
        lanes = pl.ds(pl.multiple_of(token * TOK, TOK), TOK)
        for q in range(4):
            for flip in range(2):
                j = channel_block(pos, q, flip)
                block = block_of(blocks, q, flip, at, CHANNELS)
                rows = pl.ds(pl.multiple_of(j * CHANNELS, 32), CHANNELS)
                cot_out[rows, lanes] = block
                scaled[shift, rows, :] = (block.astype(f32) * mods[j][:, 2:3]).astype(bf16)
        out[...] = jnp.dot(w2[...], scaled[shift], preferred_element_type=f32).astype(bf16)


def grad_kernel(pos, own, one, two, three, slope, rest, factor, out):
    grad = own[...].astype(f32) + one[...].astype(f32)
    grad = grad + (two[...].astype(f32) + three[...].astype(f32))
    grad = (grad * slope[...]).astype(bf16)
    out[:UNITS] = grad
    wide = grad.astype(f32)
    first = jnp.sum(wide * factor[...], 0, keepdims=True)
    second = jnp.sum(wide * rest[...], 0, keepdims=True)
    line = lax.broadcasted_iota(jnp.int32, (8, TOK), 0)
    out[UNITS:] = packed(jnp.where(line == 3, first, jnp.where(line == 4, second, 0.0)))


def collect(pos, refs, store):
    for q, ref in enumerate(refs):
        at = pl.multiple_of(turn(pos[0], -q) * TOK, TOK)
        store[:, pl.ds(at, TOK)] = ref[:UNITS]


def second_weight_kernel(pos, b0, b1, b2, b3, cot, mods, w2, send, sums, store):
    collect(pos, (b0, b1, b2, b3), store)
    line = lax.broadcasted_iota(jnp.int32, (8, CHUNK), 0)
    for at in range(0, SLICE, CHUNK):
        part = slice(at, at + CHUNK)
        raw = lax.dot_general(
            store[...], cot[part, :], across_tokens, preferred_element_type=f32
        )
        total = jnp.sum(w2[:, part].astype(f32) * raw, 0, keepdims=True)
        sums[part, :] = jnp.where(line == 2, total, 0.0).T
        send[:, part] = (raw * (mods[2:3, part] * weight_scale)).astype(bf16)


def first_weight_kernel(pos, *refs):
    grads, hiddens, offsets, means = refs[:4], refs[4:8], refs[8:12], refs[12:16]
    mods, w1, send, sums, store, others = refs[16:]
    total, lift = 0.0, 0.0
    for q in range(4):
        at = (4 - q) % 4
        extra = hiddens[q][UNITS:].astype(f32)
        stats = extra[0:2] + extra[2:4] + extra[4:6]
        grad = grads[q][:UNITS].astype(f32)
        total = total + jnp.sum(grad, 1, keepdims=True)
        grad = grad * stats[1:2]
        lift = lift + jnp.sum(grad * (means[at][...] - stats[0:1]), 1, keepdims=True)
        lanes = slice(at * TOK, (at + 1) * TOK)
        store[:, lanes] = grad.astype(bf16)
        others[:, lanes] = offsets[at][...]
    line = lax.broadcasted_iota(jnp.int32, (8, CHUNK), 0)
    for at in range(0, SLICE, CHUNK):
        part = slice(at, at + CHUNK)
        raw = lift + lax.dot_general(
            store[...], others[part, :], across_tokens, preferred_element_type=f32
        )
        weight = w1[:, part].astype(f32)
        shift = jnp.sum(weight * total, 0, keepdims=True)
        scale = jnp.sum(weight * raw, 0, keepdims=True)
        sums[part, :] = jnp.where(line == 0, shift, jnp.where(line == 1, scale, 0.0)).T
        grad = (raw * mods[1:2, part] + total * mods[0:1, part]) * weight_scale
        send[:, part] = grad.astype(bf16)


def mod_kernel(pos, g0, g1, g2, g3, w1, sums_one, sums_two, *rest):
    keeps, sends, store, line = rest[:4], rest[4:8], rest[8], rest[9]
    grads = (g0, g1, g2, g3)
    collect(pos, grads, store)
    line[...] = jnp.zeros((8, TOK), f32)
    smalls = [unpacked(ref[UNITS:]) for ref in grads]
    for core, outs in ((pos[3], keeps), (1 - pos[3], sends)):
        for p, out in enumerate(outs):
            j = turn(pos[2], p) * 2 + core
            rows = pl.ds(pl.multiple_of(j * CHANNELS, 32), CHANNELS)
            product = jnp.dot(w1[rows, :], store[...], preferred_element_type=f32).astype(bf16)
            for token in range(4):
                out[turn(token, -pos[0]), :CHANNELS] = product[
                    :, token * TOK : (token + 1) * TOK
                ]
            line[:, :CHANNELS] = (sums_one[j] + sums_two[j]).T
            for q, small in enumerate(smalls):
                out[(4 - q) % 4, CHANNELS:] = packed(small + line[...])


def add_up(out, parts):
    total = parts[0][:CHANNELS].astype(f32)
    small = unpacked(parts[0][CHANNELS:])
    for part in parts[1:]:
        total = total + part[:CHANNELS].astype(f32)
        small = small + unpacked(part[CHANNELS:])
    out[:CHANNELS] = total.astype(bf16)
    out[CHANNELS:] = packed(small)


def core_kernel(pos, *refs):
    for keep, other, out in zip(refs[:4], refs[4:8], refs[8:]):
        for s in range(4):
            add_up(out.at[s], [keep.at[s], other.at[s]])


def plane_kernel(pos, own, one, two, three, o0, o1, o2, o3):
    for s, out in enumerate((o0, o1, o2, o3)):
        add_up(out, [ref.at[s] for ref in (own, one, two, three)])


def route_kernel(pos, a0, a1, a2, a3, o0, o1, o2, o3, held):
    for q, ref in enumerate((a0, a1, a2, a3)):
        held[turn(pos[0], -q)] = ref[...]
    for p, out in enumerate((o0, o1, o2, o3)):
        out[...] = held[turn(pos[1], p)]


def states_kernel(pos, a0, a1, a2, a3, x, cot, stats, scale, out, *mods_out):
    centre, inverse = stats[0:1], stats[1:2]
    grad_mod, small = 0.0, 0.0
    for ref in (a0, a1, a2, a3):
        grad_mod = grad_mod + ref[:CHANNELS].astype(f32)
        small = small + unpacked(ref[CHANNELS:])
    normed = (x[...].astype(f32) - centre) * inverse
    grad_normed = grad_mod * (1.0 + scale[...])
    out[...] = cot[...].astype(f32) + inverse * (
        grad_normed - small[3:4] / D - normed * (small[4:5] / D)
    )
    for at, ref in enumerate(mods_out):
        ref[...] = small[at : at + 1, :CHANNELS] * token_scale


def clips_kernel(pos, own, other, out):
    out[...] = own[...].astype(f32) + other[...].astype(f32)


def on_device(states, cotangent, shift_mod, scale_mod, gate_mod, first_weight, second_weight):
    row, col = lax.axis_index("row"), lax.axis_index("col")
    high, x, core = col // INNER, lax.rem(col, INNER) // 2, lax.rem(col, 2)
    pos = jnp.stack([row, high, x, core]).astype(jnp.int32)
    weight_one, weight_two = first_weight.T, second_weight.T
    own_x, own_c = states[0].T, cotangent[0].T

    own = (CHANNELS, TOK)
    piece = (CHANNELS + EXTRA, TOK)
    units = (UNITS, TOK)
    wide_units = (UNITS + EXTRA, TOK)
    stage = pltpu.VMEM((INNER, CHANNELS, TOK), bf16)

    pair = (2 * CHANNELS, TOK)
    wide_pair = (2 * CHANNELS + EXTRA, TOK)
    plain = jnp.concatenate([own_x, own_c], 0)
    (with_mods,) = whole(pack_kernel, [shaped(wide_pair)])(
        pos, plain, jnp.concatenate([shift_mod, scale_mod, gate_mod], 0)
    )
    x_planes, c_planes = whole(
        sort_kernel,
        [shaped((4 * CHANNELS + EXTRA, TOK)), shaped((4 * CHANNELS, TOK))],
    )(pos, *[spread_rows(plain, s) for s in (1, 2, 3)], spread_rows(with_mods, 0))
    x_lines = [x_planes] + [along_x(x_planes, q) for q in (1, 2, 3)]
    (first_turned,) = whole(turned_kernel, [shaped((SLICE, UNITS))])(pos, weight_one)
    x_blocks = both_cores(pos, after(x_lines, first_turned))
    c_lines = [c_planes] + [along_x(c_planes, q) for q in (1, 2, 3)]

    mods_column, mods_row, through = whole(
        mods_kernel,
        [
            shaped((INNER, CHANNELS, 8), f32),
            shaped((8, SLICE), f32),
            shaped((8, TOK), f32),
        ],
    )(pos, *x_blocks, weight_one)

    pre_sums, offsets, means = [None] * 4, [None] * 4, [None] * 4
    blocks = x_blocks
    for shift in (1, 3, 2, 0):
        pre_sums[shift], offsets[shift], means[shift] = whole(
            functools.partial(first_kernel, shift),
            [shaped(wide_units), shaped((SLICE, TOK)), shaped((1, TOK), f32)],
            [stage],
            some,
        )(pos, *blocks, mods_column, through, weight_one)
        blocks = after(blocks, pre_sums[shift])
    pre_sums = to_rows(pre_sums)
    hidden, slope, rest, factor, stats = whole(
        hidden_kernel,
        [
            shaped(wide_units),
            shaped(units, f32),
            shaped(units, f32),
            shaped((UNITS, 1), f32),
            shaped((2, TOK), f32),
        ],
    )(pos, *pre_sums)
    c_blocks = both_cores(pos, after(c_lines, (pre_sums[1], pre_sums[0])))
    *grad_sums, cot = whole(
        second_kernel,
        [shaped(units)] * 4 + [shaped((SLICE, TOKENS))],
        [pltpu.VMEM((4, SLICE, TOK), bf16)],
    )(pos, *c_blocks, mods_column, weight_two)
    grad_sums = to_rows(grad_sums)
    (grad_pre,) = whole(grad_kernel, [shaped(wide_units)])(
        pos, *grad_sums, slope, rest, factor
    )
    hidden = all_rows(after(hidden, grad_pre))
    grad_pre = all_rows(grad_pre)

    weights = pl.BlockSpec((UNITS, CHUNK), lambda i, pos: (0, i))
    scratch = [pltpu.VMEM((UNITS, TOKENS), bf16)]

    weight_shapes = [shaped((UNITS, SLICE)), shaped((SLICE, 8), f32)]
    own_second, sums_second = whole(second_weight_kernel, weight_shapes, scratch)(
        pos, *after(hidden, grad_pre[2]), cot, mods_row, weight_two
    )
    other_second = swap_clips(own_second)
    own_first, sums_first = whole(
        first_weight_kernel, weight_shapes, scratch + [pltpu.VMEM((SLICE, TOKENS), bf16)]
    )(pos, *grad_pre, *hidden, *offsets, *means, mods_row, weight_one)
    other_first = swap_clips(own_first)

    quarter = (4,) + piece
    terms = whole(
        mod_kernel, [shaped(quarter)] * 8, scratch + [pltpu.VMEM((8, TOK), f32)]
    )(
        pos,
        *grad_pre,
        first_turned,
        sums_first.reshape(INNER, CHANNELS, 8),
        sums_second.reshape(INNER, CHANNELS, 8),
    )
    lines = whole(core_kernel, [shaped(quarter)] * 4)(
        pos, *terms[:4], *after([across(term) for term in terms[4:]], other_second)
    )
    def clips_call(own, other):
        return call(
            clips_kernel,
            (SLICE // CHUNK,),
            [weights, weights],
            weights,
            shaped((UNITS, SLICE), f32),
        )(pos, own, other)

    grad_second = clips_call(own_second, other_second)
    planes = whole(plane_kernel, [shaped(piece)] * 4)(
        pos, lines[0], *after([along_x(lines[p], p) for p in (1, 2, 3)], grad_second)
    )
    planes = to_rows(planes)
    pieces = whole(route_kernel, [shaped(piece)] * 4, [pltpu.VMEM((4,) + piece, bf16)])(
        pos, *planes
    )
    pieces = [pieces[0]] + [along_high(pieces[p], p) for p in (1, 2, 3)]

    grad_first = clips_call(own_first, other_first)
    grad_states, grad_shift, grad_scale, grad_gate = whole(
        states_kernel, [shaped(own, f32)] + [shaped((1, CHANNELS), f32)] * 3
    )(pos, *after(pieces, grad_first), own_x, own_c, stats, scale_mod.T)
    return (
        grad_states.T[None],
        grad_first.T,
        grad_second.T,
        grad_shift,
        grad_scale,
        grad_gate,
    )


def solution(mesh):
    return jax.shard_map(
        on_device,
        mesh=mesh,
        in_specs=(
            P("dp", "row", "col"),
            P("dp", "row", "col"),
            P("dp", "col"),
            P("dp", "col"),
            P("dp", "col"),
            P("row", "col"),
            P("row", "col"),
        ),
        out_specs=(
            P("dp", "row", "col"),
            P("row", "col"),
            P("row", "col"),
            P("dp", "col"),
            P("dp", "col"),
            P("dp", "col"),
        ),
        check_vma=False,
    )
```

```python
import functools
import math

import jax
import jax.numpy as jnp
from jax import lax
from jax.experimental import pallas as pl
from jax.experimental.pallas import tpu as pltpu
from jax.sharding import PartitionSpec as P

D = 5120
FF = 13824
ROWS = 4
COLS = 32
INNER = 8
CHANNELS = D // COLS
UNITS = FF // COLS
TOK = 256
SLICE = D // ROWS
TOKENS = ROWS * TOK
EXTRA = 16
CHUNK = 256

bf16, f32 = jnp.bfloat16, jnp.float32

eps = 1e-06
tanh_factor = 0.7978845608028654
cubic_term = 0.044715
token_scale = 1.0 / math.sqrt(ROWS * TOK)
weight_scale = 1.0 / math.sqrt(2 * ROWS * TOK)
across_tokens = (((1,), (1,)), ((), ()))


def gelu_pair(values):
    squares = values * values
    inner = jnp.tanh(tanh_factor * (values + cubic_term * squares * values))
    half = 0.5 * (1.0 + inner)
    slope = half + 0.5 * values * (1.0 - inner * inner) * tanh_factor * (
        1.0 + 3.0 * cubic_term * squares
    )
    return values * half, slope


def turn(value, offset):
    return lax.rem(value + offset + 8, 4)


def spread_rows(values, shift):
    pairs = [
        (a * COLS + b * INNER + i, b * COLS + ((a + shift) % 4) * INNER + i)
        for a in range(4)
        for b in range(4)
        for i in range(INNER)
    ]
    return lax.ppermute(values, ("row", "col"), pairs)


def along_high(values, shift):
    pairs = [(h * 8 + i, ((h + shift) % 4) * 8 + i) for h in range(4) for i in range(INNER)]
    return lax.ppermute(values, "col", pairs)


def along_x(values, shift):
    pairs = [
        (h * 8 + x * 2 + k, h * 8 + ((x + shift) % 4) * 2 + k)
        for h in range(4)
        for x in range(4)
        for k in range(2)
    ]
    return lax.ppermute(values, "col", pairs)


def across(values):
    return lax.ppermute(values, "col", [(c, c ^ 1) for c in range(COLS)])


def along_row(values, shift):
    return lax.ppermute(values, "row", [(a, (a + shift) % 4) for a in range(4)])


def all_rows(values):
    return [values] + [along_row(values, q) for q in (1, 2, 3)]


def to_rows(values):
    return [values[0]] + [along_row(values[q], q) for q in (1, 2, 3)]


def swap_clips(values):
    return lax.ppermute(values, "dp", [(0, 1), (1, 0)])


def both_cores(pos, lines):
    shape = shaped((2 * lines[0].shape[0], TOK))
    packs = whole(pair_kernel, [shape, shape])(pos, *lines)
    return list(lines) + [across(pack) for pack in packs]


def after(values, other):
    return lax.optimization_barrier((values, other))[0]


cheap = pl.CostEstimate(flops=1024, bytes_accessed=1024, transcendentals=0)
some = pl.CostEstimate(flops=1024, bytes_accessed=8000000, transcendentals=0)
limit = pltpu.CompilerParams(vmem_limit_bytes=16 * 1024 * 1024)


def call(kernel, grid, in_specs, out_specs, out_shape, scratch=()):
    return pl.pallas_call(
        kernel,
        grid_spec=pltpu.PrefetchScalarGridSpec(
            num_scalar_prefetch=1,
            grid=grid,
            in_specs=in_specs,
            out_specs=out_specs,
            scratch_shapes=list(scratch),
        ),
        out_shape=out_shape,
        compiler_params=limit,
        cost_estimate=cheap,
    )


def whole(kernel, out_shape, scratch=(), cost=cheap):
    vmem = pl.BlockSpec(memory_space=pltpu.VMEM)

    def run(pos, *args):
        return pl.pallas_call(
            kernel,
            in_specs=[pl.BlockSpec(memory_space=pltpu.SMEM)] + [vmem] * len(args),
            out_specs=[vmem] * len(out_shape),
            out_shape=out_shape,
            scratch_shapes=list(scratch),
            compiler_params=limit,
            cost_estimate=cost,
        )(pos, *args)

    return run


def full(shape):
    return pl.BlockSpec(shape, lambda i, pos: (0,) * len(shape))


def shaped(shape, kind=bf16):
    return jax.ShapeDtypeStruct(shape, kind)


def place_of(pos, token):
    return turn(pos[1] - token, -1)


def channel_block(pos, q, flip):
    core = pos[3] if flip == 0 else 1 - pos[3]
    return turn(pos[2], -q) * 2 + core


def parts_of(values, count):
    parts = []
    for _ in range(count):
        parts.append(values.astype(bf16).astype(f32))
        values = values - parts[-1]
    return parts


def packed(values):
    return jnp.concatenate(parts_of(values, 2), 0).astype(bf16)


def unpacked(rows):
    wide = rows.astype(f32)
    return wide[0:8] + wide[8:16]


def pack_kernel(pos, plain, mods, out):
    line = lax.broadcasted_iota(jnp.int32, (3, CHANNELS), 0)
    values = mods[...] + jnp.where(line == 1, 1.0, 0.0)
    rows = parts_of(values, 3) + [jnp.zeros((EXTRA - 9, CHANNELS), f32)]
    out[: 2 * CHANNELS] = plain[...]
    out[2 * CHANNELS :] = jnp.zeros((EXTRA, TOK), bf16)
    out[2 * CHANNELS :, :CHANNELS] = jnp.concatenate(rows, 0).astype(bf16)


def pair_kernel(pos, l0, l1, l2, l3, first, second):
    rows = l0.shape[0]
    first[:rows], first[rows:] = l0[...], l1[...]
    second[:rows], second[rows:] = l2[...], l3[...]


def block_of(blocks, q, flip, at, size):
    if flip == 0:
        return blocks[q][pl.ds(at, size), :]
    rows = blocks[0].shape[0]
    return blocks[4 + q // 2][pl.ds(at + (q % 2) * rows, size), :]


def sort_kernel(pos, b0, b1, b2, b3, x, cot):
    for at, ref in enumerate((b0, b1, b2, b3)):
        rows = slice(at * CHANNELS, (at + 1) * CHANNELS)
        x[rows] = ref[:CHANNELS]
        cot[rows] = ref[CHANNELS : 2 * CHANNELS]
    x[4 * CHANNELS :] = b3[2 * CHANNELS :]


def turned_kernel(pos, w1, out):
    out[...] = w1[...].T


def mods_kernel(pos, *refs):
    blocks, w1, mods_column, mods_row, through_out = refs[:6], refs[6], refs[7], refs[8], refs[9]
    for q in range(4):
        for flip in range(2):
            rows = block_of(blocks, q, flip, 4 * CHANNELS, EXTRA).astype(f32)
            values = jnp.concatenate([rows[0:3] + rows[3:6] + rows[6:9], rows[9:14]], 0)
            mods_column[channel_block(pos, q, flip)] = values.T[:CHANNELS]
    values = mods_column[...].reshape(SLICE, 8).T
    mods_row[...] = values
    rows = jnp.concatenate(parts_of(values, 3) + [jnp.zeros_like(values)], 0).astype(bf16)
    through = lax.dot_general(rows, w1[...], across_tokens, preferred_element_type=f32)
    through = through[0:8] + through[8:16] + through[16:24]
    through_out[...] = jnp.zeros((8, TOK), f32)
    for at, line in ((0, through[1:2]), (2, through[0:1])):
        through_out[at : at + 1] = line[:, :TOK]
        through_out[at + 1 : at + 2, : UNITS - TOK] = line[:, TOK:]


def first_kernel(shift, pos, *refs):
    blocks, mods, through, w1 = refs[:6], refs[6], refs[7], refs[8]
    out, offset_out, mean_out, offsets = refs[9:]
    place = place_of(pos, turn(pos[0], shift))
    at = pl.multiple_of(place * CHANNELS, 32)
    total = 0.0
    for q in range(4):
        for flip in range(2):
            block = block_of(blocks, q, flip, at, CHANNELS).astype(f32)
            total = total + jnp.sum(block, 0, keepdims=True)
    mean = total / SLICE
    square = 0.0
    for q in range(4):
        for flip in range(2):
            j = channel_block(pos, q, flip)
            offset = block_of(blocks, q, flip, at, CHANNELS).astype(f32) - mean
            square = square + jnp.sum(offset * offset, 0, keepdims=True)
            offsets[j] = (offset * mods[j][:, 1:2]).astype(bf16)
            rows = pl.ds(pl.multiple_of(j * CHANNELS, 32), CHANNELS)
            offset_out[rows, :] = offset.astype(bf16)
    mean_out[...] = mean
    out[:UNITS] = jnp.dot(
        w1[...], offsets[...].reshape(SLICE, TOK), preferred_element_type=f32
    ).astype(bf16)
    four = jnp.concatenate([mean, square, through[0:2]], 0)
    extra = parts_of(four, 3) + parts_of(through[2:4], 2)
    out[UNITS:] = jnp.concatenate(extra, 0).astype(bf16)


def hidden_kernel(pos, p0, p1, p2, p3, hidden_out, slope_out, rest_out, factor_out, stats_out):
    parts = (p0, p1, p2, p3)
    extras = [ref[UNITS:].astype(f32) for ref in parts]
    fours = [e[0:4] + e[4:8] + e[8:12] for e in extras]
    shifts = sum(e[12:14] + e[14:16] for e in extras)
    centre = 0.25 * (fours[0][0:1] + fours[1][0:1] + fours[2][0:1] + fours[3][0:1])
    spread = 0.0
    for four in fours:
        spread = spread + four[1:2] + SLICE * (four[0:1] - centre) ** 2
    inverse = lax.rsqrt(spread / D + eps)
    stats = jnp.concatenate([centre, inverse], 0)
    stats_out[...] = stats
    hidden_out[UNITS:] = jnp.concatenate(
        parts_of(stats, 3) + [jnp.zeros((EXTRA - 6, TOK), f32)], 0
    ).astype(bf16)
    columns = jnp.concatenate([four[2:4] for four in fours] + [shifts] * 4, 0).T
    for half, at in ((0, slice(0, TOK)), (1, slice(TOK, UNITS))):
        size = at.stop - at.start
        rest, total = 0.0, 0.0
        for i, ref in enumerate(parts):
            factor = columns[:size, 2 * i + half : 2 * i + half + 1]
            total = total + factor
            rest = rest + (ref[at].astype(f32) + factor * (fours[i][0:1] - centre))
        rest = rest * inverse
        hidden, slope = gelu_pair(rest + columns[:size, 8 + half : 9 + half])
        hidden_out[at] = hidden.astype(bf16)
        slope_out[at] = slope
        rest_out[at] = rest
        factor_out[at] = total


def second_kernel(pos, *refs):
    blocks, mods, w2 = refs[:6], refs[6], refs[7]
    sums, cot_out, scaled = refs[8:12], refs[12], refs[13]
    for shift, out in enumerate(sums):
        token = turn(pos[0], shift)
        at = pl.multiple_of(place_of(pos, token) * CHANNELS, 32)
        lanes = pl.ds(pl.multiple_of(token * TOK, TOK), TOK)
        for q in range(4):
            for flip in range(2):
                j = channel_block(pos, q, flip)
                block = block_of(blocks, q, flip, at, CHANNELS)
                rows = pl.ds(pl.multiple_of(j * CHANNELS, 32), CHANNELS)
                cot_out[rows, lanes] = block
                scaled[shift, rows, :] = (block.astype(f32) * mods[j][:, 2:3]).astype(bf16)
        out[...] = jnp.dot(w2[...], scaled[shift], preferred_element_type=f32).astype(bf16)


def grad_kernel(pos, own, one, two, three, slope, rest, factor, out):
    grad = own[...].astype(f32) + one[...].astype(f32)
    grad = grad + (two[...].astype(f32) + three[...].astype(f32))
    grad = (grad * slope[...]).astype(bf16)
    out[:UNITS] = grad
    wide = grad.astype(f32)
    first = jnp.sum(wide * factor[...], 0, keepdims=True)
    second = jnp.sum(wide * rest[...], 0, keepdims=True)
    line = lax.broadcasted_iota(jnp.int32, (8, TOK), 0)
    out[UNITS:] = packed(jnp.where(line == 3, first, jnp.where(line == 4, second, 0.0)))


def collect(pos, refs, store):
    for q, ref in enumerate(refs):
        at = pl.multiple_of(turn(pos[0], -q) * TOK, TOK)
        store[:, pl.ds(at, TOK)] = ref[:UNITS]


def second_weight_kernel(pos, b0, b1, b2, b3, cot, mods, w2, send, sums, store):
    collect(pos, (b0, b1, b2, b3), store)
    line = lax.broadcasted_iota(jnp.int32, (8, CHUNK), 0)
    for at in range(0, SLICE, CHUNK):
        part = slice(at, at + CHUNK)
        raw = lax.dot_general(
            store[...], cot[part, :], across_tokens, preferred_element_type=f32
        )
        total = jnp.sum(w2[:, part].astype(f32) * raw, 0, keepdims=True)
        sums[part, :] = jnp.where(line == 2, total, 0.0).T
        send[:, part] = (raw * (mods[2:3, part] * weight_scale)).astype(bf16)


def first_weight_kernel(pos, *refs):
    grads, hiddens, offsets, means = refs[:4], refs[4:8], refs[8:12], refs[12:16]
    mods, w1, send, sums, store, others = refs[16:]
    total, lift = 0.0, 0.0
    for q in range(4):
        at = (4 - q) % 4
        extra = hiddens[q][UNITS:].astype(f32)
        stats = extra[0:2] + extra[2:4] + extra[4:6]
        grad = grads[q][:UNITS].astype(f32)
        total = total + jnp.sum(grad, 1, keepdims=True)
        grad = grad * stats[1:2]
        lift = lift + jnp.sum(grad * (means[at][...] - stats[0:1]), 1, keepdims=True)
        lanes = slice(at * TOK, (at + 1) * TOK)
        store[:, lanes] = grad.astype(bf16)
        others[:, lanes] = offsets[at][...]
    line = lax.broadcasted_iota(jnp.int32, (8, CHUNK), 0)
    for at in range(0, SLICE, CHUNK):
        part = slice(at, at + CHUNK)
        raw = lift + lax.dot_general(
            store[...], others[part, :], across_tokens, preferred_element_type=f32
        )
        weight = w1[:, part].astype(f32)
        shift = jnp.sum(weight * total, 0, keepdims=True)
        scale = jnp.sum(weight * raw, 0, keepdims=True)
        sums[part, :] = jnp.where(line == 0, shift, jnp.where(line == 1, scale, 0.0)).T
        grad = (raw * mods[1:2, part] + total * mods[0:1, part]) * weight_scale
        send[:, part] = grad.astype(bf16)


def mod_kernel(pos, g0, g1, g2, g3, w1, sums_one, sums_two, *rest):
    keeps, sends, store, line = rest[:4], rest[4:8], rest[8], rest[9]
    grads = (g0, g1, g2, g3)
    collect(pos, grads, store)
    line[...] = jnp.zeros((8, TOK), f32)
    smalls = [unpacked(ref[UNITS:]) for ref in grads]
    for core, outs in ((pos[3], keeps), (1 - pos[3], sends)):
        for p, out in enumerate(outs):
            j = turn(pos[2], p) * 2 + core
            rows = pl.ds(pl.multiple_of(j * CHANNELS, 32), CHANNELS)
            product = jnp.dot(w1[rows, :], store[...], preferred_element_type=f32).astype(bf16)
            for token in range(4):
                out[turn(token, -pos[0]), :CHANNELS] = product[
                    :, token * TOK : (token + 1) * TOK
                ]
            line[:, :CHANNELS] = (sums_one[j] + sums_two[j]).T
            for q, small in enumerate(smalls):
                out[(4 - q) % 4, CHANNELS:] = packed(small + line[...])


def add_up(out, parts):
    total = parts[0][:CHANNELS].astype(f32)
    small = unpacked(parts[0][CHANNELS:])
    for part in parts[1:]:
        total = total + part[:CHANNELS].astype(f32)
        small = small + unpacked(part[CHANNELS:])
    out[:CHANNELS] = total.astype(bf16)
    out[CHANNELS:] = packed(small)


def core_kernel(pos, *refs):
    for keep, other, out in zip(refs[:4], refs[4:8], refs[8:]):
        for s in range(4):
            add_up(out.at[s], [keep.at[s], other.at[s]])


def plane_kernel(pos, own, one, two, three, o0, o1, o2, o3):
    for s, out in enumerate((o0, o1, o2, o3)):
        add_up(out, [ref.at[s] for ref in (own, one, two, three)])


def route_kernel(pos, a0, a1, a2, a3, o0, o1, o2, o3, held):
    for q, ref in enumerate((a0, a1, a2, a3)):
        held[turn(pos[0], -q)] = ref[...]
    for p, out in enumerate((o0, o1, o2, o3)):
        out[...] = held[turn(pos[1], p)]


def states_kernel(pos, a0, a1, a2, a3, x, cot, stats, scale, out, *mods_out):
    centre, inverse = stats[0:1], stats[1:2]
    grad_mod, small = 0.0, 0.0
    for ref in (a0, a1, a2, a3):
        grad_mod = grad_mod + ref[:CHANNELS].astype(f32)
        small = small + unpacked(ref[CHANNELS:])
    normed = (x[...].astype(f32) - centre) * inverse
    grad_normed = grad_mod * (1.0 + scale[...])
    out[...] = cot[...].astype(f32) + inverse * (
        grad_normed - small[3:4] / D - normed * (small[4:5] / D)
    )
    for at, ref in enumerate(mods_out):
        ref[...] = small[at : at + 1, :CHANNELS] * token_scale


def clips_kernel(pos, own, other, out):
    out[...] = own[...].astype(f32) + other[...].astype(f32)


def on_device(states, cotangent, shift_mod, scale_mod, gate_mod, first_weight, second_weight):
    row, col = lax.axis_index("row"), lax.axis_index("col")
    high, x, core = col // INNER, lax.rem(col, INNER) // 2, lax.rem(col, 2)
    pos = jnp.stack([row, high, x, core]).astype(jnp.int32)
    weight_one, weight_two = first_weight.T, second_weight.T
    own_x, own_c = states[0].T, cotangent[0].T

    own = (CHANNELS, TOK)
    piece = (CHANNELS + EXTRA, TOK)
    units = (UNITS, TOK)
    wide_units = (UNITS + EXTRA, TOK)
    stage = pltpu.VMEM((INNER, CHANNELS, TOK), bf16)

    pair = (2 * CHANNELS, TOK)
    wide_pair = (2 * CHANNELS + EXTRA, TOK)
    plain = jnp.concatenate([own_x, own_c], 0)
    (with_mods,) = whole(pack_kernel, [shaped(wide_pair)])(
        pos, plain, jnp.concatenate([shift_mod, scale_mod, gate_mod], 0)
    )
    x_planes, c_planes = whole(
        sort_kernel,
        [shaped((4 * CHANNELS + EXTRA, TOK)), shaped((4 * CHANNELS, TOK))],
    )(pos, *[spread_rows(plain, s) for s in (1, 2, 3)], spread_rows(with_mods, 0))
    x_lines = [x_planes] + [along_x(x_planes, q) for q in (1, 2, 3)]
    (first_turned,) = whole(turned_kernel, [shaped((SLICE, UNITS))])(pos, weight_one)
    x_blocks = both_cores(pos, after(x_lines, first_turned))
    c_lines = [c_planes] + [along_x(c_planes, q) for q in (1, 2, 3)]

    mods_column, mods_row, through = whole(
        mods_kernel,
        [
            shaped((INNER, CHANNELS, 8), f32),
            shaped((8, SLICE), f32),
            shaped((8, TOK), f32),
        ],
    )(pos, *x_blocks, weight_one)

    pre_sums, offsets, means = [None] * 4, [None] * 4, [None] * 4
    blocks = x_blocks
    for shift in (1, 3, 2, 0):
        pre_sums[shift], offsets[shift], means[shift] = whole(
            functools.partial(first_kernel, shift),
            [shaped(wide_units), shaped((SLICE, TOK)), shaped((1, TOK), f32)],
            [stage],
            some,
        )(pos, *blocks, mods_column, through, weight_one)
        blocks = after(blocks, pre_sums[shift])
    pre_sums = to_rows(pre_sums)
    hidden, slope, rest, factor, stats = whole(
        hidden_kernel,
        [
            shaped(wide_units),
            shaped(units, f32),
            shaped(units, f32),
            shaped((UNITS, 1), f32),
            shaped((2, TOK), f32),
        ],
    )(pos, *pre_sums)
    c_blocks = both_cores(pos, after(c_lines, pre_sums))
    *grad_sums, cot = whole(
        second_kernel,
        [shaped(units)] * 4 + [shaped((SLICE, TOKENS))],
        [pltpu.VMEM((4, SLICE, TOK), bf16)],
    )(pos, *c_blocks, mods_column, weight_two)
    hidden = all_rows(hidden)

    weights = pl.BlockSpec((UNITS, CHUNK), lambda i, pos: (0, i))
    scratch = [pltpu.VMEM((UNITS, TOKENS), bf16)]

    weight_shapes = [shaped((UNITS, SLICE)), shaped((SLICE, 8), f32)]
    own_second, sums_second = whole(second_weight_kernel, weight_shapes, scratch)(
        pos, *hidden, cot, mods_row, weight_two
    )
    other_second = swap_clips(own_second)
    grad_sums = to_rows(after(grad_sums, hidden[2]))
    (grad_pre,) = whole(grad_kernel, [shaped(wide_units)])(
        pos, *grad_sums, slope, rest, factor
    )
    grad_pre = all_rows(grad_pre)
    own_first, sums_first = whole(
        first_weight_kernel, weight_shapes, scratch + [pltpu.VMEM((SLICE, TOKENS), bf16)]
    )(pos, *grad_pre, *hidden, *offsets, *means, mods_row, weight_one)
    other_first = swap_clips(own_first)

    quarter = (4,) + piece
    terms = whole(
        mod_kernel, [shaped(quarter)] * 8, scratch + [pltpu.VMEM((8, TOK), f32)]
    )(
        pos,
        *grad_pre,
        first_turned,
        sums_first.reshape(INNER, CHANNELS, 8),
        sums_second.reshape(INNER, CHANNELS, 8),
    )
    lines = whole(core_kernel, [shaped(quarter)] * 4)(
        pos, *terms[:4], *after([across(term) for term in terms[4:]], other_second)
    )
    def clips_call(own, other):
        return call(
            clips_kernel,
            (SLICE // CHUNK,),
            [weights, weights],
            weights,
            shaped((UNITS, SLICE), f32),
        )(pos, own, other)

    grad_second = clips_call(own_second, other_second)
    planes = whole(plane_kernel, [shaped(piece)] * 4)(
        pos, lines[0], *after([along_x(lines[p], p) for p in (1, 2, 3)], grad_second)
    )
    planes = to_rows(planes)
    pieces = whole(route_kernel, [shaped(piece)] * 4, [pltpu.VMEM((4,) + piece, bf16)])(
        pos, *planes
    )
    pieces = [pieces[0]] + [along_high(pieces[p], p) for p in (1, 2, 3)]

    grad_first = clips_call(own_first, other_first)
    grad_states, grad_shift, grad_scale, grad_gate = whole(
        states_kernel, [shaped(own, f32)] + [shaped((1, CHANNELS), f32)] * 3
    )(pos, *after(pieces, grad_first), own_x, own_c, stats, scale_mod.T)
    return (
        grad_states.T[None],
        grad_first.T,
        grad_second.T,
        grad_shift,
        grad_scale,
        grad_gate,
    )


def solution(mesh):
    return jax.shard_map(
        on_device,
        mesh=mesh,
        in_specs=(
            P("dp", "row", "col"),
            P("dp", "row", "col"),
            P("dp", "col"),
            P("dp", "col"),
            P("dp", "col"),
            P("row", "col"),
            P("row", "col"),
        ),
        out_specs=(
            P("dp", "row", "col"),
            P("row", "col"),
            P("row", "col"),
            P("dp", "col"),
            P("dp", "col"),
            P("dp", "col"),
        ),
        check_vma=False,
    )
```

```python
import functools
import math

import jax
import jax.numpy as jnp
from jax import lax
from jax.experimental import pallas as pl
from jax.experimental.pallas import tpu as pltpu
from jax.sharding import PartitionSpec as P

D = 5120
FF = 13824
ROWS = 4
COLS = 32
INNER = 8
CHANNELS = D // COLS
UNITS = FF // COLS
TOK = 256
SLICE = D // ROWS
TOKENS = ROWS * TOK
EXTRA = 16
CHUNK = 256

bf16, f32 = jnp.bfloat16, jnp.float32

eps = 1e-06
tanh_factor = 0.7978845608028654
cubic_term = 0.044715
token_scale = 1.0 / math.sqrt(ROWS * TOK)
weight_scale = 1.0 / math.sqrt(2 * ROWS * TOK)
across_tokens = (((1,), (1,)), ((), ()))


def gelu_pair(values):
    squares = values * values
    inner = jnp.tanh(tanh_factor * (values + cubic_term * squares * values))
    half = 0.5 * (1.0 + inner)
    slope = half + 0.5 * values * (1.0 - inner * inner) * tanh_factor * (
        1.0 + 3.0 * cubic_term * squares
    )
    return values * half, slope


def turn(value, offset):
    return lax.rem(value + offset + 8, 4)


def spread_rows(values, shift):
    pairs = [
        (a * COLS + b * INNER + i, b * COLS + ((a + shift) % 4) * INNER + i)
        for a in range(4)
        for b in range(4)
        for i in range(INNER)
    ]
    return lax.ppermute(values, ("row", "col"), pairs)


def along_high(values, shift):
    pairs = [(h * 8 + i, ((h + shift) % 4) * 8 + i) for h in range(4) for i in range(INNER)]
    return lax.ppermute(values, "col", pairs)


def along_x(values, shift):
    pairs = [
        (h * 8 + x * 2 + k, h * 8 + ((x + shift) % 4) * 2 + k)
        for h in range(4)
        for x in range(4)
        for k in range(2)
    ]
    return lax.ppermute(values, "col", pairs)


def across(values):
    return lax.ppermute(values, "col", [(c, c ^ 1) for c in range(COLS)])


def along_row(values, shift):
    return lax.ppermute(values, "row", [(a, (a + shift) % 4) for a in range(4)])


def all_rows(values):
    return [values] + [along_row(values, q) for q in (1, 2, 3)]


def to_rows(values):
    return [values[0]] + [along_row(values[q], q) for q in (1, 2, 3)]


def swap_clips(values):
    return lax.ppermute(values, "dp", [(0, 1), (1, 0)])


def both_cores(pos, lines):
    shape = shaped((2 * lines[0].shape[0], TOK))
    packs = whole(pair_kernel, [shape, shape])(pos, *lines)
    return list(lines) + [across(pack) for pack in packs]


def after(values, other):
    return lax.optimization_barrier((values, other))[0]


cheap = pl.CostEstimate(flops=1024, bytes_accessed=1024, transcendentals=0)
some = pl.CostEstimate(flops=1024, bytes_accessed=8000000, transcendentals=0)
limit = pltpu.CompilerParams(vmem_limit_bytes=16 * 1024 * 1024)


def call(kernel, grid, in_specs, out_specs, out_shape, scratch=()):
    return pl.pallas_call(
        kernel,
        grid_spec=pltpu.PrefetchScalarGridSpec(
            num_scalar_prefetch=1,
            grid=grid,
            in_specs=in_specs,
            out_specs=out_specs,
            scratch_shapes=list(scratch),
        ),
        out_shape=out_shape,
        compiler_params=limit,
        cost_estimate=cheap,
    )


def whole(kernel, out_shape, scratch=(), cost=cheap):
    vmem = pl.BlockSpec(memory_space=pltpu.VMEM)

    def run(pos, *args):
        return pl.pallas_call(
            kernel,
            in_specs=[pl.BlockSpec(memory_space=pltpu.SMEM)] + [vmem] * len(args),
            out_specs=[vmem] * len(out_shape),
            out_shape=out_shape,
            scratch_shapes=list(scratch),
            compiler_params=limit,
            cost_estimate=cost,
        )(pos, *args)

    return run


def full(shape):
    return pl.BlockSpec(shape, lambda i, pos: (0,) * len(shape))


def shaped(shape, kind=bf16):
    return jax.ShapeDtypeStruct(shape, kind)


def place_of(pos, token):
    return turn(pos[1] - token, -1)


def channel_block(pos, q, flip):
    core = pos[3] if flip == 0 else 1 - pos[3]
    return turn(pos[2], -q) * 2 + core


def parts_of(values, count):
    parts = []
    for _ in range(count):
        parts.append(values.astype(bf16).astype(f32))
        values = values - parts[-1]
    return parts


def packed(values):
    return jnp.concatenate(parts_of(values, 2), 0).astype(bf16)


def unpacked(rows):
    wide = rows.astype(f32)
    return wide[0:8] + wide[8:16]


def pack_kernel(pos, plain, mods, out):
    line = lax.broadcasted_iota(jnp.int32, (3, CHANNELS), 0)
    values = mods[...] + jnp.where(line == 1, 1.0, 0.0)
    rows = parts_of(values, 3) + [jnp.zeros((EXTRA - 9, CHANNELS), f32)]
    out[: 2 * CHANNELS] = plain[...]
    out[2 * CHANNELS :] = jnp.zeros((EXTRA, TOK), bf16)
    out[2 * CHANNELS :, :CHANNELS] = jnp.concatenate(rows, 0).astype(bf16)


def pair_kernel(pos, l0, l1, l2, l3, first, second):
    rows = l0.shape[0]
    first[:rows], first[rows:] = l0[...], l1[...]
    second[:rows], second[rows:] = l2[...], l3[...]


def block_of(blocks, q, flip, at, size):
    if flip == 0:
        return blocks[q][pl.ds(at, size), :]
    rows = blocks[0].shape[0]
    return blocks[4 + q // 2][pl.ds(at + (q % 2) * rows, size), :]


def sort_kernel(pos, b0, b1, b2, b3, x, cot):
    for at, ref in enumerate((b0, b1, b2, b3)):
        rows = slice(at * CHANNELS, (at + 1) * CHANNELS)
        x[rows] = ref[:CHANNELS]
        cot[rows] = ref[CHANNELS : 2 * CHANNELS]
    x[4 * CHANNELS :] = b3[2 * CHANNELS :]


def turned_kernel(pos, w1, out):
    out[...] = w1[...].T


def mods_kernel(pos, *refs):
    blocks, w1, mods_column, mods_row, through_out = refs[:6], refs[6], refs[7], refs[8], refs[9]
    for q in range(4):
        for flip in range(2):
            rows = block_of(blocks, q, flip, 4 * CHANNELS, EXTRA).astype(f32)
            values = jnp.concatenate([rows[0:3] + rows[3:6] + rows[6:9], rows[9:14]], 0)
            mods_column[channel_block(pos, q, flip)] = values.T[:CHANNELS]
    values = mods_column[...].reshape(SLICE, 8).T
    mods_row[...] = values
    rows = jnp.concatenate(parts_of(values, 3) + [jnp.zeros_like(values)], 0).astype(bf16)
    through = lax.dot_general(rows, w1[...], across_tokens, preferred_element_type=f32)
    through = through[0:8] + through[8:16] + through[16:24]
    through_out[...] = jnp.zeros((8, TOK), f32)
    for at, line in ((0, through[1:2]), (2, through[0:1])):
        through_out[at : at + 1] = line[:, :TOK]
        through_out[at + 1 : at + 2, : UNITS - TOK] = line[:, TOK:]


def first_kernel(shift, pos, *refs):
    blocks, mods, through, w1 = refs[:6], refs[6], refs[7], refs[8]
    out, offset_out, mean_out, offsets = refs[9:]
    place = place_of(pos, turn(pos[0], shift))
    at = pl.multiple_of(place * CHANNELS, 32)
    total = 0.0
    for q in range(4):
        for flip in range(2):
            block = block_of(blocks, q, flip, at, CHANNELS).astype(f32)
            total = total + jnp.sum(block, 0, keepdims=True)
    mean = total / SLICE
    square = 0.0
    for q in range(4):
        for flip in range(2):
            j = channel_block(pos, q, flip)
            offset = block_of(blocks, q, flip, at, CHANNELS).astype(f32) - mean
            square = square + jnp.sum(offset * offset, 0, keepdims=True)
            offsets[j] = (offset * mods[j][:, 1:2]).astype(bf16)
            rows = pl.ds(pl.multiple_of(j * CHANNELS, 32), CHANNELS)
            offset_out[rows, :] = offset.astype(bf16)
    mean_out[...] = mean
    out[:UNITS] = jnp.dot(
        w1[...], offsets[...].reshape(SLICE, TOK), preferred_element_type=f32
    ).astype(bf16)
    four = jnp.concatenate([mean, square, through[0:2]], 0)
    extra = parts_of(four, 3) + parts_of(through[2:4], 2)
    out[UNITS:] = jnp.concatenate(extra, 0).astype(bf16)


def hidden_kernel(pos, p0, p1, p2, p3, hidden_out, slope_out, rest_out, factor_out, stats_out):
    parts = (p0, p1, p2, p3)
    extras = [ref[UNITS:].astype(f32) for ref in parts]
    fours = [e[0:4] + e[4:8] + e[8:12] for e in extras]
    shifts = sum(e[12:14] + e[14:16] for e in extras)
    centre = 0.25 * (fours[0][0:1] + fours[1][0:1] + fours[2][0:1] + fours[3][0:1])
    spread = 0.0
    for four in fours:
        spread = spread + four[1:2] + SLICE * (four[0:1] - centre) ** 2
    inverse = lax.rsqrt(spread / D + eps)
    stats = jnp.concatenate([centre, inverse], 0)
    stats_out[...] = stats
    hidden_out[UNITS:] = jnp.concatenate(
        parts_of(stats, 3) + [jnp.zeros((EXTRA - 6, TOK), f32)], 0
    ).astype(bf16)
    columns = jnp.concatenate([four[2:4] for four in fours] + [shifts] * 4, 0).T
    for half, at in ((0, slice(0, TOK)), (1, slice(TOK, UNITS))):
        size = at.stop - at.start
        rest, total = 0.0, 0.0
        for i, ref in enumerate(parts):
            factor = columns[:size, 2 * i + half : 2 * i + half + 1]
            total = total + factor
            rest = rest + (ref[at].astype(f32) + factor * (fours[i][0:1] - centre))
        rest = rest * inverse
        hidden, slope = gelu_pair(rest + columns[:size, 8 + half : 9 + half])
        hidden_out[at] = hidden.astype(bf16)
        slope_out[at] = slope
        rest_out[at] = rest
        factor_out[at] = total


def second_kernel(pos, *refs):
    blocks, mods, w2 = refs[:6], refs[6], refs[7]
    sums, cot_out, scaled = refs[8:12], refs[12], refs[13]
    for shift, out in enumerate(sums):
        token = turn(pos[0], shift)
        at = pl.multiple_of(place_of(pos, token) * CHANNELS, 32)
        lanes = pl.ds(pl.multiple_of(token * TOK, TOK), TOK)
        for q in range(4):
            for flip in range(2):
                j = channel_block(pos, q, flip)
                block = block_of(blocks, q, flip, at, CHANNELS)
                rows = pl.ds(pl.multiple_of(j * CHANNELS, 32), CHANNELS)
                cot_out[rows, lanes] = block
                scaled[shift, rows, :] = (block.astype(f32) * mods[j][:, 2:3]).astype(bf16)
        out[...] = jnp.dot(w2[...], scaled[shift], preferred_element_type=f32).astype(bf16)


def grad_kernel(pos, own, one, two, three, slope, rest, factor, out):
    grad = own[...].astype(f32) + one[...].astype(f32)
    grad = grad + (two[...].astype(f32) + three[...].astype(f32))
    grad = (grad * slope[...]).astype(bf16)
    out[:UNITS] = grad
    wide = grad.astype(f32)
    first = jnp.sum(wide * factor[...], 0, keepdims=True)
    second = jnp.sum(wide * rest[...], 0, keepdims=True)
    line = lax.broadcasted_iota(jnp.int32, (8, TOK), 0)
    out[UNITS:] = packed(jnp.where(line == 3, first, jnp.where(line == 4, second, 0.0)))


def collect(pos, refs, store):
    for q, ref in enumerate(refs):
        at = pl.multiple_of(turn(pos[0], -q) * TOK, TOK)
        store[:, pl.ds(at, TOK)] = ref[:UNITS]


def second_weight_kernel(pos, b0, b1, b2, b3, cot, mods, w2, send, sums, store):
    collect(pos, (b0, b1, b2, b3), store)
    line = lax.broadcasted_iota(jnp.int32, (8, CHUNK), 0)
    for at in range(0, SLICE, CHUNK):
        part = slice(at, at + CHUNK)
        raw = lax.dot_general(
            store[...], cot[part, :], across_tokens, preferred_element_type=f32
        )
        total = jnp.sum(w2[:, part].astype(f32) * raw, 0, keepdims=True)
        sums[part, :] = jnp.where(line == 2, total, 0.0).T
        send[:, part] = (raw * (mods[2:3, part] * weight_scale)).astype(bf16)


def first_weight_kernel(pos, *refs):
    grads, hiddens, offsets, means = refs[:4], refs[4:8], refs[8:12], refs[12:16]
    mods, w1, send, sums, store, others = refs[16:]
    total, lift = 0.0, 0.0
    for q in range(4):
        at = (4 - q) % 4
        extra = hiddens[q][UNITS:].astype(f32)
        stats = extra[0:2] + extra[2:4] + extra[4:6]
        grad = grads[q][:UNITS].astype(f32)
        total = total + jnp.sum(grad, 1, keepdims=True)
        grad = grad * stats[1:2]
        lift = lift + jnp.sum(grad * (means[at][...] - stats[0:1]), 1, keepdims=True)
        lanes = slice(at * TOK, (at + 1) * TOK)
        store[:, lanes] = grad.astype(bf16)
        others[:, lanes] = offsets[at][...]
    line = lax.broadcasted_iota(jnp.int32, (8, CHUNK), 0)
    for at in range(0, SLICE, CHUNK):
        part = slice(at, at + CHUNK)
        raw = lift + lax.dot_general(
            store[...], others[part, :], across_tokens, preferred_element_type=f32
        )
        weight = w1[:, part].astype(f32)
        shift = jnp.sum(weight * total, 0, keepdims=True)
        scale = jnp.sum(weight * raw, 0, keepdims=True)
        sums[part, :] = jnp.where(line == 0, shift, jnp.where(line == 1, scale, 0.0)).T
        grad = (raw * mods[1:2, part] + total * mods[0:1, part]) * weight_scale
        send[:, part] = grad.astype(bf16)


def mod_kernel(pos, g0, g1, g2, g3, w1, sums_one, sums_two, *rest):
    keeps, sends, store, line = rest[:4], rest[4:8], rest[8], rest[9]
    grads = (g0, g1, g2, g3)
    collect(pos, grads, store)
    line[...] = jnp.zeros((8, TOK), f32)
    smalls = [unpacked(ref[UNITS:]) for ref in grads]
    for core, outs in ((pos[3], keeps), (1 - pos[3], sends)):
        for p, out in enumerate(outs):
            j = turn(pos[2], p) * 2 + core
            rows = pl.ds(pl.multiple_of(j * CHANNELS, 32), CHANNELS)
            product = jnp.dot(w1[rows, :], store[...], preferred_element_type=f32).astype(bf16)
            for token in range(4):
                out[turn(token, -pos[0]), :CHANNELS] = product[
                    :, token * TOK : (token + 1) * TOK
                ]
            line[:, :CHANNELS] = (sums_one[j] + sums_two[j]).T
            for q, small in enumerate(smalls):
                out[(4 - q) % 4, CHANNELS:] = packed(small + line[...])


def add_up(out, parts):
    total = parts[0][:CHANNELS].astype(f32)
    small = unpacked(parts[0][CHANNELS:])
    for part in parts[1:]:
        total = total + part[:CHANNELS].astype(f32)
        small = small + unpacked(part[CHANNELS:])
    out[:CHANNELS] = total.astype(bf16)
    out[CHANNELS:] = packed(small)


def core_kernel(pos, *refs):
    for keep, other, out in zip(refs[:4], refs[4:8], refs[8:]):
        for s in range(4):
            add_up(out.at[s], [keep.at[s], other.at[s]])


def plane_kernel(pos, own, one, two, three, o0, o1, o2, o3):
    for s, out in enumerate((o0, o1, o2, o3)):
        add_up(out, [ref.at[s] for ref in (own, one, two, three)])


def route_kernel(pos, a0, a1, a2, a3, o0, o1, o2, o3, held):
    for q, ref in enumerate((a0, a1, a2, a3)):
        held[turn(pos[0], -q)] = ref[...]
    for p, out in enumerate((o0, o1, o2, o3)):
        out[...] = held[turn(pos[1], p)]


def states_kernel(pos, a0, a1, a2, a3, x, cot, stats, scale, out, *mods_out):
    centre, inverse = stats[0:1], stats[1:2]
    grad_mod, small = 0.0, 0.0
    for ref in (a0, a1, a2, a3):
        grad_mod = grad_mod + ref[:CHANNELS].astype(f32)
        small = small + unpacked(ref[CHANNELS:])
    normed = (x[...].astype(f32) - centre) * inverse
    grad_normed = grad_mod * (1.0 + scale[...])
    out[...] = cot[...].astype(f32) + inverse * (
        grad_normed - small[3:4] / D - normed * (small[4:5] / D)
    )
    for at, ref in enumerate(mods_out):
        ref[...] = small[at : at + 1, :CHANNELS] * token_scale


def clips_kernel(pos, own, other, out):
    out[...] = own[...].astype(f32) + other[...].astype(f32)


def on_device(states, cotangent, shift_mod, scale_mod, gate_mod, first_weight, second_weight):
    row, col = lax.axis_index("row"), lax.axis_index("col")
    high, x, core = col // INNER, lax.rem(col, INNER) // 2, lax.rem(col, 2)
    pos = jnp.stack([row, high, x, core]).astype(jnp.int32)
    weight_one, weight_two = first_weight.T, second_weight.T
    own_x, own_c = states[0].T, cotangent[0].T

    own = (CHANNELS, TOK)
    piece = (CHANNELS + EXTRA, TOK)
    units = (UNITS, TOK)
    wide_units = (UNITS + EXTRA, TOK)
    stage = pltpu.VMEM((INNER, CHANNELS, TOK), bf16)

    pair = (2 * CHANNELS, TOK)
    wide_pair = (2 * CHANNELS + EXTRA, TOK)
    plain = jnp.concatenate([own_x, own_c], 0)
    (with_mods,) = whole(pack_kernel, [shaped(wide_pair)])(
        pos, plain, jnp.concatenate([shift_mod, scale_mod, gate_mod], 0)
    )
    x_planes, c_planes = whole(
        sort_kernel,
        [shaped((4 * CHANNELS + EXTRA, TOK)), shaped((4 * CHANNELS, TOK))],
    )(pos, *[spread_rows(plain, s) for s in (1, 2, 3)], spread_rows(with_mods, 0))
    x_lines = [x_planes] + [along_x(x_planes, q) for q in (1, 2, 3)]
    (first_turned,) = whole(turned_kernel, [shaped((SLICE, UNITS))])(pos, weight_one)
    x_blocks = both_cores(pos, after(x_lines, first_turned))
    c_lines = [c_planes] + [along_x(c_planes, q) for q in (1, 2, 3)]

    mods_column, mods_row, through = whole(
        mods_kernel,
        [
            shaped((INNER, CHANNELS, 8), f32),
            shaped((8, SLICE), f32),
            shaped((8, TOK), f32),
        ],
    )(pos, *x_blocks, weight_one)

    pre_sums, offsets, means = [None] * 4, [None] * 4, [None] * 4
    blocks = x_blocks
    for shift in (1, 3, 2, 0):
        pre_sums[shift], offsets[shift], means[shift] = whole(
            functools.partial(first_kernel, shift),
            [shaped(wide_units), shaped((SLICE, TOK)), shaped((1, TOK), f32)],
            [stage],
            some,
        )(pos, *blocks, mods_column, through, weight_one)
        blocks = after(blocks, pre_sums[shift])
    pre_sums = to_rows(pre_sums)
    hidden, slope, rest, factor, stats = whole(
        hidden_kernel,
        [
            shaped(wide_units),
            shaped(units, f32),
            shaped(units, f32),
            shaped((UNITS, 1), f32),
            shaped((2, TOK), f32),
        ],
    )(pos, *pre_sums)
    c_blocks = both_cores(pos, after(c_lines, pre_sums))
    *grad_sums, cot = whole(
        second_kernel,
        [shaped(units)] * 4 + [shaped((SLICE, TOKENS))],
        [pltpu.VMEM((4, SLICE, TOK), bf16)],
    )(pos, *c_blocks, mods_column, weight_two)
    hidden = all_rows(hidden)

    weights = pl.BlockSpec((UNITS, CHUNK), lambda i, pos: (0, i))
    scratch = [pltpu.VMEM((UNITS, TOKENS), bf16)]

    weight_shapes = [shaped((UNITS, SLICE)), shaped((SLICE, 8), f32)]
    own_second, sums_second = whole(second_weight_kernel, weight_shapes, scratch)(
        pos, *hidden, cot, mods_row, weight_two
    )
    other_second = swap_clips(own_second)
    grad_sums = to_rows(after(grad_sums, hidden[2]))
    (grad_pre,) = whole(grad_kernel, [shaped(wide_units)])(
        pos, *grad_sums, slope, rest, factor
    )
    grad_pre = all_rows(grad_pre)
    own_first, sums_first = whole(
        first_weight_kernel, weight_shapes, scratch + [pltpu.VMEM((SLICE, TOKENS), bf16)]
    )(pos, *grad_pre, *hidden, *offsets, *means, mods_row, weight_one)
    other_first = swap_clips(own_first)

    quarter = (4,) + piece
    terms = whole(
        mod_kernel, [shaped(quarter)] * 8, scratch + [pltpu.VMEM((8, TOK), f32)]
    )(
        pos,
        *grad_pre,
        first_turned,
        sums_first.reshape(INNER, CHANNELS, 8),
        sums_second.reshape(INNER, CHANNELS, 8),
    )
    lines = whole(core_kernel, [shaped(quarter)] * 4)(
        pos, *terms[:4], *after([across(term) for term in terms[4:]], other_second)
    )
    def clips_call(own, other):
        return call(
            clips_kernel,
            (SLICE // CHUNK,),
            [weights, weights],
            weights,
            shaped((UNITS, SLICE), f32),
        )(pos, own, other)

    grad_second = clips_call(own_second, other_second)
    planes = whole(plane_kernel, [shaped(piece)] * 4)(
        pos, lines[0], *after([along_x(lines[p], p) for p in (1, 2, 3)], grad_second)
    )
    grad_first = clips_call(own_first, other_first)
    planes = after(to_rows(planes), grad_first)
    pieces = whole(route_kernel, [shaped(piece)] * 4, [pltpu.VMEM((4,) + piece, bf16)])(
        pos, *planes
    )
    pieces = [pieces[0]] + [along_high(pieces[p], p) for p in (1, 2, 3)]

    grad_states, grad_shift, grad_scale, grad_gate = whole(
        states_kernel, [shaped(own, f32)] + [shaped((1, CHANNELS), f32)] * 3
    )(pos, *pieces, own_x, own_c, stats, scale_mod.T)
    return (
        grad_states.T[None],
        grad_first.T,
        grad_second.T,
        grad_shift,
        grad_scale,
        grad_gate,
    )


def solution(mesh):
    return jax.shard_map(
        on_device,
        mesh=mesh,
        in_specs=(
            P("dp", "row", "col"),
            P("dp", "row", "col"),
            P("dp", "col"),
            P("dp", "col"),
            P("dp", "col"),
            P("row", "col"),
            P("row", "col"),
        ),
        out_specs=(
            P("dp", "row", "col"),
            P("row", "col"),
            P("row", "col"),
            P("dp", "col"),
            P("dp", "col"),
            P("dp", "col"),
        ),
        check_vma=False,
    )
```

```python
import functools
import math

import jax
import jax.numpy as jnp
from jax import lax
from jax.experimental import pallas as pl
from jax.experimental.pallas import tpu as pltpu
from jax.sharding import PartitionSpec as P

D = 5120
FF = 13824
ROWS = 4
COLS = 32
INNER = 8
CHANNELS = D // COLS
UNITS = FF // COLS
TOK = 256
SLICE = D // ROWS
TOKENS = ROWS * TOK
EXTRA = 16
CHUNK = 256

bf16, f32 = jnp.bfloat16, jnp.float32

eps = 1e-06
tanh_factor = 0.7978845608028654
cubic_term = 0.044715
token_scale = 1.0 / math.sqrt(ROWS * TOK)
weight_scale = 1.0 / math.sqrt(2 * ROWS * TOK)
across_tokens = (((1,), (1,)), ((), ()))


def gelu_pair(values):
    squares = values * values
    inner = jnp.tanh(tanh_factor * (values + cubic_term * squares * values))
    half = 0.5 * (1.0 + inner)
    slope = half + 0.5 * values * (1.0 - inner * inner) * tanh_factor * (
        1.0 + 3.0 * cubic_term * squares
    )
    return values * half, slope


def turn(value, offset):
    return lax.rem(value + offset + 8, 4)


def spread_rows(values, shift):
    pairs = [
        (a * COLS + b * INNER + i, b * COLS + ((a + shift) % 4) * INNER + i)
        for a in range(4)
        for b in range(4)
        for i in range(INNER)
    ]
    return lax.ppermute(values, ("row", "col"), pairs)


def along_high(values, shift):
    pairs = [(h * 8 + i, ((h + shift) % 4) * 8 + i) for h in range(4) for i in range(INNER)]
    return lax.ppermute(values, "col", pairs)


def along_x(values, shift):
    pairs = [
        (h * 8 + x * 2 + k, h * 8 + ((x + shift) % 4) * 2 + k)
        for h in range(4)
        for x in range(4)
        for k in range(2)
    ]
    return lax.ppermute(values, "col", pairs)


def across(values):
    return lax.ppermute(values, "col", [(c, c ^ 1) for c in range(COLS)])


def along_row(values, shift):
    return lax.ppermute(values, "row", [(a, (a + shift) % 4) for a in range(4)])


def all_rows(values):
    return [values] + [along_row(values, q) for q in (1, 2, 3)]


def to_rows(values):
    return [values[0]] + [along_row(values[q], q) for q in (1, 2, 3)]


def swap_clips(values):
    return lax.ppermute(values, "dp", [(0, 1), (1, 0)])


def both_cores(pos, lines):
    shape = shaped((2 * lines[0].shape[0], TOK))
    packs = whole(pair_kernel, [shape, shape])(pos, *lines)
    return list(lines) + [across(pack) for pack in packs]


def after(values, other):
    return lax.optimization_barrier((values, other))[0]


cheap = pl.CostEstimate(flops=1024, bytes_accessed=1024, transcendentals=0)
some = pl.CostEstimate(flops=1024, bytes_accessed=8000000, transcendentals=0)
limit = pltpu.CompilerParams(vmem_limit_bytes=16 * 1024 * 1024)


def call(kernel, grid, in_specs, out_specs, out_shape, scratch=()):
    return pl.pallas_call(
        kernel,
        grid_spec=pltpu.PrefetchScalarGridSpec(
            num_scalar_prefetch=1,
            grid=grid,
            in_specs=in_specs,
            out_specs=out_specs,
            scratch_shapes=list(scratch),
        ),
        out_shape=out_shape,
        compiler_params=limit,
        cost_estimate=cheap,
    )


def whole(kernel, out_shape, scratch=(), cost=cheap):
    vmem = pl.BlockSpec(memory_space=pltpu.VMEM)

    def run(pos, *args):
        return pl.pallas_call(
            kernel,
            in_specs=[pl.BlockSpec(memory_space=pltpu.SMEM)] + [vmem] * len(args),
            out_specs=[vmem] * len(out_shape),
            out_shape=out_shape,
            scratch_shapes=list(scratch),
            compiler_params=limit,
            cost_estimate=cost,
        )(pos, *args)

    return run


def full(shape):
    return pl.BlockSpec(shape, lambda i, pos: (0,) * len(shape))


def shaped(shape, kind=bf16):
    return jax.ShapeDtypeStruct(shape, kind)


def place_of(pos, token):
    return turn(pos[1] - token, -1)


def channel_block(pos, q, flip):
    core = pos[3] if flip == 0 else 1 - pos[3]
    return turn(pos[2], -q) * 2 + core


def parts_of(values, count):
    parts = []
    for _ in range(count):
        parts.append(values.astype(bf16).astype(f32))
        values = values - parts[-1]
    return parts


def packed(values):
    return jnp.concatenate(parts_of(values, 2), 0).astype(bf16)


def unpacked(rows):
    wide = rows.astype(f32)
    return wide[0:8] + wide[8:16]


def pack_kernel(pos, plain, mods, out):
    line = lax.broadcasted_iota(jnp.int32, (3, CHANNELS), 0)
    values = mods[...] + jnp.where(line == 1, 1.0, 0.0)
    rows = parts_of(values, 3) + [jnp.zeros((EXTRA - 9, CHANNELS), f32)]
    out[: 2 * CHANNELS] = plain[...]
    out[2 * CHANNELS :] = jnp.zeros((EXTRA, TOK), bf16)
    out[2 * CHANNELS :, :CHANNELS] = jnp.concatenate(rows, 0).astype(bf16)


def pair_kernel(pos, l0, l1, l2, l3, first, second):
    rows = l0.shape[0]
    first[:rows], first[rows:] = l0[...], l1[...]
    second[:rows], second[rows:] = l2[...], l3[...]


def block_of(blocks, q, flip, at, size):
    if flip == 0:
        return blocks[q][pl.ds(at, size), :]
    rows = blocks[0].shape[0]
    return blocks[4 + q // 2][pl.ds(at + (q % 2) * rows, size), :]


def sort_kernel(pos, b0, b1, b2, b3, x, cot):
    for at, ref in enumerate((b0, b1, b2, b3)):
        rows = slice(at * CHANNELS, (at + 1) * CHANNELS)
        x[rows] = ref[:CHANNELS]
        cot[rows] = ref[CHANNELS : 2 * CHANNELS]
    x[4 * CHANNELS :] = b3[2 * CHANNELS :]


def turned_kernel(pos, w1, out):
    out[...] = w1[...].T


def mods_kernel(pos, *refs):
    blocks, w1, mods_column, mods_row, through_out = refs[:6], refs[6], refs[7], refs[8], refs[9]
    for q in range(4):
        for flip in range(2):
            rows = block_of(blocks, q, flip, 4 * CHANNELS, EXTRA).astype(f32)
            values = jnp.concatenate([rows[0:3] + rows[3:6] + rows[6:9], rows[9:14]], 0)
            mods_column[channel_block(pos, q, flip)] = values.T[:CHANNELS]
    values = mods_column[...].reshape(SLICE, 8).T
    mods_row[...] = values
    rows = jnp.concatenate(parts_of(values, 3) + [jnp.zeros_like(values)], 0).astype(bf16)
    through = lax.dot_general(rows, w1[...], across_tokens, preferred_element_type=f32)
    through = through[0:8] + through[8:16] + through[16:24]
    through_out[...] = jnp.zeros((8, TOK), f32)
    for at, line in ((0, through[1:2]), (2, through[0:1])):
        through_out[at : at + 1] = line[:, :TOK]
        through_out[at + 1 : at + 2, : UNITS - TOK] = line[:, TOK:]


def first_kernel(shift, pos, *refs):
    blocks, mods, through, w1 = refs[:6], refs[6], refs[7], refs[8]
    out, offset_out, mean_out, offsets = refs[9:]
    place = place_of(pos, turn(pos[0], shift))
    at = pl.multiple_of(place * CHANNELS, 32)
    total = 0.0
    for q in range(4):
        for flip in range(2):
            block = block_of(blocks, q, flip, at, CHANNELS).astype(f32)
            total = total + jnp.sum(block, 0, keepdims=True)
    mean = total / SLICE
    square = 0.0
    for q in range(4):
        for flip in range(2):
            j = channel_block(pos, q, flip)
            offset = block_of(blocks, q, flip, at, CHANNELS).astype(f32) - mean
            square = square + jnp.sum(offset * offset, 0, keepdims=True)
            offsets[j] = (offset * mods[j][:, 1:2]).astype(bf16)
            rows = pl.ds(pl.multiple_of(j * CHANNELS, 32), CHANNELS)
            offset_out[rows, :] = offset.astype(bf16)
    mean_out[...] = mean
    out[:UNITS] = jnp.dot(
        w1[...], offsets[...].reshape(SLICE, TOK), preferred_element_type=f32
    ).astype(bf16)
    four = jnp.concatenate([mean, square, through[0:2]], 0)
    extra = parts_of(four, 3) + parts_of(through[2:4], 2)
    out[UNITS:] = jnp.concatenate(extra, 0).astype(bf16)


def hidden_kernel(pos, p0, p1, p2, p3, hidden_out, slope_out, rest_out, factor_out, stats_out):
    parts = (p0, p1, p2, p3)
    extras = [ref[UNITS:].astype(f32) for ref in parts]
    fours = [e[0:4] + e[4:8] + e[8:12] for e in extras]
    shifts = sum(e[12:14] + e[14:16] for e in extras)
    centre = 0.25 * (fours[0][0:1] + fours[1][0:1] + fours[2][0:1] + fours[3][0:1])
    spread = 0.0
    for four in fours:
        spread = spread + four[1:2] + SLICE * (four[0:1] - centre) ** 2
    inverse = lax.rsqrt(spread / D + eps)
    stats = jnp.concatenate([centre, inverse], 0)
    stats_out[...] = stats
    hidden_out[UNITS:] = jnp.concatenate(
        parts_of(stats, 3) + [jnp.zeros((EXTRA - 6, TOK), f32)], 0
    ).astype(bf16)
    columns = jnp.concatenate([four[2:4] for four in fours] + [shifts] * 4, 0).T
    for half, at in ((0, slice(0, TOK)), (1, slice(TOK, UNITS))):
        size = at.stop - at.start
        rest, total = 0.0, 0.0
        for i, ref in enumerate(parts):
            factor = columns[:size, 2 * i + half : 2 * i + half + 1]
            total = total + factor
            rest = rest + (ref[at].astype(f32) + factor * (fours[i][0:1] - centre))
        rest = rest * inverse
        hidden, slope = gelu_pair(rest + columns[:size, 8 + half : 9 + half])
        hidden_out[at] = hidden.astype(bf16)
        slope_out[at] = slope
        rest_out[at] = rest
        factor_out[at] = total


def second_kernel(pos, *refs):
    blocks, mods, w2 = refs[:6], refs[6], refs[7]
    sums, cot_out, scaled = refs[8:12], refs[12], refs[13]
    for shift, out in enumerate(sums):
        token = turn(pos[0], shift)
        at = pl.multiple_of(place_of(pos, token) * CHANNELS, 32)
        lanes = pl.ds(pl.multiple_of(token * TOK, TOK), TOK)
        for q in range(4):
            for flip in range(2):
                j = channel_block(pos, q, flip)
                block = block_of(blocks, q, flip, at, CHANNELS)
                rows = pl.ds(pl.multiple_of(j * CHANNELS, 32), CHANNELS)
                cot_out[rows, lanes] = block
                scaled[shift, rows, :] = (block.astype(f32) * mods[j][:, 2:3]).astype(bf16)
        out[...] = jnp.dot(w2[...], scaled[shift], preferred_element_type=f32).astype(bf16)


def grad_kernel(pos, own, one, two, three, slope, rest, factor, out):
    grad = own[...].astype(f32) + one[...].astype(f32)
    grad = grad + (two[...].astype(f32) + three[...].astype(f32))
    grad = (grad * slope[...]).astype(bf16)
    out[:UNITS] = grad
    wide = grad.astype(f32)
    first = jnp.sum(wide * factor[...], 0, keepdims=True)
    second = jnp.sum(wide * rest[...], 0, keepdims=True)
    line = lax.broadcasted_iota(jnp.int32, (8, TOK), 0)
    out[UNITS:] = packed(jnp.where(line == 3, first, jnp.where(line == 4, second, 0.0)))


def collect(pos, refs, store):
    for q, ref in enumerate(refs):
        at = pl.multiple_of(turn(pos[0], -q) * TOK, TOK)
        store[:, pl.ds(at, TOK)] = ref[:UNITS]


def second_weight_kernel(pos, b0, b1, b2, b3, cot, mods, w2, send, sums, store):
    collect(pos, (b0, b1, b2, b3), store)
    line = lax.broadcasted_iota(jnp.int32, (8, CHUNK), 0)
    for at in range(0, SLICE, CHUNK):
        part = slice(at, at + CHUNK)
        raw = lax.dot_general(
            store[...], cot[part, :], across_tokens, preferred_element_type=f32
        )
        total = jnp.sum(w2[:, part].astype(f32) * raw, 0, keepdims=True)
        sums[part, :] = jnp.where(line == 2, total, 0.0).T
        send[:, part] = (raw * (mods[2:3, part] * weight_scale)).astype(bf16)


def first_weight_kernel(pos, *refs):
    grads, hiddens, offsets, means = refs[:4], refs[4:8], refs[8:12], refs[12:16]
    mods, w1, send, sums, store, others = refs[16:]
    total, lift = 0.0, 0.0
    for q in range(4):
        at = (4 - q) % 4
        extra = hiddens[q][UNITS:].astype(f32)
        stats = extra[0:2] + extra[2:4] + extra[4:6]
        grad = grads[q][:UNITS].astype(f32)
        total = total + jnp.sum(grad, 1, keepdims=True)
        grad = grad * stats[1:2]
        lift = lift + jnp.sum(grad * (means[at][...] - stats[0:1]), 1, keepdims=True)
        lanes = slice(at * TOK, (at + 1) * TOK)
        store[:, lanes] = grad.astype(bf16)
        others[:, lanes] = offsets[at][...]
    line = lax.broadcasted_iota(jnp.int32, (8, CHUNK), 0)
    for at in range(0, SLICE, CHUNK):
        part = slice(at, at + CHUNK)
        raw = lift + lax.dot_general(
            store[...], others[part, :], across_tokens, preferred_element_type=f32
        )
        weight = w1[:, part].astype(f32)
        shift = jnp.sum(weight * total, 0, keepdims=True)
        scale = jnp.sum(weight * raw, 0, keepdims=True)
        sums[part, :] = jnp.where(line == 0, shift, jnp.where(line == 1, scale, 0.0)).T
        grad = (raw * mods[1:2, part] + total * mods[0:1, part]) * weight_scale
        send[:, part] = grad.astype(bf16)


def mod_kernel(pos, g0, g1, g2, g3, w1, sums_one, sums_two, *rest):
    keeps, sends, store, line = rest[:4], rest[4:8], rest[8], rest[9]
    grads = (g0, g1, g2, g3)
    collect(pos, grads, store)
    line[...] = jnp.zeros((8, TOK), f32)
    smalls = [unpacked(ref[UNITS:]) for ref in grads]
    for core, outs in ((pos[3], keeps), (1 - pos[3], sends)):
        for p, out in enumerate(outs):
            j = turn(pos[2], p) * 2 + core
            rows = pl.ds(pl.multiple_of(j * CHANNELS, 32), CHANNELS)
            product = jnp.dot(w1[rows, :], store[...], preferred_element_type=f32).astype(bf16)
            for token in range(4):
                out[turn(token, -pos[0]), :CHANNELS] = product[
                    :, token * TOK : (token + 1) * TOK
                ]
            line[:, :CHANNELS] = (sums_one[j] + sums_two[j]).T
            for q, small in enumerate(smalls):
                out[(4 - q) % 4, CHANNELS:] = packed(small + line[...])


def add_up(out, parts):
    total = parts[0][:CHANNELS].astype(f32)
    small = unpacked(parts[0][CHANNELS:])
    for part in parts[1:]:
        total = total + part[:CHANNELS].astype(f32)
        small = small + unpacked(part[CHANNELS:])
    out[:CHANNELS] = total.astype(bf16)
    out[CHANNELS:] = packed(small)


def core_kernel(pos, *refs):
    for keep, other, out in zip(refs[:4], refs[4:8], refs[8:]):
        for s in range(4):
            add_up(out.at[s], [keep.at[s], other.at[s]])


def plane_kernel(pos, own, one, two, three, o0, o1, o2, o3):
    for s, out in enumerate((o0, o1, o2, o3)):
        add_up(out, [ref.at[s] for ref in (own, one, two, three)])


def route_kernel(pos, a0, a1, a2, a3, o0, o1, o2, o3, held):
    for q, ref in enumerate((a0, a1, a2, a3)):
        held[turn(pos[0], -q)] = ref[...]
    for p, out in enumerate((o0, o1, o2, o3)):
        out[...] = held[turn(pos[1], p)]


def states_kernel(pos, a0, a1, a2, a3, x, cot, stats, scale, out, *mods_out):
    centre, inverse = stats[0:1], stats[1:2]
    grad_mod, small = 0.0, 0.0
    for ref in (a0, a1, a2, a3):
        grad_mod = grad_mod + ref[:CHANNELS].astype(f32)
        small = small + unpacked(ref[CHANNELS:])
    normed = (x[...].astype(f32) - centre) * inverse
    grad_normed = grad_mod * (1.0 + scale[...])
    out[...] = cot[...].astype(f32) + inverse * (
        grad_normed - small[3:4] / D - normed * (small[4:5] / D)
    )
    for at, ref in enumerate(mods_out):
        ref[...] = small[at : at + 1, :CHANNELS] * token_scale


def clips_kernel(pos, own, other, out):
    out[...] = own[...].astype(f32) + other[...].astype(f32)


def on_device(states, cotangent, shift_mod, scale_mod, gate_mod, first_weight, second_weight):
    row, col = lax.axis_index("row"), lax.axis_index("col")
    high, x, core = col // INNER, lax.rem(col, INNER) // 2, lax.rem(col, 2)
    pos = jnp.stack([row, high, x, core]).astype(jnp.int32)
    weight_one, weight_two = first_weight.T, second_weight.T
    own_x, own_c = states[0].T, cotangent[0].T

    own = (CHANNELS, TOK)
    piece = (CHANNELS + EXTRA, TOK)
    units = (UNITS, TOK)
    wide_units = (UNITS + EXTRA, TOK)
    stage = pltpu.VMEM((INNER, CHANNELS, TOK), bf16)

    pair = (2 * CHANNELS, TOK)
    wide_pair = (2 * CHANNELS + EXTRA, TOK)
    plain = jnp.concatenate([own_x, own_c], 0)
    (with_mods,) = whole(pack_kernel, [shaped(wide_pair)])(
        pos, plain, jnp.concatenate([shift_mod, scale_mod, gate_mod], 0)
    )
    x_planes, c_planes = whole(
        sort_kernel,
        [shaped((4 * CHANNELS + EXTRA, TOK)), shaped((4 * CHANNELS, TOK))],
    )(pos, *[spread_rows(plain, s) for s in (1, 2, 3)], spread_rows(with_mods, 0))
    x_lines = [x_planes] + [along_x(x_planes, q) for q in (1, 2, 3)]
    (first_turned,) = whole(turned_kernel, [shaped((SLICE, UNITS))])(pos, weight_one)
    x_blocks = both_cores(pos, after(x_lines, first_turned))
    c_lines = [c_planes] + [along_x(c_planes, q) for q in (1, 2, 3)]

    mods_column, mods_row, through = whole(
        mods_kernel,
        [
            shaped((INNER, CHANNELS, 8), f32),
            shaped((8, SLICE), f32),
            shaped((8, TOK), f32),
        ],
    )(pos, *x_blocks, weight_one)

    pre_sums, offsets, means = [None] * 4, [None] * 4, [None] * 4
    blocks = x_blocks
    for shift in (1, 3, 2, 0):
        pre_sums[shift], offsets[shift], means[shift] = whole(
            functools.partial(first_kernel, shift),
            [shaped(wide_units), shaped((SLICE, TOK)), shaped((1, TOK), f32)],
            [stage],
            some,
        )(pos, *blocks, mods_column, through, weight_one)
        blocks = after(blocks, pre_sums[shift])
    pre_sums = to_rows(pre_sums)
    hidden, slope, rest, factor, stats = whole(
        hidden_kernel,
        [
            shaped(wide_units),
            shaped(units, f32),
            shaped(units, f32),
            shaped((UNITS, 1), f32),
            shaped((2, TOK), f32),
        ],
    )(pos, *pre_sums)
    c_blocks = both_cores(pos, after(c_lines, pre_sums))
    *grad_sums, cot = whole(
        second_kernel,
        [shaped(units)] * 4 + [shaped((SLICE, TOKENS))],
        [pltpu.VMEM((4, SLICE, TOK), bf16)],
    )(pos, *c_blocks, mods_column, weight_two)
    hidden = all_rows(hidden)

    weights = pl.BlockSpec((UNITS, CHUNK), lambda i, pos: (0, i))
    scratch = [pltpu.VMEM((UNITS, TOKENS), bf16)]

    weight_shapes = [shaped((UNITS, SLICE)), shaped((SLICE, 8), f32)]
    own_second, sums_second = whole(second_weight_kernel, weight_shapes, scratch)(
        pos, *hidden, cot, mods_row, weight_two
    )
    other_second = swap_clips(own_second)
    grad_sums = to_rows(after(grad_sums, hidden[1]))
    (grad_pre,) = whole(grad_kernel, [shaped(wide_units)])(
        pos, *grad_sums, slope, rest, factor
    )
    grad_pre = all_rows(grad_pre)
    own_first, sums_first = whole(
        first_weight_kernel, weight_shapes, scratch + [pltpu.VMEM((SLICE, TOKENS), bf16)]
    )(pos, *grad_pre, *hidden, *offsets, *means, mods_row, weight_one)
    other_first = swap_clips(own_first)

    quarter = (4,) + piece
    terms = whole(
        mod_kernel, [shaped(quarter)] * 8, scratch + [pltpu.VMEM((8, TOK), f32)]
    )(
        pos,
        *grad_pre,
        first_turned,
        sums_first.reshape(INNER, CHANNELS, 8),
        sums_second.reshape(INNER, CHANNELS, 8),
    )
    lines = whole(core_kernel, [shaped(quarter)] * 4)(
        pos, *terms[:4], *after([across(term) for term in terms[4:]], other_second)
    )
    def clips_call(own, other):
        return call(
            clips_kernel,
            (SLICE // CHUNK,),
            [weights, weights],
            weights,
            shaped((UNITS, SLICE), f32),
        )(pos, own, other)

    grad_second = clips_call(own_second, other_second)
    planes = whole(plane_kernel, [shaped(piece)] * 4)(
        pos, lines[0], *after([along_x(lines[p], p) for p in (1, 2, 3)], grad_second)
    )
    grad_first = clips_call(own_first, other_first)
    planes = after(to_rows(planes), grad_first)
    pieces = whole(route_kernel, [shaped(piece)] * 4, [pltpu.VMEM((4,) + piece, bf16)])(
        pos, *planes
    )
    pieces = [pieces[0]] + [along_high(pieces[p], p) for p in (1, 2, 3)]

    grad_states, grad_shift, grad_scale, grad_gate = whole(
        states_kernel, [shaped(own, f32)] + [shaped((1, CHANNELS), f32)] * 3
    )(pos, *pieces, own_x, own_c, stats, scale_mod.T)
    return (
        grad_states.T[None],
        grad_first.T,
        grad_second.T,
        grad_shift,
        grad_scale,
        grad_gate,
    )


def solution(mesh):
    return jax.shard_map(
        on_device,
        mesh=mesh,
        in_specs=(
            P("dp", "row", "col"),
            P("dp", "row", "col"),
            P("dp", "col"),
            P("dp", "col"),
            P("dp", "col"),
            P("row", "col"),
            P("row", "col"),
        ),
        out_specs=(
            P("dp", "row", "col"),
            P("row", "col"),
            P("row", "col"),
            P("dp", "col"),
            P("dp", "col"),
            P("dp", "col"),
        ),
        check_vma=False,
    )
```

```python
import functools
import math

import jax
import jax.numpy as jnp
from jax import lax
from jax.experimental import pallas as pl
from jax.experimental.pallas import tpu as pltpu
from jax.sharding import PartitionSpec as P

D = 5120
FF = 13824
ROWS = 4
COLS = 32
INNER = 8
CHANNELS = D // COLS
UNITS = FF // COLS
TOK = 256
SLICE = D // ROWS
TOKENS = ROWS * TOK
EXTRA = 16
CHUNK = 256

bf16, f32 = jnp.bfloat16, jnp.float32

eps = 1e-06
tanh_factor = 0.7978845608028654
cubic_term = 0.044715
token_scale = 1.0 / math.sqrt(ROWS * TOK)
weight_scale = 1.0 / math.sqrt(2 * ROWS * TOK)
across_tokens = (((1,), (1,)), ((), ()))


def gelu_pair(values):
    squares = values * values
    inner = jnp.tanh(tanh_factor * (values + cubic_term * squares * values))
    half = 0.5 * (1.0 + inner)
    slope = half + 0.5 * values * (1.0 - inner * inner) * tanh_factor * (
        1.0 + 3.0 * cubic_term * squares
    )
    return values * half, slope


def turn(value, offset):
    return lax.rem(value + offset + 8, 4)


def spread_rows(values, shift):
    pairs = [
        (a * COLS + b * INNER + i, b * COLS + ((a + shift) % 4) * INNER + i)
        for a in range(4)
        for b in range(4)
        for i in range(INNER)
    ]
    return lax.ppermute(values, ("row", "col"), pairs)


def along_high(values, shift):
    pairs = [(h * 8 + i, ((h + shift) % 4) * 8 + i) for h in range(4) for i in range(INNER)]
    return lax.ppermute(values, "col", pairs)


def along_x(values, shift):
    pairs = [
        (h * 8 + x * 2 + k, h * 8 + ((x + shift) % 4) * 2 + k)
        for h in range(4)
        for x in range(4)
        for k in range(2)
    ]
    return lax.ppermute(values, "col", pairs)


def across(values):
    return lax.ppermute(values, "col", [(c, c ^ 1) for c in range(COLS)])


def along_row(values, shift):
    return lax.ppermute(values, "row", [(a, (a + shift) % 4) for a in range(4)])


def in_order(move):
    far, one, three = lax.optimization_barrier((move(2), move(1), move(3)))
    return [one, far, three]


def all_rows(values):
    return [values] + in_order(lambda q: along_row(values, q))


def to_rows(values):
    return [values[0]] + in_order(lambda q: along_row(values[q], q))


def swap_clips(values):
    return lax.ppermute(values, "dp", [(0, 1), (1, 0)])


def both_cores(pos, lines):
    shape = shaped((2 * lines[0].shape[0], TOK))
    packs = whole(pair_kernel, [shape, shape])(pos, *lines)
    return list(lines) + [across(pack) for pack in packs]


def after(values, other):
    return lax.optimization_barrier((values, other))[0]


cheap = pl.CostEstimate(flops=1024, bytes_accessed=1024, transcendentals=0)
some = pl.CostEstimate(flops=1024, bytes_accessed=8000000, transcendentals=0)
limit = pltpu.CompilerParams(vmem_limit_bytes=16 * 1024 * 1024)


def call(kernel, grid, in_specs, out_specs, out_shape, scratch=()):
    return pl.pallas_call(
        kernel,
        grid_spec=pltpu.PrefetchScalarGridSpec(
            num_scalar_prefetch=1,
            grid=grid,
            in_specs=in_specs,
            out_specs=out_specs,
            scratch_shapes=list(scratch),
        ),
        out_shape=out_shape,
        compiler_params=limit,
        cost_estimate=cheap,
    )


def whole(kernel, out_shape, scratch=(), cost=cheap):
    vmem = pl.BlockSpec(memory_space=pltpu.VMEM)

    def run(pos, *args):
        return pl.pallas_call(
            kernel,
            in_specs=[pl.BlockSpec(memory_space=pltpu.SMEM)] + [vmem] * len(args),
            out_specs=[vmem] * len(out_shape),
            out_shape=out_shape,
            scratch_shapes=list(scratch),
            compiler_params=limit,
            cost_estimate=cost,
        )(pos, *args)

    return run


def full(shape):
    return pl.BlockSpec(shape, lambda i, pos: (0,) * len(shape))


def shaped(shape, kind=bf16):
    return jax.ShapeDtypeStruct(shape, kind)


def place_of(pos, token):
    return turn(pos[1] - token, -1)


def channel_block(pos, q, flip):
    core = pos[3] if flip == 0 else 1 - pos[3]
    return turn(pos[2], -q) * 2 + core


def parts_of(values, count):
    parts = []
    for _ in range(count):
        parts.append(values.astype(bf16).astype(f32))
        values = values - parts[-1]
    return parts


def packed(values):
    return jnp.concatenate(parts_of(values, 2), 0).astype(bf16)


def unpacked(rows):
    wide = rows.astype(f32)
    return wide[0:8] + wide[8:16]


def pack_kernel(pos, plain, mods, out):
    line = lax.broadcasted_iota(jnp.int32, (3, CHANNELS), 0)
    values = mods[...] + jnp.where(line == 1, 1.0, 0.0)
    rows = parts_of(values, 3) + [jnp.zeros((EXTRA - 9, CHANNELS), f32)]
    out[: 2 * CHANNELS] = plain[...]
    out[2 * CHANNELS :] = jnp.zeros((EXTRA, TOK), bf16)
    out[2 * CHANNELS :, :CHANNELS] = jnp.concatenate(rows, 0).astype(bf16)


def pair_kernel(pos, l0, l1, l2, l3, first, second):
    rows = l0.shape[0]
    first[:rows], first[rows:] = l0[...], l1[...]
    second[:rows], second[rows:] = l2[...], l3[...]


def block_of(blocks, q, flip, at, size):
    if flip == 0:
        return blocks[q][pl.ds(at, size), :]
    rows = blocks[0].shape[0]
    return blocks[4 + q // 2][pl.ds(at + (q % 2) * rows, size), :]


def sort_kernel(pos, b0, b1, b2, b3, x, cot):
    for at, ref in enumerate((b0, b1, b2, b3)):
        rows = slice(at * CHANNELS, (at + 1) * CHANNELS)
        x[rows] = ref[:CHANNELS]
        cot[rows] = ref[CHANNELS : 2 * CHANNELS]
    x[4 * CHANNELS :] = b3[2 * CHANNELS :]


def turned_kernel(pos, w1, out):
    out[...] = w1[...].T


def mods_kernel(pos, *refs):
    blocks, w1, mods_column, mods_row, through_out = refs[:6], refs[6], refs[7], refs[8], refs[9]
    for q in range(4):
        for flip in range(2):
            rows = block_of(blocks, q, flip, 4 * CHANNELS, EXTRA).astype(f32)
            values = jnp.concatenate([rows[0:3] + rows[3:6] + rows[6:9], rows[9:14]], 0)
            mods_column[channel_block(pos, q, flip)] = values.T[:CHANNELS]
    values = mods_column[...].reshape(SLICE, 8).T
    mods_row[...] = values
    rows = jnp.concatenate(parts_of(values, 3) + [jnp.zeros_like(values)], 0).astype(bf16)
    through = lax.dot_general(rows, w1[...], across_tokens, preferred_element_type=f32)
    through = through[0:8] + through[8:16] + through[16:24]
    through_out[...] = jnp.zeros((8, TOK), f32)
    for at, line in ((0, through[1:2]), (2, through[0:1])):
        through_out[at : at + 1] = line[:, :TOK]
        through_out[at + 1 : at + 2, : UNITS - TOK] = line[:, TOK:]


def first_kernel(shift, pos, *refs):
    blocks, mods, through, w1 = refs[:6], refs[6], refs[7], refs[8]
    out, offset_out, mean_out, offsets = refs[9:]
    place = place_of(pos, turn(pos[0], shift))
    at = pl.multiple_of(place * CHANNELS, 32)
    total = 0.0
    for q in range(4):
        for flip in range(2):
            block = block_of(blocks, q, flip, at, CHANNELS).astype(f32)
            total = total + jnp.sum(block, 0, keepdims=True)
    mean = total / SLICE
    square = 0.0
    for q in range(4):
        for flip in range(2):
            j = channel_block(pos, q, flip)
            offset = block_of(blocks, q, flip, at, CHANNELS).astype(f32) - mean
            square = square + jnp.sum(offset * offset, 0, keepdims=True)
            offsets[j] = (offset * mods[j][:, 1:2]).astype(bf16)
            rows = pl.ds(pl.multiple_of(j * CHANNELS, 32), CHANNELS)
            offset_out[rows, :] = offset.astype(bf16)
    mean_out[...] = mean
    out[:UNITS] = jnp.dot(
        w1[...], offsets[...].reshape(SLICE, TOK), preferred_element_type=f32
    ).astype(bf16)
    four = jnp.concatenate([mean, square, through[0:2]], 0)
    extra = parts_of(four, 3) + parts_of(through[2:4], 2)
    out[UNITS:] = jnp.concatenate(extra, 0).astype(bf16)


def hidden_kernel(pos, p0, p1, p2, p3, hidden_out, slope_out, rest_out, factor_out, stats_out):
    parts = (p0, p1, p2, p3)
    extras = [ref[UNITS:].astype(f32) for ref in parts]
    fours = [e[0:4] + e[4:8] + e[8:12] for e in extras]
    shifts = sum(e[12:14] + e[14:16] for e in extras)
    centre = 0.25 * (fours[0][0:1] + fours[1][0:1] + fours[2][0:1] + fours[3][0:1])
    spread = 0.0
    for four in fours:
        spread = spread + four[1:2] + SLICE * (four[0:1] - centre) ** 2
    inverse = lax.rsqrt(spread / D + eps)
    stats = jnp.concatenate([centre, inverse], 0)
    stats_out[...] = stats
    hidden_out[UNITS:] = jnp.concatenate(
        parts_of(stats, 3) + [jnp.zeros((EXTRA - 6, TOK), f32)], 0
    ).astype(bf16)
    columns = jnp.concatenate([four[2:4] for four in fours] + [shifts] * 4, 0).T
    for half, at in ((0, slice(0, TOK)), (1, slice(TOK, UNITS))):
        size = at.stop - at.start
        rest, total = 0.0, 0.0
        for i, ref in enumerate(parts):
            factor = columns[:size, 2 * i + half : 2 * i + half + 1]
            total = total + factor
            rest = rest + (ref[at].astype(f32) + factor * (fours[i][0:1] - centre))
        rest = rest * inverse
        hidden, slope = gelu_pair(rest + columns[:size, 8 + half : 9 + half])
        hidden_out[at] = hidden.astype(bf16)
        slope_out[at] = slope
        rest_out[at] = rest
        factor_out[at] = total


def second_kernel(pos, *refs):
    blocks, mods, w2 = refs[:6], refs[6], refs[7]
    sums, cot_out, scaled = refs[8:12], refs[12], refs[13]
    for shift, out in enumerate(sums):
        token = turn(pos[0], shift)
        at = pl.multiple_of(place_of(pos, token) * CHANNELS, 32)
        lanes = pl.ds(pl.multiple_of(token * TOK, TOK), TOK)
        for q in range(4):
            for flip in range(2):
                j = channel_block(pos, q, flip)
                block = block_of(blocks, q, flip, at, CHANNELS)
                rows = pl.ds(pl.multiple_of(j * CHANNELS, 32), CHANNELS)
                cot_out[rows, lanes] = block
                scaled[shift, rows, :] = (block.astype(f32) * mods[j][:, 2:3]).astype(bf16)
        out[...] = jnp.dot(w2[...], scaled[shift], preferred_element_type=f32).astype(bf16)


def grad_kernel(pos, own, one, two, three, slope, rest, factor, out):
    grad = own[...].astype(f32) + one[...].astype(f32)
    grad = grad + (two[...].astype(f32) + three[...].astype(f32))
    grad = (grad * slope[...]).astype(bf16)
    out[:UNITS] = grad
    wide = grad.astype(f32)
    first = jnp.sum(wide * factor[...], 0, keepdims=True)
    second = jnp.sum(wide * rest[...], 0, keepdims=True)
    line = lax.broadcasted_iota(jnp.int32, (8, TOK), 0)
    out[UNITS:] = packed(jnp.where(line == 3, first, jnp.where(line == 4, second, 0.0)))


def collect(pos, refs, store):
    for q, ref in enumerate(refs):
        at = pl.multiple_of(turn(pos[0], -q) * TOK, TOK)
        store[:, pl.ds(at, TOK)] = ref[:UNITS]


def second_weight_kernel(pos, b0, b1, b2, b3, cot, mods, w2, send, sums, store):
    collect(pos, (b0, b1, b2, b3), store)
    line = lax.broadcasted_iota(jnp.int32, (8, CHUNK), 0)
    for at in range(0, SLICE, CHUNK):
        part = slice(at, at + CHUNK)
        raw = lax.dot_general(
            store[...], cot[part, :], across_tokens, preferred_element_type=f32
        )
        total = jnp.sum(w2[:, part].astype(f32) * raw, 0, keepdims=True)
        sums[part, :] = jnp.where(line == 2, total, 0.0).T
        send[:, part] = (raw * (mods[2:3, part] * weight_scale)).astype(bf16)


def first_weight_kernel(pos, *refs):
    grads, hiddens, offsets, means = refs[:4], refs[4:8], refs[8:12], refs[12:16]
    mods, w1, send, sums, store, others = refs[16:]
    total, lift = 0.0, 0.0
    for q in range(4):
        at = (4 - q) % 4
        extra = hiddens[q][UNITS:].astype(f32)
        stats = extra[0:2] + extra[2:4] + extra[4:6]
        grad = grads[q][:UNITS].astype(f32)
        total = total + jnp.sum(grad, 1, keepdims=True)
        grad = grad * stats[1:2]
        lift = lift + jnp.sum(grad * (means[at][...] - stats[0:1]), 1, keepdims=True)
        lanes = slice(at * TOK, (at + 1) * TOK)
        store[:, lanes] = grad.astype(bf16)
        others[:, lanes] = offsets[at][...]
    line = lax.broadcasted_iota(jnp.int32, (8, CHUNK), 0)
    for at in range(0, SLICE, CHUNK):
        part = slice(at, at + CHUNK)
        raw = lift + lax.dot_general(
            store[...], others[part, :], across_tokens, preferred_element_type=f32
        )
        weight = w1[:, part].astype(f32)
        shift = jnp.sum(weight * total, 0, keepdims=True)
        scale = jnp.sum(weight * raw, 0, keepdims=True)
        sums[part, :] = jnp.where(line == 0, shift, jnp.where(line == 1, scale, 0.0)).T
        grad = (raw * mods[1:2, part] + total * mods[0:1, part]) * weight_scale
        send[:, part] = grad.astype(bf16)


def mod_kernel(pos, g0, g1, g2, g3, w1, sums_one, sums_two, *rest):
    keeps, sends, store, line = rest[:4], rest[4:8], rest[8], rest[9]
    grads = (g0, g1, g2, g3)
    collect(pos, grads, store)
    line[...] = jnp.zeros((8, TOK), f32)
    smalls = [unpacked(ref[UNITS:]) for ref in grads]
    for core, outs in ((pos[3], keeps), (1 - pos[3], sends)):
        for p, out in enumerate(outs):
            j = turn(pos[2], p) * 2 + core
            rows = pl.ds(pl.multiple_of(j * CHANNELS, 32), CHANNELS)
            product = jnp.dot(w1[rows, :], store[...], preferred_element_type=f32).astype(bf16)
            for token in range(4):
                out[turn(token, -pos[0]), :CHANNELS] = product[
                    :, token * TOK : (token + 1) * TOK
                ]
            line[:, :CHANNELS] = (sums_one[j] + sums_two[j]).T
            for q, small in enumerate(smalls):
                out[(4 - q) % 4, CHANNELS:] = packed(small + line[...])


def add_up(out, parts):
    total = parts[0][:CHANNELS].astype(f32)
    small = unpacked(parts[0][CHANNELS:])
    for part in parts[1:]:
        total = total + part[:CHANNELS].astype(f32)
        small = small + unpacked(part[CHANNELS:])
    out[:CHANNELS] = total.astype(bf16)
    out[CHANNELS:] = packed(small)


def core_kernel(pos, *refs):
    for keep, other, out in zip(refs[:4], refs[4:8], refs[8:]):
        for s in range(4):
            add_up(out.at[s], [keep.at[s], other.at[s]])


def plane_kernel(pos, own, one, two, three, o0, o1, o2, o3):
    for s, out in enumerate((o0, o1, o2, o3)):
        add_up(out, [ref.at[s] for ref in (own, one, two, three)])


def route_kernel(pos, a0, a1, a2, a3, o0, o1, o2, o3, held):
    for q, ref in enumerate((a0, a1, a2, a3)):
        held[turn(pos[0], -q)] = ref[...]
    for p, out in enumerate((o0, o1, o2, o3)):
        out[...] = held[turn(pos[1], p)]


def states_kernel(pos, a0, a1, a2, a3, x, cot, stats, scale, out, *mods_out):
    centre, inverse = stats[0:1], stats[1:2]
    grad_mod, small = 0.0, 0.0
    for ref in (a0, a1, a2, a3):
        grad_mod = grad_mod + ref[:CHANNELS].astype(f32)
        small = small + unpacked(ref[CHANNELS:])
    normed = (x[...].astype(f32) - centre) * inverse
    grad_normed = grad_mod * (1.0 + scale[...])
    out[...] = cot[...].astype(f32) + inverse * (
        grad_normed - small[3:4] / D - normed * (small[4:5] / D)
    )
    for at, ref in enumerate(mods_out):
        ref[...] = small[at : at + 1, :CHANNELS] * token_scale


def clips_kernel(pos, own, other, out):
    out[...] = own[...].astype(f32) + other[...].astype(f32)


def on_device(states, cotangent, shift_mod, scale_mod, gate_mod, first_weight, second_weight):
    row, col = lax.axis_index("row"), lax.axis_index("col")
    high, x, core = col // INNER, lax.rem(col, INNER) // 2, lax.rem(col, 2)
    pos = jnp.stack([row, high, x, core]).astype(jnp.int32)
    weight_one, weight_two = first_weight.T, second_weight.T
    own_x, own_c = states[0].T, cotangent[0].T

    own = (CHANNELS, TOK)
    piece = (CHANNELS + EXTRA, TOK)
    units = (UNITS, TOK)
    wide_units = (UNITS + EXTRA, TOK)
    stage = pltpu.VMEM((INNER, CHANNELS, TOK), bf16)

    pair = (2 * CHANNELS, TOK)
    wide_pair = (2 * CHANNELS + EXTRA, TOK)
    plain = jnp.concatenate([own_x, own_c], 0)
    (with_mods,) = whole(pack_kernel, [shaped(wide_pair)])(
        pos, plain, jnp.concatenate([shift_mod, scale_mod, gate_mod], 0)
    )
    x_planes, c_planes = whole(
        sort_kernel,
        [shaped((4 * CHANNELS + EXTRA, TOK)), shaped((4 * CHANNELS, TOK))],
    )(pos, *[spread_rows(plain, s) for s in (1, 2, 3)], spread_rows(with_mods, 0))
    x_lines = [x_planes] + in_order(lambda q: along_x(x_planes, q))
    (first_turned,) = whole(turned_kernel, [shaped((SLICE, UNITS))])(pos, weight_one)
    x_blocks = both_cores(pos, after(x_lines, first_turned))
    c_lines = [c_planes] + in_order(lambda q: along_x(c_planes, q))

    mods_column, mods_row, through = whole(
        mods_kernel,
        [
            shaped((INNER, CHANNELS, 8), f32),
            shaped((8, SLICE), f32),
            shaped((8, TOK), f32),
        ],
    )(pos, *x_blocks, weight_one)

    pre_sums, offsets, means = [None] * 4, [None] * 4, [None] * 4
    blocks = x_blocks
    for shift in (1, 3, 2, 0):
        pre_sums[shift], offsets[shift], means[shift] = whole(
            functools.partial(first_kernel, shift),
            [shaped(wide_units), shaped((SLICE, TOK)), shaped((1, TOK), f32)],
            [stage],
            some,
        )(pos, *blocks, mods_column, through, weight_one)
        blocks = after(blocks, pre_sums[shift])
    pre_sums = to_rows(pre_sums)
    hidden, slope, rest, factor, stats = whole(
        hidden_kernel,
        [
            shaped(wide_units),
            shaped(units, f32),
            shaped(units, f32),
            shaped((UNITS, 1), f32),
            shaped((2, TOK), f32),
        ],
    )(pos, *pre_sums)
    c_blocks = both_cores(pos, after(c_lines, pre_sums))
    *grad_sums, cot = whole(
        second_kernel,
        [shaped(units)] * 4 + [shaped((SLICE, TOKENS))],
        [pltpu.VMEM((4, SLICE, TOK), bf16)],
    )(pos, *c_blocks, mods_column, weight_two)
    hidden = [hidden] + [along_row(hidden, q) for q in (1, 2, 3)]

    weights = pl.BlockSpec((UNITS, CHUNK), lambda i, pos: (0, i))
    scratch = [pltpu.VMEM((UNITS, TOKENS), bf16)]

    weight_shapes = [shaped((UNITS, SLICE)), shaped((SLICE, 8), f32)]
    own_second, sums_second = whole(second_weight_kernel, weight_shapes, scratch)(
        pos, *hidden, cot, mods_row, weight_two
    )
    other_second = swap_clips(own_second)
    grad_sums = to_rows(after(grad_sums, hidden[1]))
    (grad_pre,) = whole(grad_kernel, [shaped(wide_units)])(
        pos, *grad_sums, slope, rest, factor
    )
    grad_pre = all_rows(grad_pre)
    own_first, sums_first = whole(
        first_weight_kernel, weight_shapes, scratch + [pltpu.VMEM((SLICE, TOKENS), bf16)]
    )(pos, *grad_pre, *hidden, *offsets, *means, mods_row, weight_one)
    other_first = swap_clips(own_first)

    quarter = (4,) + piece
    terms = whole(
        mod_kernel, [shaped(quarter)] * 8, scratch + [pltpu.VMEM((8, TOK), f32)]
    )(
        pos,
        *grad_pre,
        first_turned,
        sums_first.reshape(INNER, CHANNELS, 8),
        sums_second.reshape(INNER, CHANNELS, 8),
    )
    lines = whole(core_kernel, [shaped(quarter)] * 4)(
        pos, *terms[:4], *after([across(term) for term in terms[4:]], other_second)
    )
    def clips_call(own, other):
        return call(
            clips_kernel,
            (SLICE // CHUNK,),
            [weights, weights],
            weights,
            shaped((UNITS, SLICE), f32),
        )(pos, own, other)

    grad_second = clips_call(own_second, other_second)
    planes = whole(plane_kernel, [shaped(piece)] * 4)(
        pos, lines[0], *after(in_order(lambda p: along_x(lines[p], p)), grad_second)
    )
    grad_first = clips_call(own_first, other_first)
    planes = after(to_rows(planes), grad_first)
    pieces = whole(route_kernel, [shaped(piece)] * 4, [pltpu.VMEM((4,) + piece, bf16)])(
        pos, *planes
    )
    pieces = [pieces[0]] + in_order(lambda p: along_high(pieces[p], p))

    grad_states, grad_shift, grad_scale, grad_gate = whole(
        states_kernel, [shaped(own, f32)] + [shaped((1, CHANNELS), f32)] * 3
    )(pos, *pieces, own_x, own_c, stats, scale_mod.T)
    return (
        grad_states.T[None],
        grad_first.T,
        grad_second.T,
        grad_shift,
        grad_scale,
        grad_gate,
    )


def solution(mesh):
    return jax.shard_map(
        on_device,
        mesh=mesh,
        in_specs=(
            P("dp", "row", "col"),
            P("dp", "row", "col"),
            P("dp", "col"),
            P("dp", "col"),
            P("dp", "col"),
            P("row", "col"),
            P("row", "col"),
        ),
        out_specs=(
            P("dp", "row", "col"),
            P("row", "col"),
            P("row", "col"),
            P("dp", "col"),
            P("dp", "col"),
            P("dp", "col"),
        ),
        check_vma=False,
    )
```
